32 devices in a mesh: section: 4 (over z), dp: 8 (over y, x, core).
Axes of the slice: x: 2, y: 2, z: 4, core: 2. Of those that a mesh axis runs over, the one named last changes fastest.
Arguments:
- tokens: float32 [16384, 768], P('dp'), may hold values from -6 to 6
- absorbed: int32 [16384], P('dp'), may hold values from 0 to 1, as said below
- timesteps: int32 [16], replicated, may hold values from 62 to 999
- mask_embedding: float32 [768], replicated, may hold values from -6 to 6
- time_table: float32 [1000, 768], replicated, may hold values from -6 to 6
- attn_gain: float32 [4, 768], P('section'), may hold values from 0.5 to 1.5
- attn_shift: float32 [4, 768], P('section'), may hold values from -1.75 to 1.75
- joint_weight: float32 [4, 768, 1152], P('section'), may hold values from -0.21875 to 0.21875
- pair_bias: float32 [4, 768], P('section'), may hold values from -1.75 to 1.75
- out_weight: float32 [4, 384, 768], P('section'), may hold values from -4 to 4
- out_bias: float32 [4, 768], P('section'), may hold values from -1.75 to 1.75
- ffn_gain: float32 [4, 768], P('section'), may hold values from 0.5 to 1.5
- ffn_shift: float32 [4, 768], P('section'), may hold values from -1.75 to 1.75
- up_weight: float32 [4, 768, 1536], P('section'), may hold values from -0.21875 to 0.21875
- up_bias: float32 [4, 1536], P('section'), may hold values from -1.75 to 1.75
- down_weight: float32 [4, 1536, 768], P('section'), may hold values from -0.15625 to 0.15625
- down_bias: float32 [4, 768], P('section'), may hold values from -1.75 to 1.75
- cotangent: float32 [16384, 768], P('dp'), may hold values from -8 to 8
Outputs:
- output: float32 [16384, 768], P('dp', 'section')
- input_grad: float32 [16384, 768], P('dp', 'section')
- mask_embedding_grad: float32 [768], P('section')
- time_table_grad: float32 [1000, 768], P(None, 'section')
- attn_gain_grad: float32 [4, 768], P('section', 'dp')
- attn_shift_grad: float32 [4, 768], P('section', 'dp')
- joint_weight_grad: float32 [4, 768, 1152], P('section', 'dp')
- pair_bias_grad: float32 [4, 768], P('section', 'dp')
- out_weight_grad: float32 [4, 384, 768], P('section', None, 'dp')
- out_bias_grad: float32 [4, 768], P('section', 'dp')
- ffn_gain_grad: float32 [4, 768], P('section', 'dp')
- ffn_shift_grad: float32 [4, 768], P('section', 'dp')
- up_weight_grad: float32 [4, 768, 1536], P('section', None, 'dp')
- up_bias_grad: float32 [4, 1536], P('section', 'dp')
- down_weight_grad: float32 [4, 1536, 768], P('section', None, 'dp')
- down_bias_grad: float32 [4, 768], P('section', 'dp')
The draws below stay inside these ranges and needn't reach their ends.
Inputs may be any that keep to these rules, and one draw needn't show every extreme that they name: A token of a sequence with timestep t is absorbed independently with probability (t + 1) / 1000, except in one sequence of every draw, which has no absorbed token.
All inputs are finite; a program needn't handle non-finite values.
Results may differ from the reference program's by a relative error of at most 0.0003.
Values sent between devices are 32-bit elements; how exact they have to be, the bound alone decides.
No kernel may reach another device: no remote copies, remote signals or barrier semaphores. Data moves between devices by JAX's collectives and lax.ppermute only.
A program may use at most 384 MiB of HBM per device.

```python
import math
import jax
import jax.numpy as jnp
from jax import lax

D = 768
HS = 64
FF = 3072
TSTEPS = 1000
LAYERS = 2
LEN = 1024
HALF_HEADS = 6
HALF_FF = 1536
SEQS = 16
TOKENS = 16384


def draw_levels(key):
    first_key, second_key, third_key, fourth_key = jax.random.split(key, 4)
    first_draw = jax.random.randint(first_key, (SEQS,), 0, TSTEPS)
    second_draw = jax.random.randint(second_key, (SEQS,), 0, TSTEPS)
    levels = jnp.minimum(TSTEPS // 16 + first_draw * second_draw // TSTEPS, TSTEPS - 1)
    places = jnp.arange(SEQS, dtype=jnp.int32)
    high_seq = jax.random.randint(third_key, (), 0, SEQS)
    low_seq = (high_seq + 1 + jax.random.randint(fourth_key, (), 0, SEQS - 1)) % SEQS
    levels = jnp.where(places == high_seq, TSTEPS - 1, levels)
    levels = jnp.where(places == low_seq, TSTEPS // 16, levels).astype(jnp.int32)
    return (levels, high_seq)


def draw_timesteps(key, part):
    levels, high_seq = draw_levels(key)
    return levels


def draw_absorbed(key, part):
    levels, high_seq = draw_levels(key)
    chance_key = jax.random.fold_in(key, 7)
    empty_key = jax.random.fold_in(key, 11)
    chances = jax.random.randint(chance_key, (SEQS, LEN), 0, TSTEPS)
    empty_seq = (high_seq + 1 + jax.random.randint(empty_key, (), 0, SEQS - 1)) % SEQS
    places = jnp.arange(SEQS, dtype=jnp.int32)
    taken = (chances <= levels[:, None]) & (places[:, None] != empty_seq)
    return taken.astype(jnp.int32).reshape(TOKENS)


def with_spikes(drawn, own_key, source, target, blocks, factor):
    def block_of(position):
        return (jnp.arange(drawn.shape[position]) // (drawn.shape[position] // blocks)).reshape((-1,) + (1,) * (drawn.ndim - 1 - position))

    near = jax.random.permutation(own_key, blocks)[block_of(target)]
    other_side = (block_of(target) + blocks // 2) % blocks
    return jnp.where((block_of(source) == near) | (block_of(source) == other_side), factor * drawn, drawn)


def block_levels(stream_key, dims, pieces, low, largest):
    def one(dim, blocks):
        draws = jax.random.uniform(jax.random.fold_in(jax.random.fold_in(stream_key, 6), dim), (blocks,), jnp.float32, low / len(pieces), largest / len(pieces))
        return jnp.repeat(jnp.exp(draws), dims[dim] // blocks).reshape((-1,) + (1,) * (len(dims) - dim - 1))

    loudness = one(*pieces[0])
    for cut in pieces[1:]:
        loudness = loudness * one(*cut)
    return loudness


def bell_draw(stream_key, shape, scale, bound, pieces=(), kind=jnp.bfloat16):
    gain = block_levels(stream_key, shape, pieces, -0.22, 0.18) if pieces else 1.0
    values = jax.random.normal(stream_key, shape, jnp.float32) * scale * gain
    return jnp.minimum(jnp.maximum(values, -bound), bound).astype(kind)


def heavy_noise(key, dims, deviation, reach, cuts, heavy, kind=jnp.bfloat16):
    array = deviation * jax.random.normal(key, dims, jnp.float32)
    if cuts:
        array = array * block_levels(key, dims, cuts, -0.22, 0.18)
    return jnp.clip(with_spikes(array, jax.random.fold_in(key, 3), *heavy), -reach, reach).astype(kind)


def setup_inputs(seed: int = 0) -> dict:
    key_list = jax.random.split(jax.random.key(seed), 19)
    return {
        "tokens": bell_draw(key_list[0], (TOKENS, D), 1.0, 6.0, ((0, 8),), jnp.float32),
        "absorbed": draw_absorbed(jax.random.fold_in(key_list[18], 71), 0),
        "timesteps": draw_timesteps(jax.random.fold_in(key_list[18], 71), 0),
        "mask_embedding": bell_draw(key_list[3], (D,), 1.0, 6.0, (), jnp.float32),
        "time_table": bell_draw(key_list[4], (TSTEPS, D), 1.0, 6.0, (), jnp.float32),
        "attn_gain": jnp.clip(1.0 + 0.1 * jax.random.normal(key_list[5], (2 * LAYERS, D), jnp.float32), 0.5, 1.5),
        "attn_shift": bell_draw(key_list[6], (2 * LAYERS, D), 0.3, 1.75, ((0, 4),), jnp.float32),
        "joint_weight": bell_draw(key_list[7], (2 * LAYERS, D, 3 * HALF_HEADS * HS), D ** -0.5, 0.21875, ((0, 4),), jnp.float32),
        "pair_bias": bell_draw(key_list[8], (2 * LAYERS, 2 * HALF_HEADS * HS), 0.3, 1.75, ((0, 4),), jnp.float32),
        "out_weight": bell_draw(key_list[9], (2 * LAYERS, HALF_HEADS * HS, D), ((LEN / (3.0 * D)) ** 0.5), 4.0, ((0, 4),), jnp.float32),
        "out_bias": bell_draw(key_list[10], (2 * LAYERS, D), 0.3, 1.75, ((0, 4),), jnp.float32),
        "ffn_gain": jnp.clip(1.0 + 0.1 * jax.random.normal(key_list[11], (2 * LAYERS, D), jnp.float32), 0.5, 1.5),
        "ffn_shift": bell_draw(key_list[12], (2 * LAYERS, D), 0.3, 1.75, ((0, 4),), jnp.float32),
        "up_weight": bell_draw(key_list[13], (2 * LAYERS, D, HALF_FF), D ** -0.5, 0.21875, ((0, 4),), jnp.float32),
        "up_bias": bell_draw(key_list[14], (2 * LAYERS, HALF_FF), 0.3, 1.75, ((0, 4),), jnp.float32),
        "down_weight": bell_draw(key_list[15], (2 * LAYERS, HALF_FF, D), (FF // 2) ** -0.5, 0.15625, ((0, 4),), jnp.float32),
        "down_bias": bell_draw(key_list[16], (2 * LAYERS, D), 0.3, 1.75, ((0, 4),), jnp.float32),
        "cotangent": heavy_noise(key_list[17], (TOKENS, D), 1.0, 8.0, ((0, 8),), (0, 1, 8, 2.0), jnp.float32),
    }


PRECISE = lax.Precision.HIGHEST

def normalize(matrix):
    center = matrix - lax.optimization_barrier(jnp.mean(matrix, axis=-1, keepdims=True))
    return center * lax.rsqrt(lax.optimization_barrier(jnp.mean(center * center, axis=-1, keepdims=True)) + 1e-05)

def attention_half(inputs, norm_gain, norm_shift, joint_matrix, pair_offset, out_matrix, out_offset):
    inner_width = out_matrix.shape[0]
    head_count = inner_width // HS
    normed = normalize(inputs) * norm_gain + norm_shift
    projected = jnp.dot(normed, joint_matrix, precision=PRECISE)
    queries = (projected[:, :inner_width] + pair_offset[:inner_width]).reshape(-1, head_count, HS)
    key_rows = projected[:, inner_width:2 * inner_width].reshape(-1, head_count, HS)
    values = (projected[:, 2 * inner_width:] + pair_offset[inner_width:]).reshape(-1, head_count, HS)
    scores = jnp.einsum('qhd,khd->hqk', queries, key_rows, precision=PRECISE) / math.sqrt(HS)
    probs = jax.nn.softmax(scores, axis=-1)
    attended = jnp.einsum('hqk,khd->qhd', probs, values, precision=PRECISE).reshape(-1, inner_width)
    return jnp.dot(attended, out_matrix, precision=PRECISE) + out_offset

def feed_half(inputs, norm_gain, norm_shift, up_matrix, up_offset, down_matrix, down_offset):
    normed = normalize(inputs) * norm_gain + norm_shift
    hidden = jax.nn.gelu(jnp.dot(normed, up_matrix, precision=PRECISE) + up_offset, approximate=False)
    return jnp.dot(hidden, down_matrix, precision=PRECISE) + down_offset

def forward_layers(params, state):
    attn_gain, attn_shift, joint_weight, pair_bias, out_weight, out_bias, ffn_gain, ffn_shift, up_weight, up_bias, down_weight, down_bias = params
    for layer_index in range(LAYERS):
        first_half = 2 * layer_index
        second_half = first_half + 1
        left_term = attention_half(state, attn_gain[first_half], attn_shift[first_half], joint_weight[first_half], pair_bias[first_half], out_weight[first_half], out_bias[first_half])
        right_term = attention_half(state, attn_gain[second_half], attn_shift[second_half], joint_weight[second_half], pair_bias[second_half], out_weight[second_half], out_bias[second_half])
        state = state + (left_term + right_term)
        left_term = feed_half(state, ffn_gain[first_half], ffn_shift[first_half], up_weight[first_half], up_bias[first_half], down_weight[first_half], down_bias[first_half])
        right_term = feed_half(state, ffn_gain[second_half], ffn_shift[second_half], up_weight[second_half], up_bias[second_half], down_weight[second_half], down_bias[second_half])
        state = state + (left_term + right_term)
    return state

def reference(tokens, absorbed, timesteps, mask_embedding, time_table, attn_gain, attn_shift, joint_weight, pair_bias, out_weight, out_bias, ffn_gain, ffn_shift, up_weight, up_bias, down_weight, down_bias, cotangent):
    params = (attn_gain, attn_shift, joint_weight, pair_bias, out_weight, out_bias, ffn_gain, ffn_shift, up_weight, up_bias, down_weight, down_bias)
    token_blocks = tokens.reshape(-1, LEN, D)
    masked = absorbed.reshape(-1, LEN).astype(jnp.float32)
    step_range = jnp.arange(TSTEPS, dtype=jnp.int32)
    step_picks = (timesteps[:, None] == step_range[None, :]).astype(jnp.float32)
    cot_blocks = cotangent.reshape(-1, LEN, D)
    zero_state = jax.tree.map(jnp.zeros_like, (params, mask_embedding, time_table))

    def per_sequence(carried, block_item):
        block_tokens, block_mask, block_pick, block_cot = block_item

        def forward_pass(weights, clean_rows, embedding, table):
            step_row = jnp.dot(block_pick, table, precision=PRECISE)
            start = jnp.where(block_mask[:, None] > 0.5, embedding + step_row, clean_rows)
            return forward_layers(weights, start)
        result, pullback = jax.vjp(forward_pass, params, block_tokens, mask_embedding, time_table)
        weighting = LEN / jnp.maximum(jnp.sum(block_mask), 1.0)
        weighted = block_cot * block_mask[:, None] * weighting
        grad_params, grad_rows, grad_embedding, grad_table = pullback(weighted)
        carried = jax.tree.map(jnp.add, carried, (grad_params, grad_embedding, grad_table))
        return (carried, (result, grad_rows))
    (grad_params, grad_embedding, grad_table), (results, input_rows) = lax.scan(per_sequence, zero_state, (token_blocks, masked, step_picks, cot_blocks))
    return (results.reshape(-1, D), input_rows.reshape(-1, D), grad_embedding, grad_table, grad_params[0], grad_params[1], grad_params[2], grad_params[3], grad_params[4], grad_params[5], grad_params[6], grad_params[7], grad_params[8], grad_params[9], grad_params[10], grad_params[11])
```

```python
import functools
import math

import jax
import jax.numpy as jnp
from jax import lax
from jax.experimental import pallas as pl
from jax.experimental.pallas import tpu as pltpu
from jax.sharding import PartitionSpec as P

HS = 64
LEN = 1024
EPS = 1e-05
AXES = ("section", "dp")
f32 = jnp.float32
bf16 = jnp.bfloat16

NN = ((1,), (0,))
NT = ((1,), (1,))
TN = ((0,), (0,))
BM = 256
VMEM_LIMIT = 60 * 1024 * 1024


def dot(a, b, dims):
    return lax.dot_general(a, b, (dims, ((), ())), preferred_element_type=f32)


def split(value):
    high = value.astype(bf16)
    return high, (value - high.astype(f32)).astype(bf16)


def dot3(ah, al, bh, bl, dims):
    return dot(ah, bh, dims) + (dot(ah, bl, dims) + dot(al, bh, dims))


def unit_rows(x):
    center = x - jnp.mean(x, axis=-1, keepdims=True)
    scale = lax.rsqrt(jnp.mean(center * center, axis=-1, keepdims=True) + EPS)
    return center * scale, scale


def pull_rows(n, scale, e):
    return (e - jnp.mean(e, axis=-1, keepdims=True) - n * jnp.mean(e * n, axis=-1, keepdims=True)) * scale


class Pieces:
    def __init__(self, entries):
        self.arrays, self.entries = [], []
        for array, *rest in entries:
            index = next((i for i, known in enumerate(self.arrays) if known is array), len(self.arrays))
            if index == len(self.arrays):
                self.arrays.append(array)
            self.entries.append((index, *rest))


def load_split(entries, flags, refs, stage, sems, high_out, low_out):
    quarter = stage.shape[1] // 4
    near = flags[0] == 1
    copies = {"near": [], "far": [], "all": []}
    for number, (index, first, count, slot, place, offset, when) in enumerate(entries):
        row = offset if place is None else pl.multiple_of(flags[1 + place] * quarter + offset, 8)
        copies[when].append(
            pltpu.make_async_copy(
                refs[index].at[pl.ds(first, count)], stage.at[slot, pl.ds(row, count)], sems.at[number]
            )
        )
    for act in ("start", "wait"):

        @pl.when(near)
        def _():
            for copy in copies["near"]:
                getattr(copy, act)()

        @pl.when(jnp.logical_not(near))
        def _():
            for copy in copies["far"]:
                getattr(copy, act)()

        for copy in copies["all"]:
            getattr(copy, act)()
    for slot in range(2):
        high, low = split(stage[slot])
        high_out[slot] = high
        low_out[slot] = low


def store_pieces(flags, read, order, refs):
    split_rows = order == 3
    for number, ref in enumerate(refs):
        send = number % 2 == 0
        along = 1 + number // 2 if split_rows else order
        kinds = ((1, 3) if send else (0, 2)) if along == 1 else ((2, 3) if send else (0, 1))
        count = ref.shape[2]
        for slot in range(2):
            for place, k in enumerate(kinds):
                step = 2 * count if split_rows else count
                row = pl.multiple_of(flags[1 + k] * step + (number // 2) * count, 8)
                ref[place, slot] = read(slot, row, count)


def full(shape):
    zeros = (0,) * len(shape)
    return pl.BlockSpec(shape, lambda i: zeros)


def rows(width, bm=BM):
    return pl.BlockSpec((bm, width), lambda i: (i, 0))


def lanes(height, bm=BM):
    return pl.BlockSpec((height, bm), lambda i: (0, i))


def halves(width, bm=BM):
    first = LEN // bm // 2
    return [
        pl.BlockSpec((bm, width), lambda i: (jnp.minimum(i, first - 1), 0)),
        pl.BlockSpec((bm, width), lambda i: (jnp.maximum(i - first, 0), 0)),
    ]


def read_halves(first, second):
    early = pl.program_id(0) < pl.num_programs(0) // 2
    return jnp.where(early, first[...], second[...])


def write_halves(first, second, value):
    early = pl.program_id(0) < pl.num_programs(0) // 2

    @pl.when(early)
    def _():
        first[...] = value

    @pl.when(jnp.logical_not(early))
    def _():
        second[...] = value


ANY = pl.BlockSpec(memory_space=pl.ANY)
SMEM = pl.BlockSpec(memory_space=pltpu.SMEM)


def call(kernel, grid, in_specs, out_specs, out_shapes, scratch, name, flops, nbytes, *args):
    return pl.pallas_call(
        kernel,
        grid=(grid,),
        in_specs=in_specs,
        out_specs=out_specs,
        out_shape=[jax.ShapeDtypeStruct(s, t) for s, t in out_shapes],
        scratch_shapes=scratch,
        name=name,
        cost_estimate=pl.CostEstimate(flops=int(flops), bytes_accessed=int(nbytes), transcendentals=0),
        compiler_params=pltpu.CompilerParams(
            vmem_limit_bytes=VMEM_LIMIT, dimension_semantics=("arbitrary",)
        ),
    )(*args)


def attn_in_kernel(added, entries, count, flags, *refs):
    base = refs[0]
    refs = refs[1:]
    if added:
        added_refs, refs = refs[:4], refs[4:]
    vec, bias = refs[:2]
    sources, refs = refs[2 : 2 + count], refs[2 + count :]
    if added:
        x_out = refs[0]
        refs = refs[1:]
    nh_out, nl_out, scale_out, ph_out, pl_out, wh_out, wl_out, stage, sems = refs
    inner = 3 * (ph_out.shape[0] // 6)

    @pl.when(pl.program_id(0) == 0)
    def _():
        load_split(entries, flags, sources, stage, sems, wh_out, wl_out)

    x = base[...]
    if added:
        x = x + (read_halves(*added_refs[:2]) + read_halves(*added_refs[2:]))
        x_out[...] = x
    n, scale = unit_rows(x)
    high, low = split(n)
    nh_out[...] = high
    nl_out[...] = low
    scale_out[...] = scale
    third = inner // 3
    for slot in range(2):
        ah, al = split(n * vec[slot, 0:1, :] + vec[slot, 1:2, :])
        projected = dot3(wh_out[slot, :inner], wl_out[slot, :inner], ah, al, NT)
        projected = projected + bias[slot * inner : (slot + 1) * inner]
        queries = projected[:third] * (1.0 / math.sqrt(HS))
        for first, value in ((0, queries), (third, projected[third:])):
            high, low = split(value)
            start = slot * inner + first
            ph_out[start : start + value.shape[0]] = high
            pl_out[start : start + value.shape[0]] = low


def attn_in(flags, x, added, vec, bias, pieces):
    length, width = x.shape
    inner = bias.shape[0] // 2
    outs = [((length, width), f32)] if added else []
    out_specs = [rows(width)] if added else []
    outs += [
        ((length, width), bf16),
        ((length, width), bf16),
        ((length, 1), f32),
        ((2 * inner, length), bf16),
        ((2 * inner, length), bf16),
        ((2, width, width), bf16),
        ((2, width, width), bf16),
    ]
    out_specs += [rows(width), rows(width), rows(1), lanes(2 * inner), lanes(2 * inner)]
    out_specs += [full((2, width, width))] * 2
    in_specs = [SMEM, rows(width)] + halves(width) * (len(added) // 2) + [full(vec.shape), full(bias.shape)]
    in_specs += [ANY] * len(pieces.arrays)
    result = call(
        functools.partial(attn_in_kernel, bool(added), pieces.entries, len(pieces.arrays)),
        length // BM,
        in_specs,
        out_specs,
        outs,
        [pltpu.VMEM((2, width, width), f32), pltpu.SemaphoreType.DMA((len(pieces.entries),))],
        "attn_in",
        6 * length * width * 2 * inner,
        20e6,
        flags, x, *added, vec, bias, *pieces.arrays,
    )
    if not added:
        result = [x] + list(result)
    return result


def heads_kernel(qh, ql, kh, kl, vh, vl, wh, wl, vec, oh_out, ol_out, lse_out, part_a, part_b, oh_all, ol_all):
    head = pl.program_id(0)
    keys = jnp.concatenate([kh[...], kh[...], kl[...]], axis=0)
    values = jnp.concatenate([vh[...], vl[...]], axis=0)
    value_high = vh[...]
    for block in range(qh.shape[1] // BM):
        cut = slice(block * BM, (block + 1) * BM)
        queries = jnp.concatenate([qh[:, cut], ql[:, cut], qh[:, cut]], axis=0)
        scores = dot(keys, queries, TN)
        top = jnp.max(scores, axis=0, keepdims=True)
        weights = jnp.exp(scores - top)
        total = jnp.sum(weights, axis=0, keepdims=True)
        high, low = split(weights)
        both = dot(values, high, NN)
        attended = (both[:HS] + (both[HS:] + dot(value_high, low, NN))) / total
        high, low = split(attended)
        oh_out[:, cut] = high
        ol_out[:, cut] = low
        lse_out[0, :, cut] = top + jnp.log(total)
    place = pl.ds(pl.multiple_of(head * HS, HS), HS)
    oh_all[place, :] = oh_out[...]
    ol_all[place, :] = ol_out[...]

    @pl.when(head == pl.num_programs(0) - 1)
    def _():
        inner, width = oh_all.shape[0], wh.shape[2]
        offset = 0.5 * (vec[0, 3:4, :] + vec[1, 3:4, :])
        for part, cut in ((part_a, slice(0, LEN // 2)), (part_b, slice(LEN // 2, LEN))):
            part[...] = offset + dot3(
                oh_all[:, cut], ol_all[:, cut], wh[...].reshape(inner, width), wl[...].reshape(inner, width), TN
            )


def head_spec(length, which, half_heads):
    return pl.BlockSpec(
        (HS, length), lambda h: (3 * half_heads * (h // half_heads) + which * half_heads + h % half_heads, 0)
    )


def attn_heads(ph, pl_, wh, wl, vec):
    inner2, length = ph.shape
    width = wh.shape[2]
    heads = inner2 // (3 * HS)
    half = heads // 2
    out_rows = half * HS
    specs = []
    for which in range(3):
        specs += [head_spec(length, which, half)] * 2
    tail = pl.BlockSpec((2, out_rows, width), lambda h: (0, width // out_rows - 1, 0))
    return call(
        heads_kernel,
        heads,
        specs + [tail, tail, full(vec.shape)],
        [
            pl.BlockSpec((HS, length), lambda h: (h, 0)),
            pl.BlockSpec((HS, length), lambda h: (h, 0)),
            pl.BlockSpec((1, 1, length), lambda h: (h, 0, 0)),
            full((length // 2, width)),
            full((length // 2, width)),
        ],
        [
            ((heads * HS, length), bf16),
            ((heads * HS, length), bf16),
            ((heads, 1, length), f32),
            ((length // 2, width), f32),
            ((length // 2, width), f32),
        ],
        [pltpu.VMEM((heads * HS, length), bf16)] * 2,
        "attn_heads",
        heads * length * length * HS * 2 * 10,
        15e6,
        ph, pl_, ph, pl_, ph, pl_, wh, wl, vec,
    )


def gate(u):
    phi = 0.5 * (1.0 + lax.erf(u * math.sqrt(0.5)))
    slope = phi + u * (jnp.exp(-0.5 * u * u) * (1.0 / math.sqrt(2.0 * math.pi)))
    return u * phi, slope


def feed_up_kernel(entries, count, flags, base, mine_a, mine_b, other_a, other_b, vec, bias, *refs):
    y_out, nh_out, nl_out, scale_out, hh_out, hl_out, slope_out, uh_out, ul_out, stage, sems = refs[count:]
    hidden = stage.shape[1]

    @pl.when(pl.program_id(0) == 0)
    def _():
        load_split(entries, flags, refs[:count], stage, sems, uh_out, ul_out)

    y = base[...] + (read_halves(mine_a, mine_b) + read_halves(other_a, other_b))
    y_out[...] = y
    n, scale = unit_rows(y)
    high, low = split(n)
    nh_out[...] = high
    nl_out[...] = low
    scale_out[...] = scale
    for slot in range(2):
        ah, al = split(n * vec[slot, 4:5, :] + vec[slot, 5:6, :])
        before = dot3(ah, al, uh_out[slot], ul_out[slot], NT) + bias[slot : slot + 1, :]
        active, slope = gate(before)
        cut = slice(slot * hidden, (slot + 1) * hidden)
        slope_out[:, cut] = slope
        high, low = split(active)
        hh_out[:, cut] = high
        hl_out[:, cut] = low


def feed_up(flags, base, added, vec, bias, pieces):
    length, width = base.shape
    hidden = bias.shape[1]
    weight = ((2, hidden, width), bf16)
    return call(
        functools.partial(feed_up_kernel, pieces.entries, len(pieces.arrays)),
        length // BM,
        [SMEM, rows(width)] + halves(width) * 2 + [full(vec.shape), full(bias.shape)] + [ANY] * len(pieces.arrays),
        [rows(width)] * 3 + [rows(1)] + [rows(2 * hidden)] * 3 + [full(weight[0])] * 2,
        [
            ((length, width), f32),
            ((length, width), bf16),
            ((length, width), bf16),
            ((length, 1), f32),
            ((length, 2 * hidden), bf16),
            ((length, 2 * hidden), bf16),
            ((length, 2 * hidden), f32),
            weight, weight,
        ],
        [pltpu.VMEM((2, hidden, width), f32), pltpu.SemaphoreType.DMA((len(pieces.entries),))],
        "feed_up",
        6 * length * width * 2 * hidden,
        40e6,
        flags, base, *added, vec, bias, *pieces.arrays,
    )


def feed_down_kernel(entries, count, flags, hh, hl, vec, *refs):
    part_a, part_b, dh_out, dl_out, stage, sems = refs[count:]
    hidden = stage.shape[1]

    @pl.when(pl.program_id(0) == 0)
    def _():
        load_split(entries, flags, refs[:count], stage, sems, dh_out, dl_out)

    partial = 0.5 * (vec[0, 6:7, :] + vec[1, 6:7, :])
    for slot in range(2):
        cut = slice(slot * hidden, (slot + 1) * hidden)
        partial = partial + dot3(hh[:, cut], hl[:, cut], dh_out[slot], dl_out[slot], NN)
    write_halves(part_a, part_b, partial)


def feed_down(flags, hh, hl, vec, pieces):
    length, hidden, width = hh.shape[0], hh.shape[1] // 2, vec.shape[2]
    weight = ((2, hidden, width), bf16)
    return call(
        functools.partial(feed_down_kernel, pieces.entries, len(pieces.arrays)),
        length // BM,
        [SMEM] + [rows(2 * hidden)] * 2 + [full(vec.shape)] + [ANY] * len(pieces.arrays),
        halves(width) + [full(weight[0])] * 2,
        [((length // 2, width), f32)] * 2 + [weight, weight],
        [pltpu.VMEM((2, hidden, width), f32), pltpu.SemaphoreType.DMA((len(pieces.entries),))],
        "feed_down",
        6 * length * width * 2 * hidden,
        25e6,
        flags, hh, hl, vec, *pieces.arrays,
    )


def piece_outs(width, order):
    count = 4 if order == 3 else 2
    shape = (2, 2, width // 2 // count, width)
    return [full(shape)] * count, [(shape, f32)] * count


def feed_back_one_kernel(pulled, order, flags, g_in, *refs):
    if pulled:
        added_refs, (nh, nl, scale) = refs[:4], refs[4:7]
        refs = refs[7:]
    (dh, dl, hh, hl, slope, g_out, uh_out, ul_out, *piece_refs, bias_out, total_out, acc) = refs
    step = pl.program_id(0)
    hidden = dh.shape[1]
    g = g_in[...]
    if pulled:
        n = nh[...].astype(f32) + nl[...].astype(f32)
        g = g + pull_rows(n, scale[...], read_halves(*added_refs[:2]) + read_halves(*added_refs[2:]))
    g_out[...] = g

    @pl.when(step == 0)
    def _():
        acc[...] = jnp.zeros_like(acc)
        bias_out[...] = jnp.zeros_like(bias_out)
        total_out[...] = jnp.zeros_like(total_out)

    total_out[...] += jnp.sum(g, axis=0, keepdims=True)
    gh, gl = split(g)
    for slot in range(2):
        cut = slice(slot * hidden, (slot + 1) * hidden)
        delta = dot3(gh, gl, dh[slot], dl[slot], NT) * slope[:, cut]
        bias_out[slot : slot + 1, :] += jnp.sum(delta, axis=0, keepdims=True)
        high, low = split(delta)
        uh_out[:, cut] = high
        ul_out[:, cut] = low
        acc[slot] += dot3(gh, gl, hh[:, cut], hl[:, cut], TN)

    @pl.when(step == pl.num_programs(0) - 1)
    def _():
        store_pieces(flags, lambda slot, row, count: acc[slot, pl.ds(row, count), :], order, piece_refs)


def feed_back_one(order, flags, g, pulled, dh, dl, hh, hl, slope):
    length, width = g.shape
    hidden = dh.shape[1]
    piece_specs, piece_shapes = piece_outs(width, order)
    pulled_specs = halves(width) * 2 + [rows(width)] * 2 + [rows(1)] if pulled else []
    return call(
        functools.partial(feed_back_one_kernel, bool(pulled), order),
        length // BM,
        [SMEM, rows(width)] + pulled_specs + [full(dh.shape)] * 2 + [rows(2 * hidden)] * 3,
        [rows(width)] + [rows(2 * hidden)] * 2 + piece_specs + [full((2, hidden)), full((1, width))],
        [((length, width), f32), ((length, 2 * hidden), bf16), ((length, 2 * hidden), bf16)]
        + piece_shapes
        + [((2, hidden), f32), ((1, width), f32)],
        [pltpu.VMEM((2, width, hidden), f32)],
        "feed_back_one",
        6 * length * width * 4 * hidden,
        40e6,
        flags, g, *pulled, dh, dl, hh, hl, slope,
    )


def feed_back_two_kernel(parts, order, flags, uh, ul, nh, nl, vec, *refs):
    if "e" in parts:
        wh, wl, e_a, e_b, vec_out = refs
    else:
        *piece_refs, acc = refs
    step = pl.program_id(0)
    hidden = uh.shape[1] // 2

    @pl.when(step == 0)
    def _():
        if "e" in parts:
            vec_out[...] = jnp.zeros_like(vec_out)
        else:
            acc[...] = jnp.zeros_like(acc)

    n = nh[...].astype(f32) + nl[...].astype(f32)
    e = None
    for slot in range(2):
        cut = slice(slot * hidden, (slot + 1) * hidden)
        gain = vec[slot, 4:5, :]
        if "e" in parts:
            delta = dot3(uh[:, cut], ul[:, cut], wh[slot], wl[slot], NN)
            vec_out[2 * slot : 2 * slot + 1, :] += jnp.sum(delta * n, axis=0, keepdims=True)
            vec_out[2 * slot + 1 : 2 * slot + 2, :] += jnp.sum(delta, axis=0, keepdims=True)
            e = delta * gain if e is None else e + delta * gain
        else:
            ah, al = split(n * gain + vec[slot, 5:6, :])
            acc[slot] += dot3(uh[:, cut], ul[:, cut], ah, al, TN)
    if "e" in parts:
        write_halves(e_a, e_b, e)
    else:

        @pl.when(step == pl.num_programs(0) - 1)
        def _():
            store_pieces(flags, lambda slot, row, count: acc[slot, pl.ds(row, count), :], order, piece_refs)


def feed_back_two(parts, order, flags, uh, ul, nh, nl, vec, wh, wl):
    length, width = nh.shape
    hidden = wh.shape[1]
    piece_specs, piece_shapes = piece_outs(width, order)
    if parts == "e":
        weights, out_specs = (wh, wl), halves(width) + [full((4, width))]
        out_shapes = [((length // 2, width), f32)] * 2 + [((4, width), f32)]
    else:
        weights, out_specs, out_shapes = (), piece_specs, piece_shapes
    return call(
        functools.partial(feed_back_two_kernel, parts, order),
        length // BM,
        [SMEM] + [rows(2 * hidden)] * 2 + [rows(width)] * 2 + [full(vec.shape)] + [full(w.shape) for w in weights],
        out_specs,
        out_shapes,
        [pltpu.VMEM((2, hidden, width), f32)] if parts == "w" else [],
        "feed_back_two_" + parts,
        6 * length * width * 2 * hidden,
        25e6,
        flags, uh, ul, nh, nl, vec, *weights,
    )


def attn_back_one_kernel(
    g_in, mine_a, mine_b, other_a, other_b, nh, nl, scale, wh, wl, oh, ol, g_out, dh_out, dl_out, do_out, total_out
):
    step = pl.program_id(0)
    inner, width = oh.shape[0], g_in.shape[1]

    @pl.when(step == 0)
    def _():
        do_out[...] = jnp.zeros_like(do_out)
        total_out[...] = jnp.zeros_like(total_out)

    n = nh[...].astype(f32) + nl[...].astype(f32)
    g = g_in[...] + pull_rows(n, scale[...], read_halves(mine_a, mine_b) + read_halves(other_a, other_b))
    g_out[...] = g
    total_out[...] += jnp.sum(g, axis=0, keepdims=True)
    gh, gl = split(g)
    delta = dot3(wh[...].reshape(inner, width), wl[...].reshape(inner, width), gh, gl, NT)
    high, low = split(delta)
    dh_out[...] = high
    dl_out[...] = low
    do_out[...] += dot3(oh[...], ol[...], gh, gl, NN)


def attn_back_one(g, added, nh, nl, scale, wh, wl, oh, ol):
    length, width = g.shape
    inner = oh.shape[0]
    out_rows = inner // 2
    tail = pl.BlockSpec((2, out_rows, width), lambda i: (0, width // out_rows - 1, 0))
    return call(
        attn_back_one_kernel,
        length // BM,
        [rows(width)] + halves(width) * 2 + [rows(width)] * 2 + [rows(1)] + [tail, tail] + [lanes(inner)] * 2,
        [rows(width), lanes(inner), lanes(inner), full((inner, width)), full((1, width))],
        [
            ((length, width), f32),
            ((inner, length), bf16),
            ((inner, length), bf16),
            ((inner, width), f32),
            ((1, width), f32),
        ],
        [],
        "attn_back_one",
        6 * length * width * 2 * inner,
        20e6,
        g, *added, nh, nl, scale, wh, wl, oh, ol,
    )


def heads_back_kernel(qh, ql, kh, kl, vh, vl, dh, dl, oh, ol, lse, dqh, dql, dkh, dkl, dvh, dvl, acc_k, acc_v):
    keys = jnp.concatenate([kh[...], kh[...], kl[...]], axis=0)
    keys_two = jnp.concatenate([kh[...], kl[...]], axis=0)
    values = jnp.concatenate([vh[...], vh[...], vl[...]], axis=0)
    key_high = kh[...]
    for block in range(qh.shape[1] // BM):
        cut = slice(block * BM, (block + 1) * BM)
        q_high, q_low = qh[:, cut], ql[:, cut]
        d_high, d_low = dh[:, cut], dl[:, cut]
        delta = d_high.astype(f32) + d_low.astype(f32)
        attended = oh[:, cut].astype(f32) + ol[:, cut].astype(f32)
        diagonal = jnp.sum(delta * attended, axis=0, keepdims=True)
        scores = dot(keys, jnp.concatenate([q_high, q_low, q_high], axis=0), TN)
        probs = jnp.exp(scores - lse[0, :, cut])
        p_high, p_low = split(probs)
        delta_probs = dot(values, jnp.concatenate([d_high, d_low, d_high], axis=0), TN)
        delta_scores = probs * (delta_probs - diagonal)
        s_high, s_low = split(delta_scores)
        both = dot(jnp.concatenate([d_high, d_low], axis=0), p_high, NT)
        part_v = both[:HS] + (both[HS:] + dot(d_high, p_low, NT))
        both = dot(jnp.concatenate([q_high, q_low], axis=0), s_high, NT)
        part_k = both[:HS] + (both[HS:] + dot(q_high, s_low, NT))
        if block == 0:
            acc_v[...] = part_v
            acc_k[...] = part_k
        else:
            acc_v[...] += part_v
            acc_k[...] += part_k
        both = dot(keys_two, s_high, NN)
        delta_q = (both[:HS] + (both[HS:] + dot(key_high, s_low, NN))) * (1.0 / math.sqrt(HS))
        high, low = split(delta_q)
        dqh[:, cut] = high
        dql[:, cut] = low
    high, low = split(acc_k[...])
    dkh[...] = high
    dkl[...] = low
    high, low = split(acc_v[...])
    dvh[...] = high
    dvl[...] = low


def attn_heads_back(ph, pl_, dh, dl, oh, ol, lse):
    inner2, length = ph.shape
    heads = inner2 // (3 * HS)
    half = heads // 2
    specs = []
    for which in range(3):
        specs += [head_spec(length, which, half)] * 2
    plain = pl.BlockSpec((HS, length), lambda h: (h, 0))
    return call(
        heads_back_kernel,
        heads,
        specs + [plain] * 4 + [pl.BlockSpec((1, 1, length), lambda h: (h, 0, 0))],
        [plain] * 6,
        [((heads * HS, length), bf16)] * 6,
        [pltpu.VMEM((HS, length), f32)] * 2,
        "attn_heads_back",
        heads * length * length * HS * 2 * 26,
        15e6,
        ph, pl_, ph, pl_, ph, pl_, dh, dl, oh, ol, lse,
    )


def attn_back_two_kernel(parts, order, flags, *refs):
    dqh, dql, dkh, dkl, dvh, dvl, nh, nl, vec = refs[:9]
    refs = refs[9:]
    if "e" in parts:
        (wh, wl), refs = refs[:2], refs[2:]
    if "w" in parts:
        do, refs = refs[0], refs[1:]
    if "e" in parts:
        (e_a, e_b, vec_out), refs = refs[:3], refs[3:]
    if "w" in parts:
        *piece_refs, pair_out, acc, turned = refs
    step = pl.program_id(0)
    third = dqh.shape[0] // 2
    inner = 3 * third

    @pl.when(step == 0)
    def _():
        if "e" in parts:
            vec_out[...] = jnp.zeros_like(vec_out)
        if "w" in parts:
            acc[...] = jnp.zeros_like(acc)
            pair_out[...] = jnp.zeros_like(pair_out)

    n = nh[...].astype(f32) + nl[...].astype(f32)
    ones = jnp.ones((8, n.shape[0]), bf16)
    e = None
    for slot in range(2):
        cut = slice(slot * third, (slot + 1) * third)
        high = jnp.concatenate([dqh[cut], dkh[cut], dvh[cut]], axis=0)
        low = jnp.concatenate([dql[cut], dkl[cut], dvl[cut]], axis=0)
        gain = vec[slot, 0:1, :]
        if "w" in parts:
            ah, al = split(n * gain + vec[slot, 1:2, :])
            acc[slot] += dot3(high, low, ah, al, NN)
            pair_out[slot] += dot(ones, high, NT) + dot(ones, low, NT)
        if "e" in parts:
            delta = dot3(high, low, wh[slot, :inner], wl[slot, :inner], TN)
            vec_out[2 * slot : 2 * slot + 1, :] += jnp.sum(delta * n, axis=0, keepdims=True)
            vec_out[2 * slot + 1 : 2 * slot + 2, :] += jnp.sum(delta, axis=0, keepdims=True)
            e = delta * gain if e is None else e + delta * gain
    if "e" in parts:
        write_halves(e_a, e_b, e)

    if "w" in parts:

        @pl.when(step == pl.num_programs(0) - 1)
        def _():
            for slot in range(2):
                whole = jnp.concatenate([acc[slot], do[slot * third : (slot + 1) * third]], axis=0)
                turned[slot] = jnp.transpose(whole)
            store_pieces(flags, lambda slot, row, count: turned[slot, pl.ds(row, count), :], order, piece_refs)


def attn_back_two(parts, order, flags, grads, nh, nl, vec, wh, wl, do):
    length, width = nh.shape
    heads_rows = grads[0].shape[0]
    inner = 3 * heads_rows // 2
    piece_specs, piece_shapes = piece_outs(width, order)
    in_specs = [SMEM] + [lanes(heads_rows)] * 6 + [rows(width)] * 2 + [full(vec.shape)]
    args = [flags, *grads, nh, nl, vec]
    out_specs, out_shapes, scratch = [], [], []
    if "e" in parts:
        in_specs += [full(wh.shape)] * 2
        args += [wh, wl]
        out_specs += halves(width) + [full((4, width))]
        out_shapes += [((length // 2, width), f32)] * 2 + [((4, width), f32)]
    if "w" in parts:
        in_specs += [full(do.shape)]
        args += [do]
        out_specs += piece_specs + [full((2, 8, inner))]
        out_shapes += piece_shapes + [((2, 8, inner), f32)]
        scratch = [pltpu.VMEM((2, inner, width), f32), pltpu.VMEM((2, width, width), f32)]
    return call(
        functools.partial(attn_back_two_kernel, parts, order),
        length // BM,
        in_specs,
        out_specs,
        out_shapes,
        scratch,
        "attn_back_two_" + parts,
        6 * length * width * 2 * inner * len(parts),
        15e6 * len(parts),
        *args,
    )


def finish_kernel(g_in, mine_a, mine_b, other_a, other_b, nh, nl, scale, mask, grad_out, sums_out):
    @pl.when(pl.program_id(0) == 0)
    def _():
        sums_out[...] = jnp.zeros_like(sums_out)

    n = nh[...].astype(f32) + nl[...].astype(f32)
    g = g_in[...] + pull_rows(n, scale[...], read_halves(mine_a, mine_b) + read_halves(other_a, other_b))
    absorbed = mask[...]
    grad_out[...] = g * (1.0 - absorbed)
    sums_out[...] += jnp.sum(g * absorbed, axis=0, keepdims=True)


def finish(g, added, nh, nl, scale, mask):
    length, width = g.shape
    return call(
        finish_kernel,
        length // BM,
        [rows(width)] + halves(width) * 2 + [rows(width)] * 2 + [rows(1)] * 2,
        [rows(width), full((1, width))],
        [((length, width), f32), ((1, width), f32)],
        [],
        "finish",
        10 * length * width,
        15e6,
        g, *added, nh, nl, scale, mask,
    )


VEC_ROWS = 10


def pack_kernel(columns, flags, *refs):
    table = refs[-1]
    row_sum = refs[-2]
    width = row_sum.shape[1]
    odd, core, sequence = flags[0], flags[1], flags[2]
    table[...] = jnp.zeros_like(table)

    def place(parts):
        zero = jnp.zeros_like(parts[0])
        first = jnp.concatenate([v for p in parts for v in (p, zero)], axis=1)
        second = jnp.concatenate([v for p in parts for v in (zero, p)], axis=1)
        return jnp.where(core == 0, first, second)

    for layer in range(2):
        attn_vec, pair_sum, out_total, ffn_vec, up_sum, down_total = refs[6 * layer : 6 * layer + 6]
        third = pair_sum.shape[2] // 3
        block = up_sum.shape[1] // columns
        for slot in range(2):
            section = 2 * layer + jnp.where(odd == 1, 1 - slot, slot)
            base = section * VEC_ROWS

            def put(row, value):
                table[pl.ds(base + row, 1), :] = value

            put(0, attn_vec[2 * slot : 2 * slot + 1, :])
            put(1, attn_vec[2 * slot + 1 : 2 * slot + 2, :])
            pair = pair_sum[slot, 0:1, :]
            put(2, place([pair[:, :third], pair[:, 2 * third :]]))
            put(3, 0.5 * out_total[...])
            put(4, ffn_vec[2 * slot : 2 * slot + 1, :])
            put(5, ffn_vec[2 * slot + 1 : 2 * slot + 2, :])
            put(6, 0.5 * down_total[...])
            ups = up_sum[slot : slot + 1, :]
            spread = place([ups[:, k * block : (k + 1) * block] for k in range(columns)])
            for k in range(spread.shape[1] // width):
                put(7 + k, spread[:, k * width : (k + 1) * width])
    table[pl.ds(4 * VEC_ROWS + sequence, 1), :] = 0.5 * row_sum[...]


def pack(flags, small, row_sum, columns, sequences):
    width = row_sum.shape[1]
    arrays = [*small[0], *small[1], row_sum]
    count = -(-(4 * VEC_ROWS + sequences) // 8) * 8
    return call(
        functools.partial(pack_kernel, columns),
        1,
        [SMEM] + [full(v.shape) for v in arrays],
        [full((count, width))],
        [((count, width), f32)],
        [],
        "pack",
        1e4,
        1e6,
        flags, *arrays,
    )[0]


def after(value, *others):
    return lax.optimization_barrier((value, *others))[0]


class Plan:
    def __init__(self, planes, dp):
        self.planes, self.dp, self.columns = planes, dp, dp // 2
        self.z = lax.axis_index("section")
        device = lax.axis_index("dp")
        self.column, self.core = device // 2, device % 2

    def permute(self, value, target):
        pairs = []
        for z in range(self.planes):
            for d in range(self.dp):
                to = target(z, d)
                if to is not None:
                    pairs.append((z * self.dp + d, to[0] * self.dp + to[1]))
        return lax.ppermute(value, AXES, pairs)

    def groups(self):
        return [
            [z * self.dp + 2 * j + c for j in range(self.columns)] for z in range(self.planes) for c in range(2)
        ]

    def across(self, value):
        return self.permute(value, lambda z, d: (z, d ^ 1))

    def added(self, first, second):
        return (first, second, self.across(first), self.across(second))

    def along_z(self, value, bit, planes=None):
        return self.permute(value, lambda z, d: (z ^ bit, d) if planes is None or z in planes else None)

    def in_plane(self, value, bit):
        return self.permute(value, lambda z, d: (z, d ^ (2 * bit)))

    def whole(self, shard):
        return lax.all_gather(shard, AXES, axis_index_groups=self.groups(), axis=0, tiled=True)

    def all_sum(self, table):
        if self.columns == 4:
            for step in (self.across, *[functools.partial(self.in_plane, bit=b) for b in (1, 2)]):
                table = table + step(table)
            for bit in (1, 2):
                table = table + self.along_z(table, bit)
            return table
        return lax.psum(table, AXES)


class Group:
    def __init__(self, plan, shard, order):
        self.plan, self.shard, self.order = plan, shard, order
        if plan.columns == 4:
            self.got = plan.in_plane(shard, order)

    def step(self, *others):
        if self.plan.columns != 4:
            return self.shard
        self.kept = after(self.got, *others)
        on = jnp.concatenate([self.shard, self.kept])
        self.last = self.plan.in_plane(on, 3 - self.order)
        return on

    def pieces(self, first, count, slot, offset, when):
        if self.plan.columns != 4:
            whole = self.plan.whole(self.shard[first : first + count])
            return [(whole, 0, whole.shape[0], slot, None, 0, when)]
        rows_all = self.shard.shape[0]
        near, far = (1, 2) if self.order == 1 else (2, 1)
        return [
            (self.shard, first, count, slot, 0, offset, when),
            (self.kept, first, count, slot, near, offset, when),
            (self.last, first, count, slot, far, offset, when),
            (self.last, rows_all + first, count, slot, 3, offset, when),
        ]


class Sum:
    def __init__(self, plan, layer, order, pieces):
        self.plan, self.layer, self.stage = plan, layer, 0
        self.ways = [1, 2] if order == 3 else [order]
        self.send, self.keep = pieces[0::2], pieces[1::2]
        if plan.columns == 4:
            self.got = [plan.in_plane(v, way) for v, way in zip(self.send, self.ways)]
        else:
            parts = []
            for k in range(4):
                for send, keep, way in zip(self.send, self.keep, self.ways):
                    kinds = ((0, 2), (1, 3)) if way == 1 else ((0, 1), (2, 3))
                    parts.append(keep[kinds[0].index(k)] if k in kinds[0] else send[kinds[1].index(k)])
            whole = jnp.concatenate(parts, axis=1)
            self.done = [
                lax.psum_scatter(whole, AXES, axis_index_groups=plan.groups(), scatter_dimension=1, tiled=True)
            ]
            self.stage = 1

    def advance(self, *others):
        plan = self.plan
        if self.stage == 4:
            return ()
        self.stage += 1
        if self.stage == 1:
            got = [after(v, *others) for v in self.got]
            self.mine = [k[0] + v[0] for k, v in zip(self.keep, got)]
            on = [k[1] + v[1] for k, v in zip(self.keep, got)]
            self.got = [plan.in_plane(v, 3 - way) for v, way in zip(on, self.ways)]
            return on
        if self.stage == 2:
            if plan.columns == 4:
                got = [after(v, *others) for v in self.got]
                opposite = [m[1] + v[1] for m, v in zip(self.mine, got)]
                par = [m[0] + v[0] for m, v in zip(self.mine, got)]
            else:
                opposite, par = [v[1] for v in self.done], [v[0] for v in self.done]
            opposite = jnp.concatenate(opposite)
            self.par = jnp.concatenate(par)
            self.got = plan.along_z(opposite, 1)
            return (opposite,)
        if self.stage == 3:
            self.par = self.par + after(self.got, *others)
            far = (0, 1) if self.layer == 1 else (2, 3)
            self.got = plan.along_z(self.par, 2, far)
            return (self.par,)
        self.par = self.par + after(self.got, *others)
        return (self.par,)

    def finish(self):
        while self.stage < 4:
            self.advance()
        return self.par


def body(
    tokens, absorbed, timesteps, mask_embedding, time_table,
    attn_gain, attn_shift, joint_weight, pair_bias, out_weight, out_bias,
    ffn_gain, ffn_shift, up_weight, up_bias, down_weight, down_bias, cotangent,
):
    plan = Plan(lax.axis_size("section"), lax.axis_size("dp"))
    z, column, core = plan.z, plan.column, plan.core
    columns = plan.columns
    width = tokens.shape[1]
    inner = out_weight.shape[1]
    hidden = up_weight.shape[2]
    inner_half, hidden_half = inner // 2, hidden // 2
    block = hidden_half // columns
    low_planes = z < 2

    joint_half = lax.dynamic_index_in_dim(joint_weight[0].reshape(width, 3, 2, inner_half), core, 2, keepdims=False)
    joint_half = joint_half.reshape(width, 3 * inner_half).T
    out_half = lax.dynamic_slice_in_dim(out_weight[0], core * inner_half, inner_half, 0)
    own_attn = jnp.concatenate([joint_half, out_half], axis=0)
    up_half = lax.dynamic_index_in_dim(up_weight[0].reshape(width, columns, 2, block), core, 2, keepdims=False)
    own_up = up_half.reshape(width, hidden_half).T
    down_half = lax.dynamic_index_in_dim(down_weight[0].reshape(columns, 2, block, width), core, 1, keepdims=False)
    own_down = down_half.reshape(hidden_half, width)
    own = (own_attn, own_up, own_down)

    own_vec = jnp.stack(
        [attn_gain[0], attn_shift[0], pair_bias[0], out_bias[0], ffn_gain[0], ffn_shift[0], down_bias[0]]
        + [up_bias[0, k * width : (k + 1) * width] for k in range(hidden // width)]
    )
    vec_count = own_vec.shape[0]
    count = width // columns

    def shard_of(matrix):
        return lax.dynamic_slice_in_dim(matrix, column * count, count, 0)

    tail = jnp.zeros((-vec_count % 8, width), f32)
    shards = [jnp.concatenate([shard_of(own[0]), own_vec, tail]), shard_of(own[1]), shard_of(own[2])]
    far, far_opp = [], []
    for shard in shards:
        far.append(plan.along_z(after(shard, *far[-1:]), 2))
    near_attn = plan.along_z(shards[0], 1)
    far_opp.append(plan.along_z(far[0], 1))
    near_feed = plan.along_z(after(jnp.concatenate(shards[1:]), far_opp[0]), 1)
    near_opp = (near_attn, near_feed[:count], near_feed[count:])
    far_opp += [plan.along_z(far[1], 1), plan.along_z(far[2], 1)]
    opp = [
        [jnp.where(low_planes == (layer == 0), near_opp[k], far_opp[k]) for k in range(3)] for layer in range(2)
    ]

    near_vec = jnp.stack([own_vec, near_attn[count : count + vec_count]])
    far_vec = jnp.stack([far[0][count : count + vec_count], far_opp[0][count : count + vec_count]])
    vectors = jnp.stack([jnp.where(low_planes, near_vec, far_vec), jnp.where(low_planes, far_vec, near_vec)])
    pair_all = lax.dynamic_index_in_dim(vectors[:, :, 2].reshape(2, 2, 2, 2, inner_half), core, 3, keepdims=False)
    pair_rows = jnp.stack([pair_all[:, :, 0], jnp.zeros_like(pair_all[:, :, 0]), pair_all[:, :, 1]], axis=2)
    pair_cols = pair_rows.reshape(2, 2 * 3 * inner_half, 1)
    up_rows = lax.dynamic_index_in_dim(
        vectors[:, :, 7:].reshape(2, 2, columns, 2, block), core, 3, keepdims=False
    ).reshape(2, 2, hidden_half)

    natural = jnp.arange(4, dtype=jnp.int32)
    order = column ^ natural if columns == 4 else natural
    flags = [
        jnp.concatenate([(low_planes == (layer == 0)).astype(jnp.int32)[None], order.astype(jnp.int32)])
        for layer in range(2)
    ]

    local = core == z // 2
    which = z % 2

    def fetch(array):
        piece = lax.dynamic_slice_in_dim(array, which * LEN, LEN, 0)
        other = plan.permute(piece, lambda zz, d: (zz, d ^ 1) if d % 2 == zz // 2 else None)
        return jnp.where(local, piece, other)

    absorbed, tokens, cotangent = (after(v, far[0]) for v in (absorbed, tokens, cotangent))
    mask_row = fetch(absorbed).astype(f32)
    sequence = 4 * column + z
    step = lax.dynamic_index_in_dim(timesteps, sequence, 0, keepdims=False)
    step_row = lax.dynamic_slice_in_dim(time_table, step, 1, 0)
    mask = mask_row[:, None]
    x = jnp.where(mask > 0.5, mask_embedding[None, :] + step_row, fetch(tokens))
    weight = LEN / jnp.maximum(jnp.sum(mask_row), 1.0)
    g = fetch(cotangent) * (mask * weight)

    half = count // 2
    far_group, near_group = Group(plan, far[0], 1), Group(plan, near_attn, 2)
    rest = [Group(plan, far_opp[0][:half], 1), Group(plan, far_opp[0][half:count], 2)]
    for group in (far_group, near_group, *rest):
        group.step()
    ups = Group(plan, jnp.concatenate([far[1], opp[0][1]]), 1)
    downs = Group(plan, jnp.concatenate([far[2], opp[0][2]]), 2)
    lasts = Group(plan, jnp.concatenate([opp[1][1], opp[1][2]]), 1)

    def own_rows(matrix):
        return [(matrix, 0, matrix.shape[0], 0, None, 0, "near")]

    attn_pieces = Pieces(
        own_rows(own[0])
        + far_group.pieces(0, count, 0, 0, "far")
        + near_group.pieces(0, count, 1, 0, "near")
        + (
            rest[0].pieces(0, half, 1, 0, "far") + rest[1].pieces(0, half, 1, half, "far")
            if columns == 4
            else [(plan.whole(far_opp[0][:count]), 0, width, 1, None, 0, "far")]
        )
    )

    kept = []
    added = ()
    for layer in range(2):
        vec = vectors[layer]
        if layer == 0:
            x = after(x, g, ups.shard)
        x, xh, xl, x_scale, ph, pl_, wh, wl = attn_in(flags[layer], x, added, vec, pair_cols[layer], attn_pieces)
        if layer == 0:
            ph = after(ph, downs.shard, ups.step(ph))
        oh, ol, lse, *part = attn_heads(ph, pl_, wh, wl, vec)
        if layer == 0:
            part[0] = after(part[0], downs.step(part[0]))
            up_opp, down_opp = ups.pieces(count, count, 1, 0, "all"), downs.pieces(count, count, 1, 0, "all")
        else:
            up_opp, down_opp = lasts.pieces(0, count, 1, 0, "all"), lasts.pieces(count, count, 1, 0, "all")
        up_pieces = Pieces(own_rows(own[1]) + ups.pieces(0, count, 0, 0, "far") + up_opp)
        y, yh, yl, y_scale, hh, hl, slope, uh, ul = feed_up(
            flags[layer], x, plan.added(*part), vec, up_rows[layer], up_pieces
        )
        down_pieces = Pieces(own_rows(own[2]) + downs.pieces(0, count, 0, 0, "far") + down_opp)
        *feed_part, dh, dl = feed_down(flags[layer], hh, hl, vec, down_pieces)
        if layer == 0:
            feed_part[0] = after(feed_part[0], lasts.step(feed_part[0]))
        kept.append((vec, xh, xl, x_scale, ph, pl_, wh, wl, oh, ol, lse, yh, yl, y_scale, hh, hl, slope, uh, ul, dh, dl))
        added = plan.added(*feed_part)
        x = y
    last = (x, *added)

    quarter = width // plan.planes

    def spread(value):
        def cut(plane):
            cols = lax.dynamic_slice_in_dim(value, plane * quarter, quarter, 1)
            return jnp.concatenate([cols[: LEN // 2], cols[LEN // 2 :]], axis=1)

        def open_up(packed):
            return jnp.concatenate([packed[:, :quarter], packed[:, quarter:]], axis=0)

        arrived = [cut(z)]
        for step in range(1, plan.planes):
            arrived.append(
                plan.permute(cut(z ^ step), lambda zz, d: (zz ^ step, d) if d % 2 == zz // 2 else None)
            )
        result = []
        for index in range(2):
            distance = z ^ (2 * core + index)
            result.append(open_up(lax.select_n(distance, *arrived)))
        return jnp.concatenate(result, axis=0)

    def steps(token, *numbers):
        return [v for number in numbers for v in sums[number].advance(token)]

    pulled = ()
    small = [None] * 2
    sums = []
    for layer in (1, 0):
        (vec, xh, xl, x_scale, ph, pl_, wh, wl, oh, ol, lse, yh, yl, y_scale, hh, hl, slope, uh, ul, dh, dl) = kept[layer]
        order = 1 if layer == 1 else 2
        g, duh, dul, *pieces, up_bias_sum, down_bias_sum = feed_back_one(
            order, flags[layer], g, pulled, dh, dl, hh, hl, slope
        )
        sums.append(Sum(plan, layer, order, pieces))
        if layer == 1:
            final = after(last[0], up_bias_sum) + jnp.concatenate([last[1] + last[3], last[2] + last[4]])
            out_rows = spread(final)
        else:
            duh = after(duh, *steps(up_bias_sum, 0, 1))
        *e, ffn_vec = feed_back_two("e", 0, flags[layer], duh, dul, yh, yl, vec, uh, ul)
        e = plan.added(*e)
        duh = after(duh, ffn_vec)
        if layer == 0:
            duh = after(duh, *steps(ffn_vec, 2))
        pieces = feed_back_two("w", 3 - order, flags[layer], duh, dul, yh, yl, vec, uh, ul)
        sums.append(Sum(plan, layer, 3 - order, pieces))
        g, e = after(g, pieces[0]), (*e[:2], after(e[2], pieces[0]), after(e[3], pieces[0]))
        if layer == 0:
            g = after(g, *steps(pieces[0], 1, 2))
        g, doh, dol, do, out_bias_sum = attn_back_one(g, e, yh, yl, y_scale, wh, wl, oh, ol)
        grads = attn_heads_back(ph, pl_, doh, dol, oh, ol, lse)
        if layer == 1:
            do, first = after(do, *steps(grads[0], 0, 1)), after(grads[0], out_rows)
            *e, attn_vec = attn_back_two("e", 0, flags[layer], [first, *grads[1:]], xh, xl, vec, wh, wl, do)
            e = plan.added(*e)
            do = after(do, *steps(attn_vec, 0))
            *pieces, pair_sum = attn_back_two("w", order, flags[layer], grads, xh, xl, vec, wh, wl, do)
            sums.append(Sum(plan, layer, order, pieces))
            g = after(g, pair_sum, *steps(pair_sum, 0, 1))
            e = (*e[:2], after(e[2], pair_sum), after(e[3], pair_sum))
        else:
            do = after(do, *steps(grads[0], 2, 3, 4))
            *pieces, pair_sum = attn_back_two("w", 3, flags[layer], grads, xh, xl, vec, wh, wl, do)
            sums.append(Sum(plan, layer, 3, pieces))
            first = after(grads[0], *steps(pair_sum, 3))
            *e, attn_vec = attn_back_two("e", 0, flags[layer], [first, *grads[1:]], xh, xl, vec, wh, wl, do)
            e = plan.added(*e)
        pulled = (*e, xh, xl, x_scale)
        small[layer] = (attn_vec, pair_sum, out_bias_sum, ffn_vec, up_bias_sum, down_bias_sum)
    input_grad, row_sum = finish(g, pulled[:4], *pulled[4:], mask)
    grad_rows = spread(input_grad)

    pack_flags = jnp.stack([z % 2, core, sequence]).astype(jnp.int32)
    table = plan.all_sum(pack(pack_flags, small, row_sum, columns, timesteps.shape[0]))

    def settle(index):
        return jnp.where(low_planes, sums[3 + index].finish(), sums[index].finish())

    down_mine, up_mine, attn_mine = (settle(index) for index in range(3))

    def exchange(rows_all):
        halves = rows_all.reshape(2, -1, width)
        mine = lax.dynamic_index_in_dim(halves, core, 0, keepdims=False)
        theirs = plan.across(lax.dynamic_index_in_dim(halves, 1 - core, 0, keepdims=False))
        first = core == 0
        return jnp.where(first, mine, theirs), jnp.where(first, theirs, mine)

    zero, one = exchange(attn_mine)
    count = zero.shape[0]
    joint = jnp.stack([v[:, : 3 * inner_half].reshape(count, 3, inner_half) for v in (zero, one)], axis=2)
    joint_grad = joint.reshape(count, 3 * inner)
    out_grad = jnp.concatenate([zero[:, 3 * inner_half :], one[:, 3 * inner_half :]], axis=1).T
    zero, one = exchange(down_mine)
    down_grad = jnp.stack([v.reshape(count, columns, block) for v in (zero, one)], axis=2).reshape(count, hidden).T
    up_grad = up_mine.reshape(-1, width).T

    mine = lax.dynamic_slice_in_dim(table, VEC_ROWS * z, VEC_ROWS, 0)
    device = 2 * column + core
    share = lax.dynamic_slice_in_dim(mine, device * (width // plan.dp), width // plan.dp, 1)
    up_count = hidden // width
    up_share = lax.dynamic_slice_in_dim(
        mine[7 : 7 + up_count].reshape(-1), device * (hidden // plan.dp), hidden // plan.dp, 0
    )

    seq_rows = table[4 * VEC_ROWS : 4 * VEC_ROWS + timesteps.shape[0]]
    seq_cols = lax.dynamic_slice_in_dim(seq_rows, z * quarter, quarter, 1)
    picks = (timesteps[:, None] == jnp.arange(time_table.shape[0], dtype=jnp.int32)[None, :]).astype(f32)
    table_grad = jnp.einsum("st,sd->td", picks, seq_cols, precision=lax.Precision.HIGHEST)
    mask_grad = jnp.sum(seq_cols, axis=0)

    return (
        out_rows,
        grad_rows,
        mask_grad,
        table_grad,
        share[0:1],
        share[1:2],
        joint_grad[None],
        share[2:3],
        out_grad[None],
        share[3:4],
        share[4:5],
        share[5:6],
        up_grad[None],
        up_share[None],
        down_grad[None],
        share[6:7],
    )


def solution(mesh):
    placed = (
        P("dp", None), P("dp"), P(), P(), P(),
        P("section", None), P("section", None), P("section", None, None), P("section", None),
        P("section", None, None), P("section", None), P("section", None), P("section", None),
        P("section", None, None), P("section", None), P("section", None, None), P("section", None),
        P("dp", None),
    )
    vector = P("section", "dp")
    return jax.shard_map(
        body,
        mesh=mesh,
        in_specs=placed,
        out_specs=(
            P("dp", "section"), P("dp", "section"), P("section"), P(None, "section"),
            vector, vector, P("section", "dp", None), vector, P("section", None, "dp"), vector,
            vector, vector, P("section", None, "dp"), vector, P("section", None, "dp"), vector,
        ),
        check_vma=False,
    )
```

```python
import functools
import math

import jax
import jax.numpy as jnp
from jax import lax
from jax.experimental import pallas as pl
from jax.experimental.pallas import tpu as pltpu
from jax.sharding import PartitionSpec as P

HS = 64
LEN = 1024
EPS = 1e-05
AXES = ("section", "dp")
f32 = jnp.float32
bf16 = jnp.bfloat16

NN = ((1,), (0,))
NT = ((1,), (1,))
TN = ((0,), (0,))
BM = 256
VMEM_LIMIT = 60 * 1024 * 1024


def dot(a, b, dims):
    return lax.dot_general(a, b, (dims, ((), ())), preferred_element_type=f32)


def split(value):
    high = value.astype(bf16)
    return high, (value - high.astype(f32)).astype(bf16)


def dot3(ah, al, bh, bl, dims):
    return dot(ah, bh, dims) + (dot(ah, bl, dims) + dot(al, bh, dims))


def unit_rows(x):
    center = x - jnp.mean(x, axis=-1, keepdims=True)
    scale = lax.rsqrt(jnp.mean(center * center, axis=-1, keepdims=True) + EPS)
    return center * scale, scale


def pull_rows(n, scale, e):
    return (e - jnp.mean(e, axis=-1, keepdims=True) - n * jnp.mean(e * n, axis=-1, keepdims=True)) * scale


class Pieces:
    def __init__(self, entries):
        self.arrays, self.entries = [], []
        for array, *rest in entries:
            index = next((i for i, known in enumerate(self.arrays) if known is array), len(self.arrays))
            if index == len(self.arrays):
                self.arrays.append(array)
            self.entries.append((index, *rest))


def load_split(entries, flags, refs, stage, sems, high_out, low_out):
    quarter = stage.shape[1] // 4
    near = flags[0] == 1
    copies = {"near": [], "far": [], "all": []}
    for number, (index, first, count, slot, place, offset, when) in enumerate(entries):
        row = offset if place is None else pl.multiple_of(flags[1 + place] * quarter + offset, 8)
        copies[when].append(
            pltpu.make_async_copy(
                refs[index].at[pl.ds(first, count)], stage.at[slot, pl.ds(row, count)], sems.at[number]
            )
        )
    for act in ("start", "wait"):

        @pl.when(near)
        def _():
            for copy in copies["near"]:
                getattr(copy, act)()

        @pl.when(jnp.logical_not(near))
        def _():
            for copy in copies["far"]:
                getattr(copy, act)()

        for copy in copies["all"]:
            getattr(copy, act)()
    for slot in range(2):
        high, low = split(stage[slot])
        high_out[slot] = high
        low_out[slot] = low


def store_pieces(flags, read, order, refs):
    split_rows = order == 3
    for number, ref in enumerate(refs):
        send = number % 2 == 0
        along = 1 + number // 2 if split_rows else order
        kinds = ((1, 3) if send else (0, 2)) if along == 1 else ((2, 3) if send else (0, 1))
        count = ref.shape[2]
        for slot in range(2):
            for place, k in enumerate(kinds):
                step = 2 * count if split_rows else count
                row = pl.multiple_of(flags[1 + k] * step + (number // 2) * count, 8)
                ref[place, slot] = read(slot, row, count)


def full(shape):
    zeros = (0,) * len(shape)
    return pl.BlockSpec(shape, lambda i: zeros)


def rows(width, bm=BM):
    return pl.BlockSpec((bm, width), lambda i: (i, 0))


def lanes(height, bm=BM):
    return pl.BlockSpec((height, bm), lambda i: (0, i))


def halves(width, bm=BM):
    first = LEN // bm // 2
    return [
        pl.BlockSpec((bm, width), lambda i: (jnp.minimum(i, first - 1), 0)),
        pl.BlockSpec((bm, width), lambda i: (jnp.maximum(i - first, 0), 0)),
    ]


def read_halves(first, second):
    early = pl.program_id(0) < pl.num_programs(0) // 2
    return jnp.where(early, first[...], second[...])


def write_halves(first, second, value):
    early = pl.program_id(0) < pl.num_programs(0) // 2

    @pl.when(early)
    def _():
        first[...] = value

    @pl.when(jnp.logical_not(early))
    def _():
        second[...] = value


ANY = pl.BlockSpec(memory_space=pl.ANY)
SMEM = pl.BlockSpec(memory_space=pltpu.SMEM)


class Rider:
    def __init__(self, count, *segments):
        self.count, self.segments = count, segments

    def arrays(self):
        return [v for a, _, b, _ in self.segments for v in (a, b)]

    def specs(self, grid):
        each = grid // len(self.segments)
        block, width = self.count // each, self.segments[0][0].shape[1]
        result = []
        for number, (_, first_a, _, first_b) in enumerate(self.segments):
            for first in (first_a, first_b):
                def place(i, start=number * each, base=first // block):
                    return (base + jnp.clip(i - start, 0, each - 1), 0)

                result.append(pl.BlockSpec((block, width), place))
        return result

    def out(self, grid):
        width = self.segments[0][0].shape[1]
        total = self.count * len(self.segments)
        return pl.BlockSpec((total // grid, width), lambda i: (i, 0)), ((total, width), f32)

    def run(self, grid, refs, out):
        each = grid // len(self.segments)
        value = refs[0][...] + refs[1][...]
        for number in range(1, len(self.segments)):
            other = refs[2 * number][...] + refs[2 * number + 1][...]
            value = jnp.where(pl.program_id(0) >= number * each, other, value)
        out[...] = value


def call(kernel, grid, in_specs, out_specs, out_shapes, scratch, name, flops, nbytes, *args, riders=()):
    ins, outs = len(in_specs), len(out_specs)
    extra = [v for rider in riders for v in rider.arrays()]
    in_specs = list(in_specs) + [v for rider in riders for v in rider.specs(grid)]
    rider_outs = [rider.out(grid) for rider in riders]

    def whole(*refs):
        mine, refs = refs[:ins], refs[ins:]
        sources, refs = refs[: len(extra)], refs[len(extra) :]
        results, refs = refs[:outs], refs[outs:]
        sums, refs = refs[: len(riders)], refs[len(riders) :]
        kernel(*mine, *results, *refs)
        for rider, out in zip(riders, sums):
            own, sources = sources[: len(rider.arrays())], sources[len(rider.arrays()) :]
            rider.run(grid, own, out)

    return pl.pallas_call(
        whole,
        grid=(grid,),
        in_specs=in_specs,
        out_specs=list(out_specs) + [spec for spec, _ in rider_outs],
        out_shape=[jax.ShapeDtypeStruct(s, t) for s, t in list(out_shapes) + [shape for _, shape in rider_outs]],
        scratch_shapes=scratch,
        name=name,
        cost_estimate=pl.CostEstimate(flops=1, bytes_accessed=1, transcendentals=0),
        compiler_params=pltpu.CompilerParams(
            vmem_limit_bytes=VMEM_LIMIT, dimension_semantics=("arbitrary",)
        ),
    )(*args, *extra)


def attn_in_kernel(added, entries, count, flags, *refs):
    base = refs[0]
    refs = refs[1:]
    if added:
        added_refs, refs = refs[:4], refs[4:]
    vec, bias = refs[:2]
    sources, refs = refs[2 : 2 + count], refs[2 + count :]
    if added:
        x_out = refs[0]
        refs = refs[1:]
    nh_out, nl_out, scale_out, ph_out, pl_out, wh_out, wl_out, stage, sems = refs
    inner = 3 * (ph_out.shape[0] // 6)

    @pl.when(pl.program_id(0) == 0)
    def _():
        load_split(entries, flags, sources, stage, sems, wh_out, wl_out)

    x = base[...]
    if added:
        x = x + (read_halves(*added_refs[:2]) + read_halves(*added_refs[2:]))
        x_out[...] = x
    n, scale = unit_rows(x)
    high, low = split(n)
    nh_out[...] = high
    nl_out[...] = low
    scale_out[...] = scale
    third = inner // 3
    for slot in range(2):
        ah, al = split(n * vec[slot, 0:1, :] + vec[slot, 1:2, :])
        projected = dot3(wh_out[slot, :inner], wl_out[slot, :inner], ah, al, NT)
        projected = projected + bias[slot * inner : (slot + 1) * inner]
        queries = projected[:third] * (1.0 / math.sqrt(HS))
        for first, value in ((0, queries), (third, projected[third:])):
            high, low = split(value)
            start = slot * inner + first
            ph_out[start : start + value.shape[0]] = high
            pl_out[start : start + value.shape[0]] = low


def attn_in(flags, x, added, vec, bias, pieces):
    length, width = x.shape
    inner = bias.shape[0] // 2
    outs = [((length, width), f32)] if added else []
    out_specs = [rows(width)] if added else []
    outs += [
        ((length, width), bf16),
        ((length, width), bf16),
        ((length, 1), f32),
        ((2 * inner, length), bf16),
        ((2 * inner, length), bf16),
        ((2, width, width), bf16),
        ((2, width, width), bf16),
    ]
    out_specs += [rows(width), rows(width), rows(1), lanes(2 * inner), lanes(2 * inner)]
    out_specs += [full((2, width, width))] * 2
    in_specs = [SMEM, rows(width)] + halves(width) * (len(added) // 2) + [full(vec.shape), full(bias.shape)]
    in_specs += [ANY] * len(pieces.arrays)
    result = call(
        functools.partial(attn_in_kernel, bool(added), pieces.entries, len(pieces.arrays)),
        length // BM,
        in_specs,
        out_specs,
        outs,
        [pltpu.VMEM((2, width, width), f32), pltpu.SemaphoreType.DMA((len(pieces.entries),))],
        "attn_in",
        6 * length * width * 2 * inner,
        20e6,
        flags, x, *added, vec, bias, *pieces.arrays,
    )
    if not added:
        result = [x] + list(result)
    return result


def heads_kernel(qh, ql, kh, kl, vh, vl, wh, wl, vec, oh_out, ol_out, lse_out, part_a, part_b, oh_all, ol_all):
    head = pl.program_id(0)
    keys = jnp.concatenate([kh[...], kh[...], kl[...]], axis=0)
    values = jnp.concatenate([vh[...], vl[...]], axis=0)
    value_high = vh[...]
    for block in range(qh.shape[1] // BM):
        cut = slice(block * BM, (block + 1) * BM)
        queries = jnp.concatenate([qh[:, cut], ql[:, cut], qh[:, cut]], axis=0)
        scores = dot(keys, queries, TN)
        top = jnp.max(scores, axis=0, keepdims=True)
        weights = jnp.exp(scores - top)
        total = jnp.sum(weights, axis=0, keepdims=True)
        high, low = split(weights)
        both = dot(values, high, NN)
        attended = (both[:HS] + (both[HS:] + dot(value_high, low, NN))) / total
        high, low = split(attended)
        oh_out[:, cut] = high
        ol_out[:, cut] = low
        lse_out[0, :, cut] = top + jnp.log(total)
    place = pl.ds(pl.multiple_of(head * HS, HS), HS)
    oh_all[place, :] = oh_out[...]
    ol_all[place, :] = ol_out[...]

    @pl.when(head == pl.num_programs(0) - 1)
    def _():
        inner, width = oh_all.shape[0], wh.shape[2]
        offset = 0.5 * (vec[0, 3:4, :] + vec[1, 3:4, :])
        for part, cut in ((part_a, slice(0, LEN // 2)), (part_b, slice(LEN // 2, LEN))):
            part[...] = offset + dot3(
                oh_all[:, cut], ol_all[:, cut], wh[...].reshape(inner, width), wl[...].reshape(inner, width), TN
            )


def head_spec(length, which, half_heads):
    return pl.BlockSpec(
        (HS, length), lambda h: (3 * half_heads * (h // half_heads) + which * half_heads + h % half_heads, 0)
    )


def attn_heads(ph, pl_, wh, wl, vec):
    inner2, length = ph.shape
    width = wh.shape[2]
    heads = inner2 // (3 * HS)
    half = heads // 2
    out_rows = half * HS
    specs = []
    for which in range(3):
        specs += [head_spec(length, which, half)] * 2
    tail = pl.BlockSpec((2, out_rows, width), lambda h: (0, width // out_rows - 1, 0))
    return call(
        heads_kernel,
        heads,
        specs + [tail, tail, full(vec.shape)],
        [
            pl.BlockSpec((HS, length), lambda h: (h, 0)),
            pl.BlockSpec((HS, length), lambda h: (h, 0)),
            pl.BlockSpec((1, 1, length), lambda h: (h, 0, 0)),
            full((length // 2, width)),
            full((length // 2, width)),
        ],
        [
            ((heads * HS, length), bf16),
            ((heads * HS, length), bf16),
            ((heads, 1, length), f32),
            ((length // 2, width), f32),
            ((length // 2, width), f32),
        ],
        [pltpu.VMEM((heads * HS, length), bf16)] * 2,
        "attn_heads",
        heads * length * length * HS * 2 * 10,
        15e6,
        ph, pl_, ph, pl_, ph, pl_, wh, wl, vec,
    )


def gate(u):
    phi = 0.5 * (1.0 + lax.erf(u * math.sqrt(0.5)))
    slope = phi + u * (jnp.exp(-0.5 * u * u) * (1.0 / math.sqrt(2.0 * math.pi)))
    return u * phi, slope


def feed_up_kernel(entries, count, flags, base, mine_a, mine_b, other_a, other_b, vec, bias, *refs):
    y_out, nh_out, nl_out, scale_out, hh_out, hl_out, slope_out, uh_out, ul_out, stage, sems = refs[count:]
    hidden = stage.shape[1]

    @pl.when(pl.program_id(0) == 0)
    def _():
        load_split(entries, flags, refs[:count], stage, sems, uh_out, ul_out)

    y = base[...] + (read_halves(mine_a, mine_b) + read_halves(other_a, other_b))
    y_out[...] = y
    n, scale = unit_rows(y)
    high, low = split(n)
    nh_out[...] = high
    nl_out[...] = low
    scale_out[...] = scale
    for slot in range(2):
        ah, al = split(n * vec[slot, 4:5, :] + vec[slot, 5:6, :])
        before = dot3(ah, al, uh_out[slot], ul_out[slot], NT) + bias[slot : slot + 1, :]
        active, slope = gate(before)
        cut = slice(slot * hidden, (slot + 1) * hidden)
        slope_out[:, cut] = slope
        high, low = split(active)
        hh_out[:, cut] = high
        hl_out[:, cut] = low


def feed_up(flags, base, added, vec, bias, pieces):
    length, width = base.shape
    hidden = bias.shape[1]
    weight = ((2, hidden, width), bf16)
    return call(
        functools.partial(feed_up_kernel, pieces.entries, len(pieces.arrays)),
        length // BM,
        [SMEM, rows(width)] + halves(width) * 2 + [full(vec.shape), full(bias.shape)] + [ANY] * len(pieces.arrays),
        [rows(width)] * 3 + [rows(1)] + [rows(2 * hidden)] * 3 + [full(weight[0])] * 2,
        [
            ((length, width), f32),
            ((length, width), bf16),
            ((length, width), bf16),
            ((length, 1), f32),
            ((length, 2 * hidden), bf16),
            ((length, 2 * hidden), bf16),
            ((length, 2 * hidden), f32),
            weight, weight,
        ],
        [pltpu.VMEM((2, hidden, width), f32), pltpu.SemaphoreType.DMA((len(pieces.entries),))],
        "feed_up",
        6 * length * width * 2 * hidden,
        40e6,
        flags, base, *added, vec, bias, *pieces.arrays,
    )


def feed_down_kernel(entries, count, flags, hh, hl, vec, *refs):
    part_a, part_b, dh_out, dl_out, stage, sems = refs[count:]
    hidden = stage.shape[1]

    @pl.when(pl.program_id(0) == 0)
    def _():
        load_split(entries, flags, refs[:count], stage, sems, dh_out, dl_out)

    partial = 0.5 * (vec[0, 6:7, :] + vec[1, 6:7, :])
    for slot in range(2):
        cut = slice(slot * hidden, (slot + 1) * hidden)
        partial = partial + dot3(hh[:, cut], hl[:, cut], dh_out[slot], dl_out[slot], NN)
    write_halves(part_a, part_b, partial)


def feed_down(flags, hh, hl, vec, pieces):
    length, hidden, width = hh.shape[0], hh.shape[1] // 2, vec.shape[2]
    weight = ((2, hidden, width), bf16)
    return call(
        functools.partial(feed_down_kernel, pieces.entries, len(pieces.arrays)),
        length // BM,
        [SMEM] + [rows(2 * hidden)] * 2 + [full(vec.shape)] + [ANY] * len(pieces.arrays),
        halves(width) + [full(weight[0])] * 2,
        [((length // 2, width), f32)] * 2 + [weight, weight],
        [pltpu.VMEM((2, hidden, width), f32), pltpu.SemaphoreType.DMA((len(pieces.entries),))],
        "feed_down",
        6 * length * width * 2 * hidden,
        25e6,
        flags, hh, hl, vec, *pieces.arrays,
    )


def piece_outs(width, order):
    count = 4 if order == 3 else 2
    shape = (2, 2, width // 2 // count, width)
    return [full(shape)] * count, [(shape, f32)] * count


def feed_back_one_kernel(pulled, order, flags, g_in, *refs):
    if pulled:
        added_refs, (nh, nl, scale) = refs[:4], refs[4:7]
        refs = refs[7:]
    (dh, dl, hh, hl, slope, g_out, uh_out, ul_out, *piece_refs, bias_out, total_out, acc) = refs
    step = pl.program_id(0)
    hidden = dh.shape[1]
    g = g_in[...]
    if pulled:
        n = nh[...].astype(f32) + nl[...].astype(f32)
        g = g + pull_rows(n, scale[...], read_halves(*added_refs[:2]) + read_halves(*added_refs[2:]))
    g_out[...] = g

    @pl.when(step == 0)
    def _():
        acc[...] = jnp.zeros_like(acc)
        bias_out[...] = jnp.zeros_like(bias_out)
        total_out[...] = jnp.zeros_like(total_out)

    total_out[...] += jnp.sum(g, axis=0, keepdims=True)
    gh, gl = split(g)
    for slot in range(2):
        cut = slice(slot * hidden, (slot + 1) * hidden)
        delta = dot3(gh, gl, dh[slot], dl[slot], NT) * slope[:, cut]
        bias_out[slot : slot + 1, :] += jnp.sum(delta, axis=0, keepdims=True)
        high, low = split(delta)
        uh_out[:, cut] = high
        ul_out[:, cut] = low
        acc[slot] += dot3(gh, gl, hh[:, cut], hl[:, cut], TN)

    @pl.when(step == pl.num_programs(0) - 1)
    def _():
        store_pieces(flags, lambda slot, row, count: acc[slot, pl.ds(row, count), :], order, piece_refs)


def feed_back_one(order, flags, g, pulled, dh, dl, hh, hl, slope, riders=()):
    length, width = g.shape
    hidden = dh.shape[1]
    piece_specs, piece_shapes = piece_outs(width, order)
    pulled_specs = halves(width) * 2 + [rows(width)] * 2 + [rows(1)] if pulled else []
    return call(
        functools.partial(feed_back_one_kernel, bool(pulled), order),
        length // BM,
        [SMEM, rows(width)] + pulled_specs + [full(dh.shape)] * 2 + [rows(2 * hidden)] * 3,
        [rows(width)] + [rows(2 * hidden)] * 2 + piece_specs + [full((2, hidden)), full((1, width))],
        [((length, width), f32), ((length, 2 * hidden), bf16), ((length, 2 * hidden), bf16)]
        + piece_shapes
        + [((2, hidden), f32), ((1, width), f32)],
        [pltpu.VMEM((2, width, hidden), f32)],
        "feed_back_one",
        6 * length * width * 4 * hidden,
        40e6,
        flags, g, *pulled, dh, dl, hh, hl, slope,
        riders=riders,
    )


def feed_back_two_kernel(parts, order, flags, uh, ul, nh, nl, vec, *refs):
    if "e" in parts:
        wh, wl, e_a, e_b, vec_out = refs
    else:
        *piece_refs, acc = refs
    step = pl.program_id(0)
    hidden = uh.shape[1] // 2

    @pl.when(step == 0)
    def _():
        if "e" in parts:
            vec_out[...] = jnp.zeros_like(vec_out)
        else:
            acc[...] = jnp.zeros_like(acc)

    n = nh[...].astype(f32) + nl[...].astype(f32)
    e = None
    for slot in range(2):
        cut = slice(slot * hidden, (slot + 1) * hidden)
        gain = vec[slot, 4:5, :]
        if "e" in parts:
            delta = dot3(uh[:, cut], ul[:, cut], wh[slot], wl[slot], NN)
            vec_out[2 * slot : 2 * slot + 1, :] += jnp.sum(delta * n, axis=0, keepdims=True)
            vec_out[2 * slot + 1 : 2 * slot + 2, :] += jnp.sum(delta, axis=0, keepdims=True)
            e = delta * gain if e is None else e + delta * gain
        else:
            ah, al = split(n * gain + vec[slot, 5:6, :])
            acc[slot] += dot3(uh[:, cut], ul[:, cut], ah, al, TN)
    if "e" in parts:
        write_halves(e_a, e_b, e)
    else:

        @pl.when(step == pl.num_programs(0) - 1)
        def _():
            store_pieces(flags, lambda slot, row, count: acc[slot, pl.ds(row, count), :], order, piece_refs)


def feed_back_two(parts, order, flags, uh, ul, nh, nl, vec, wh, wl, riders=()):
    length, width = nh.shape
    hidden = wh.shape[1]
    piece_specs, piece_shapes = piece_outs(width, order)
    if parts == "e":
        weights, out_specs = (wh, wl), halves(width) + [full((4, width))]
        out_shapes = [((length // 2, width), f32)] * 2 + [((4, width), f32)]
    else:
        weights, out_specs, out_shapes = (), piece_specs, piece_shapes
    return call(
        functools.partial(feed_back_two_kernel, parts, order),
        length // BM,
        [SMEM] + [rows(2 * hidden)] * 2 + [rows(width)] * 2 + [full(vec.shape)] + [full(w.shape) for w in weights],
        out_specs,
        out_shapes,
        [pltpu.VMEM((2, hidden, width), f32)] if parts == "w" else [],
        "feed_back_two_" + parts,
        6 * length * width * 2 * hidden,
        25e6,
        flags, uh, ul, nh, nl, vec, *weights,
        riders=riders,
    )


def attn_back_one_kernel(
    g_in, mine_a, mine_b, other_a, other_b, nh, nl, scale, wh, wl, oh, ol, g_out, dh_out, dl_out, do_out, total_out
):
    step = pl.program_id(0)
    inner, width = oh.shape[0], g_in.shape[1]

    @pl.when(step == 0)
    def _():
        do_out[...] = jnp.zeros_like(do_out)
        total_out[...] = jnp.zeros_like(total_out)

    n = nh[...].astype(f32) + nl[...].astype(f32)
    g = g_in[...] + pull_rows(n, scale[...], read_halves(mine_a, mine_b) + read_halves(other_a, other_b))
    g_out[...] = g
    total_out[...] += jnp.sum(g, axis=0, keepdims=True)
    gh, gl = split(g)
    delta = dot3(wh[...].reshape(inner, width), wl[...].reshape(inner, width), gh, gl, NT)
    high, low = split(delta)
    dh_out[...] = high
    dl_out[...] = low
    do_out[...] += dot3(oh[...], ol[...], gh, gl, NN)


def attn_back_one(g, added, nh, nl, scale, wh, wl, oh, ol, riders=()):
    length, width = g.shape
    inner = oh.shape[0]
    out_rows = inner // 2
    tail = pl.BlockSpec((2, out_rows, width), lambda i: (0, width // out_rows - 1, 0))
    return call(
        attn_back_one_kernel,
        length // BM,
        [rows(width)] + halves(width) * 2 + [rows(width)] * 2 + [rows(1)] + [tail, tail] + [lanes(inner)] * 2,
        [rows(width), lanes(inner), lanes(inner), full((inner, width)), full((1, width))],
        [
            ((length, width), f32),
            ((inner, length), bf16),
            ((inner, length), bf16),
            ((inner, width), f32),
            ((1, width), f32),
        ],
        [],
        "attn_back_one",
        6 * length * width * 2 * inner,
        20e6,
        g, *added, nh, nl, scale, wh, wl, oh, ol,
        riders=riders,
    )


def heads_back_kernel(qh, ql, kh, kl, vh, vl, dh, dl, oh, ol, lse, dqh, dql, dkh, dkl, dvh, dvl, acc_k, acc_v):
    keys = jnp.concatenate([kh[...], kh[...], kl[...]], axis=0)
    keys_two = jnp.concatenate([kh[...], kl[...]], axis=0)
    values = jnp.concatenate([vh[...], vh[...], vl[...]], axis=0)
    key_high = kh[...]
    for block in range(qh.shape[1] // BM):
        cut = slice(block * BM, (block + 1) * BM)
        q_high, q_low = qh[:, cut], ql[:, cut]
        d_high, d_low = dh[:, cut], dl[:, cut]
        delta = d_high.astype(f32) + d_low.astype(f32)
        attended = oh[:, cut].astype(f32) + ol[:, cut].astype(f32)
        diagonal = jnp.sum(delta * attended, axis=0, keepdims=True)
        scores = dot(keys, jnp.concatenate([q_high, q_low, q_high], axis=0), TN)
        probs = jnp.exp(scores - lse[0, :, cut])
        p_high, p_low = split(probs)
        delta_probs = dot(values, jnp.concatenate([d_high, d_low, d_high], axis=0), TN)
        delta_scores = probs * (delta_probs - diagonal)
        s_high, s_low = split(delta_scores)
        both = dot(jnp.concatenate([d_high, d_low], axis=0), p_high, NT)
        part_v = both[:HS] + (both[HS:] + dot(d_high, p_low, NT))
        both = dot(jnp.concatenate([q_high, q_low], axis=0), s_high, NT)
        part_k = both[:HS] + (both[HS:] + dot(q_high, s_low, NT))
        if block == 0:
            acc_v[...] = part_v
            acc_k[...] = part_k
        else:
            acc_v[...] += part_v
            acc_k[...] += part_k
        both = dot(keys_two, s_high, NN)
        delta_q = (both[:HS] + (both[HS:] + dot(key_high, s_low, NN))) * (1.0 / math.sqrt(HS))
        high, low = split(delta_q)
        dqh[:, cut] = high
        dql[:, cut] = low
    high, low = split(acc_k[...])
    dkh[...] = high
    dkl[...] = low
    high, low = split(acc_v[...])
    dvh[...] = high
    dvl[...] = low


def attn_heads_back(ph, pl_, dh, dl, oh, ol, lse, riders=()):
    inner2, length = ph.shape
    heads = inner2 // (3 * HS)
    half = heads // 2
    specs = []
    for which in range(3):
        specs += [head_spec(length, which, half)] * 2
    plain = pl.BlockSpec((HS, length), lambda h: (h, 0))
    return call(
        heads_back_kernel,
        heads,
        specs + [plain] * 4 + [pl.BlockSpec((1, 1, length), lambda h: (h, 0, 0))],
        [plain] * 6,
        [((heads * HS, length), bf16)] * 6,
        [pltpu.VMEM((HS, length), f32)] * 2,
        "attn_heads_back",
        heads * length * length * HS * 2 * 26,
        15e6,
        ph, pl_, ph, pl_, ph, pl_, dh, dl, oh, ol, lse,
        riders=riders,
    )


def attn_back_two_kernel(parts, order, flags, *refs):
    dqh, dql, dkh, dkl, dvh, dvl, nh, nl, vec = refs[:9]
    refs = refs[9:]
    if "e" in parts:
        (wh, wl), refs = refs[:2], refs[2:]
    if "w" in parts:
        do, refs = refs[0], refs[1:]
    if "e" in parts:
        (e_a, e_b, vec_out), refs = refs[:3], refs[3:]
    if "w" in parts:
        *piece_refs, pair_out, acc, turned = refs
    step = pl.program_id(0)
    third = dqh.shape[0] // 2
    inner = 3 * third

    @pl.when(step == 0)
    def _():
        if "e" in parts:
            vec_out[...] = jnp.zeros_like(vec_out)
        if "w" in parts:
            acc[...] = jnp.zeros_like(acc)
            pair_out[...] = jnp.zeros_like(pair_out)

    n = nh[...].astype(f32) + nl[...].astype(f32)
    ones = jnp.ones((8, n.shape[0]), bf16)
    e = None
    for slot in range(2):
        cut = slice(slot * third, (slot + 1) * third)
        high = jnp.concatenate([dqh[cut], dkh[cut], dvh[cut]], axis=0)
        low = jnp.concatenate([dql[cut], dkl[cut], dvl[cut]], axis=0)
        gain = vec[slot, 0:1, :]
        if "w" in parts:
            ah, al = split(n * gain + vec[slot, 1:2, :])
            acc[slot] += dot3(high, low, ah, al, NN)
            pair_out[slot] += dot(ones, high, NT) + dot(ones, low, NT)
        if "e" in parts:
            delta = dot3(high, low, wh[slot, :inner], wl[slot, :inner], TN)
            vec_out[2 * slot : 2 * slot + 1, :] += jnp.sum(delta * n, axis=0, keepdims=True)
            vec_out[2 * slot + 1 : 2 * slot + 2, :] += jnp.sum(delta, axis=0, keepdims=True)
            e = delta * gain if e is None else e + delta * gain
    if "e" in parts:
        write_halves(e_a, e_b, e)

    if "w" in parts:

        @pl.when(step == pl.num_programs(0) - 1)
        def _():
            for slot in range(2):
                whole = jnp.concatenate([acc[slot], do[slot * third : (slot + 1) * third]], axis=0)
                turned[slot] = jnp.transpose(whole)
            store_pieces(flags, lambda slot, row, count: turned[slot, pl.ds(row, count), :], order, piece_refs)


def attn_back_two(parts, order, flags, grads, nh, nl, vec, wh, wl, do, riders=()):
    length, width = nh.shape
    heads_rows = grads[0].shape[0]
    inner = 3 * heads_rows // 2
    piece_specs, piece_shapes = piece_outs(width, order)
    in_specs = [SMEM] + [lanes(heads_rows)] * 6 + [rows(width)] * 2 + [full(vec.shape)]
    args = [flags, *grads, nh, nl, vec]
    out_specs, out_shapes, scratch = [], [], []
    if "e" in parts:
        in_specs += [full(wh.shape)] * 2
        args += [wh, wl]
        out_specs += halves(width) + [full((4, width))]
        out_shapes += [((length // 2, width), f32)] * 2 + [((4, width), f32)]
    if "w" in parts:
        in_specs += [full(do.shape)]
        args += [do]
        out_specs += piece_specs + [full((2, 8, inner))]
        out_shapes += piece_shapes + [((2, 8, inner), f32)]
        scratch = [pltpu.VMEM((2, inner, width), f32), pltpu.VMEM((2, width, width), f32)]
    return call(
        functools.partial(attn_back_two_kernel, parts, order),
        length // BM,
        in_specs,
        out_specs,
        out_shapes,
        scratch,
        "attn_back_two_" + parts,
        6 * length * width * 2 * inner * len(parts),
        15e6 * len(parts),
        *args,
        riders=riders,
    )


def by_planes(flags, value, near_out, far_out):
    quarter = value.shape[1] // 4
    parts = [value[:, k * quarter : (k + 1) * quarter] for k in range(4)]
    odd, high = flags[0] % 2 == 1, flags[0] // 2 == 1
    parts = [jnp.where(odd, parts[k ^ 1], parts[k]) for k in range(4)]
    parts = [jnp.where(high, parts[k ^ 2], parts[k]) for k in range(4)]
    near_out[...] = jnp.concatenate([parts[0], parts[2]], axis=1)
    far_out[...] = jnp.concatenate([parts[1], parts[3]], axis=1)


def finish_kernel(flags, g_in, mine_a, mine_b, other_a, other_b, nh, nl, scale, mask, near_out, far_out, sums_out):
    @pl.when(pl.program_id(0) == 0)
    def _():
        sums_out[...] = jnp.zeros_like(sums_out)

    n = nh[...].astype(f32) + nl[...].astype(f32)
    g = g_in[...] + pull_rows(n, scale[...], read_halves(mine_a, mine_b) + read_halves(other_a, other_b))
    absorbed = mask[...]
    by_planes(flags, g * (1.0 - absorbed), near_out, far_out)
    sums_out[...] += jnp.sum(g * absorbed, axis=0, keepdims=True)


def finish(flags, g, added, nh, nl, scale, mask, riders=()):
    length, width = g.shape
    return call(
        finish_kernel,
        length // BM,
        [SMEM, rows(width)] + halves(width) * 2 + [rows(width)] * 2 + [rows(1)] * 2,
        [rows(width // 2)] * 2 + [full((1, width))],
        [((length, width // 2), f32)] * 2 + [((1, width), f32)],
        [],
        "finish",
        10 * length * width,
        15e6,
        flags, g, *added, nh, nl, scale, mask,
        riders=riders,
    )


def leave_kernel(flags, base, mine_a, mine_b, other_a, other_b, near_out, far_out):
    value = base[...] + (read_halves(mine_a, mine_b) + read_halves(other_a, other_b))
    by_planes(flags, value, near_out, far_out)


def leave(flags, base, added):
    length, width = base.shape
    return call(
        leave_kernel,
        length // BM,
        [SMEM, rows(width)] + halves(width) * 2,
        [rows(width // 2)] * 2,
        [((length, width // 2), f32)] * 2,
        [],
        "leave",
        10 * length * width,
        10e6,
        flags, base, *added,
    )


VEC_ROWS = 10


def pack_kernel(columns, flags, *refs):
    table = refs[-1]
    row_sum = refs[-2]
    width = row_sum.shape[1]
    odd, core, sequence = flags[0], flags[1], flags[2]
    table[...] = jnp.zeros_like(table)

    def place(parts):
        zero = jnp.zeros_like(parts[0])
        first = jnp.concatenate([v for p in parts for v in (p, zero)], axis=1)
        second = jnp.concatenate([v for p in parts for v in (zero, p)], axis=1)
        return jnp.where(core == 0, first, second)

    for layer in range(2):
        attn_vec, pair_sum, out_total, ffn_vec, up_sum, down_total = refs[6 * layer : 6 * layer + 6]
        third = pair_sum.shape[2] // 3
        block = up_sum.shape[1] // columns
        for slot in range(2):
            section = 2 * layer + jnp.where(odd == 1, 1 - slot, slot)
            base = section * VEC_ROWS

            def put(row, value):
                table[pl.ds(base + row, 1), :] = value

            put(0, attn_vec[2 * slot : 2 * slot + 1, :])
            put(1, attn_vec[2 * slot + 1 : 2 * slot + 2, :])
            pair = pair_sum[slot, 0:1, :]
            put(2, place([pair[:, :third], pair[:, 2 * third :]]))
            put(3, 0.5 * out_total[...])
            put(4, ffn_vec[2 * slot : 2 * slot + 1, :])
            put(5, ffn_vec[2 * slot + 1 : 2 * slot + 2, :])
            put(6, 0.5 * down_total[...])
            ups = up_sum[slot : slot + 1, :]
            spread = place([ups[:, k * block : (k + 1) * block] for k in range(columns)])
            for k in range(spread.shape[1] // width):
                put(7 + k, spread[:, k * width : (k + 1) * width])
    table[pl.ds(4 * VEC_ROWS + sequence, 1), :] = 0.5 * row_sum[...]


def pack(flags, small, row_sum, columns, sequences):
    width = row_sum.shape[1]
    arrays = [*small[0], *small[1], row_sum]
    count = -(-(4 * VEC_ROWS + sequences) // 8) * 8
    return call(
        functools.partial(pack_kernel, columns),
        1,
        [SMEM] + [full(v.shape) for v in arrays],
        [full((count, width))],
        [((count, width), f32)],
        [],
        "pack",
        1e4,
        1e6,
        flags, *arrays,
    )[0]


def after(value, *others):
    return lax.optimization_barrier((value, *others))[0]


class Plan:
    def __init__(self, planes, dp):
        self.planes, self.dp, self.columns = planes, dp, dp // 2
        self.z = lax.axis_index("section")
        device = lax.axis_index("dp")
        self.column, self.core = device // 2, device % 2

    def permute(self, value, target):
        pairs = []
        for z in range(self.planes):
            for d in range(self.dp):
                to = target(z, d)
                if to is not None:
                    pairs.append((z * self.dp + d, to[0] * self.dp + to[1]))
        return lax.ppermute(value, AXES, pairs)

    def groups(self):
        return [
            [z * self.dp + 2 * j + c for j in range(self.columns)] for z in range(self.planes) for c in range(2)
        ]

    def across(self, value):
        return self.permute(value, lambda z, d: (z, d ^ 1))

    def added(self, first, second):
        return (first, second, self.across(first), self.across(second))

    def along_z(self, value, bit, planes=None):
        return self.permute(value, lambda z, d: (z ^ bit, d) if planes is None or z in planes else None)

    def in_plane(self, value, bit):
        return self.permute(value, lambda z, d: (z, d ^ (2 * bit)))

    def whole(self, shard):
        return lax.all_gather(shard, AXES, axis_index_groups=self.groups(), axis=0, tiled=True)

    def sum_step(self, table, step):
        if self.columns != 4:
            return lax.psum(table, AXES) if step == 0 else table
        if step == 0:
            return table + self.across(table)
        if step < 3:
            return table + self.in_plane(table, step)
        return table + self.along_z(table, step - 2)


class Group:
    def __init__(self, plan, shard, order):
        self.plan, self.shard, self.order = plan, shard, order
        if plan.columns == 4:
            self.got = plan.in_plane(shard, order)

    def step(self):
        if self.plan.columns != 4:
            return self.shard
        self.kept = self.got
        on = jnp.concatenate([self.shard, self.kept])
        self.last = self.plan.in_plane(on, 3 - self.order)
        return on

    def pieces(self, first, count, slot, offset, when):
        if self.plan.columns != 4:
            whole = self.plan.whole(self.shard[first : first + count])
            return [(whole, 0, whole.shape[0], slot, None, 0, when)]
        rows_all = self.shard.shape[0]
        near, far = (1, 2) if self.order == 1 else (2, 1)
        return [
            (self.shard, first, count, slot, 0, offset, when),
            (self.kept, first, count, slot, near, offset, when),
            (self.last, first, count, slot, far, offset, when),
            (self.last, rows_all + first, count, slot, 3, offset, when),
        ]


def arrive(groups, *others):
    names = [(g, "got" if not hasattr(g, "last") else "last") for g in groups if g.plan.columns == 4]
    values = lax.optimization_barrier((*(getattr(g, name) for g, name in names), *others))
    for (group, name), value in zip(names, values):
        setattr(group, name, value)
    return values[len(names) :]


class Sum:
    def __init__(self, plan, order, pieces):
        self.plan, self.stage = plan, 0
        self.ways = [1, 2] if order == 3 else [order]
        self.count = pieces[0].shape[2]
        width = pieces[0].shape[3]
        if plan.columns == 4:
            send, keep = ([v.reshape(-1, width) for v in pieces[k::2]] for k in (0, 1))
            self.mine = keep
            self.got = [plan.in_plane(v, way) for v, way in zip(send, self.ways)]
        else:
            parts = []
            for k in range(4):
                for send, keep, way in zip(pieces[0::2], pieces[1::2], self.ways):
                    kinds = ((0, 2), (1, 3)) if way == 1 else ((0, 1), (2, 3))
                    parts.append(keep[kinds[0].index(k)] if k in kinds[0] else send[kinds[1].index(k)])
            whole = jnp.concatenate(parts, axis=1)
            whole = lax.psum_scatter(whole, AXES, axis_index_groups=plan.groups(), scatter_dimension=1, tiled=True)
            self.whole = [whole]

    def merge(self, other):
        if self.plan.columns == 4:
            self.mine, self.got = self.mine + other.mine, self.got + other.got
        else:
            self.whole = self.whole + other.whole
        return self

    def riders(self):
        if self.plan.columns != 4 or self.stage == 3:
            return []
        count = self.count
        pairs = list(zip(self.mine, self.got))
        if self.stage == 0:
            return [Rider(2 * count, (m, first, v, first)) for first in (0, 2 * count) for m, v in pairs]
        if self.stage == 1:
            return [Rider(count, *((m, first, v, first) for m, v in pairs)) for first in (0, count)]
        return [Rider(self.mine[0].shape[0], *((m, 0, v, 0) for m, v in pairs))]

    def take(self, values):
        if not values:
            return self.advance()
        plan = self.plan
        self.stage += 1
        if self.stage == 1:
            half = len(values) // 2
            self.mine = values[:half]
            self.got = [plan.in_plane(v, 3 - way) for v, way in zip(values[half:], self.ways)]
        elif self.stage == 2:
            self.mine = values[:1]
            self.got = [plan.along_z(values[1], 1)]
        else:
            self.mine = values
        return values

    def advance(self):
        if self.stage == 3:
            return []
        if self.plan.columns == 4:
            values = []
            for rider in self.riders():
                parts = [
                    a[i : i + rider.count] + b[j : j + rider.count] for a, i, b, j in rider.segments
                ]
                values.append(parts[0] if len(parts) == 1 else jnp.concatenate(parts))
            return self.take(values)
        if self.stage == 0:
            self.stage = 1
            return []
        if self.stage == 1:
            return self.take([jnp.concatenate([w[slot] for w in self.whole]) for slot in range(2)])
        return self.take([self.mine[0] + self.got[0]])

    def wait(self, *others):
        if self.plan.columns != 4 and self.stage < 2:
            return others
        self.got, others = lax.optimization_barrier((self.got, others))
        return others

    def after(self, *others):
        if self.plan.columns == 4 and self.stage < 3:
            self.got = [after(v, *others) for v in self.got]
        return self

    def finish(self):
        while self.stage < 3:
            self.advance()
        return self.mine[0]


def body(
    tokens, absorbed, timesteps, mask_embedding, time_table,
    attn_gain, attn_shift, joint_weight, pair_bias, out_weight, out_bias,
    ffn_gain, ffn_shift, up_weight, up_bias, down_weight, down_bias, cotangent,
):
    plan = Plan(lax.axis_size("section"), lax.axis_size("dp"))
    z, column, core = plan.z, plan.column, plan.core
    columns = plan.columns
    width = tokens.shape[1]
    inner = out_weight.shape[1]
    hidden = up_weight.shape[2]
    inner_half, hidden_half = inner // 2, hidden // 2
    block = hidden_half // columns
    low_planes = z < 2

    joint_half = lax.dynamic_index_in_dim(joint_weight[0].reshape(width, 3, 2, inner_half), core, 2, keepdims=False)
    joint_half = joint_half.reshape(width, 3 * inner_half).T
    out_half = lax.dynamic_slice_in_dim(out_weight[0], core * inner_half, inner_half, 0)
    own_attn = jnp.concatenate([joint_half, out_half], axis=0)
    up_half = lax.dynamic_index_in_dim(up_weight[0].reshape(width, columns, 2, block), core, 2, keepdims=False)
    own_up = up_half.reshape(width, hidden_half).T
    down_half = lax.dynamic_index_in_dim(down_weight[0].reshape(columns, 2, block, width), core, 1, keepdims=False)
    own_down = down_half.reshape(hidden_half, width)
    own = (own_attn, own_up, own_down)

    own_vec = jnp.stack(
        [attn_gain[0], attn_shift[0], pair_bias[0], out_bias[0], ffn_gain[0], ffn_shift[0], down_bias[0]]
        + [up_bias[0, k * width : (k + 1) * width] for k in range(hidden // width)]
    )
    vec_count = own_vec.shape[0]
    count = width // columns

    def shard_of(matrix):
        return lax.dynamic_slice_in_dim(matrix, column * count, count, 0)

    local = core == z // 2
    which = z % 2
    sequence = 4 * column + z

    def fetch(array):
        piece = lax.dynamic_slice_in_dim(array, which * LEN, LEN, 0)
        return piece, plan.permute(piece, lambda zz, d: (zz, d ^ 1) if d % 2 == zz // 2 else None)

    tail = jnp.zeros((-vec_count % 8, width), f32)
    shard = jnp.concatenate([shard_of(own[0]), own_vec, tail])
    far_attn, near_attn = plan.along_z(shard, 2), plan.along_z(shard, 1)
    mask_parts, token_parts = fetch(after(absorbed, shard)), fetch(after(tokens, shard))
    far_attn, near_attn, mask_other, token_other, up_shard, down_shard = lax.optimization_barrier(
        (far_attn, near_attn, mask_parts[1], token_parts[1], shard_of(own[1]), shard_of(own[2]))
    )
    opp_attn = plan.along_z(far_attn, 1)
    far_up = plan.along_z(up_shard, 2)
    token_parts = (*token_parts, token_other)

    near_vec = jnp.stack([own_vec, near_attn[count : count + vec_count]])
    far_vec = jnp.stack([far_attn[count : count + vec_count], opp_attn[count : count + vec_count]])
    vectors = jnp.stack([jnp.where(low_planes, near_vec, far_vec), jnp.where(low_planes, far_vec, near_vec)])

    def opposite(near, far):
        return jnp.where(low_planes, near, far), jnp.where(low_planes, far, near)

    attn_opp = opposite(near_attn[:count], opp_attn[:count])
    attn_groups = [Group(plan, far_attn[:count], 1), Group(plan, attn_opp[0], 2)]
    near_up = plan.along_z(after(up_shard, attn_opp[0]), 1)
    far_up, near_up = arrive(attn_groups, far_up, near_up)
    sent = [group.step() for group in attn_groups]
    mask_other, token_parts = lax.optimization_barrier((mask_other, token_parts, *sent))[:2]
    mask_row = jnp.where(local, mask_parts[0], mask_other).astype(f32)
    step = lax.dynamic_index_in_dim(timesteps, sequence, 0, keepdims=False)
    step_row = lax.dynamic_slice_in_dim(time_table, step, 1, 0)
    mask = mask_row[:, None]
    x = jnp.where(mask > 0.5, mask_embedding[None, :] + step_row, jnp.where(local, token_parts[0], token_parts[2]))
    weight = LEN / jnp.maximum(jnp.sum(mask_row), 1.0)
    far_down = plan.along_z(after(down_shard, far_up), 2)
    opp_up = plan.along_z(far_up, 1)
    opp_up, x = arrive(attn_groups, opp_up, x)
    near_down = plan.along_z(after(down_shard, opp_up), 1)
    up_opp = opposite(near_up, opp_up)
    pair_all = lax.dynamic_index_in_dim(vectors[:, :, 2].reshape(2, 2, 2, 2, inner_half), core, 3, keepdims=False)
    pair_rows = jnp.stack([pair_all[:, :, 0], jnp.zeros_like(pair_all[:, :, 0]), pair_all[:, :, 1]], axis=2)
    pair_cols = pair_rows.reshape(2, 2 * 3 * inner_half, 1)
    up_rows = lax.dynamic_index_in_dim(
        vectors[:, :, 7:].reshape(2, 2, columns, 2, block), core, 3, keepdims=False
    ).reshape(2, 2, hidden_half)

    natural = jnp.arange(4, dtype=jnp.int32)
    order = column ^ natural if columns == 4 else natural
    flags = [
        jnp.concatenate([(low_planes == (layer == 0)).astype(jnp.int32)[None], order.astype(jnp.int32)])
        for layer in range(2)
    ]

    def own_rows(matrix):
        return [(matrix, 0, matrix.shape[0], 0, None, 0, "near")]

    def pieces_of(matrix, par, opp):
        return Pieces(own_rows(matrix) + par.pieces(0, count, 0, 0, "far") + opp)

    kept = []

    def keep(layer, *values):
        kept.append((vectors[layer], *values))

    half = count // 2
    up_groups = [Group(plan, far_up, 1), Group(plan, up_opp[0], 2)]
    x, xh, xl, x_scale, ph, pl_, wh, wl = attn_in(
        flags[0], x, (), vectors[0], pair_cols[0], pieces_of(own[0], attn_groups[0], attn_groups[1].pieces(0, count, 1, 0, "all"))
    )
    ph, far_down, near_down, cotangent = arrive(up_groups, ph, far_down, near_down, cotangent)
    cot_parts = fetch(cotangent)
    opp_down = plan.along_z(far_down, 1)
    for group in up_groups:
        group.step()
    oh, ol, lse, *part = attn_heads(ph, pl_, wh, wl, vectors[0])
    opp_down, *part = arrive(up_groups, opp_down, *part)
    down_opp = opposite(near_down, opp_down)
    down_groups = [Group(plan, far_down, 1), Group(plan, down_opp[0], 2)]
    added = plan.added(*part)
    added = added[:2] + arrive(down_groups, *added[2:])
    for group in down_groups:
        group.step()
    if columns == 4:
        last_attn = [Group(plan, attn_opp[1][:half], 1), Group(plan, attn_opp[1][half:], 2)]
    else:
        last_attn = [Group(plan, attn_opp[1], 1)]
    y, yh, yl, y_scale, hh, hl, slope, uh, ul = feed_up(
        flags[0], x, added, vectors[0], up_rows[0], pieces_of(own[1], up_groups[0], up_groups[1].pieces(0, count, 1, 0, "all"))
    )
    hh, cot_other = arrive(last_attn, hh, cot_parts[1])
    for group in last_attn:
        group.step()
    *feed_part, dh, dl = feed_down(
        flags[0], hh, hl, vectors[0], pieces_of(own[2], down_groups[0], down_groups[1].pieces(0, count, 1, 0, "all"))
    )
    keep(0, xh, xl, x_scale, ph, pl_, wh, wl, oh, ol, lse, yh, yl, y_scale, hh, hl, slope, uh, ul, dh, dl)

    g = jnp.where(local, cot_parts[0], after(cot_other, dh)) * (mask * weight)
    last_groups = [Group(plan, up_opp[1], 1), Group(plan, down_opp[1], 2)]
    feed_part = arrive([*last_attn, *last_groups], *feed_part)
    for group in last_groups:
        group.step()
    added = plan.added(*feed_part)
    if columns == 4:
        attn_last = last_attn[0].pieces(0, half, 1, 0, "all") + last_attn[1].pieces(0, half, 1, half, "all")
    else:
        attn_last = last_attn[0].pieces(0, count, 1, 0, "all")
    x, xh, xl, x_scale, ph, pl_, wh, wl = attn_in(
        flags[1], y, added, vectors[1], pair_cols[1], pieces_of(own[0], attn_groups[0], attn_last)
    )
    oh, ol, lse, *part = attn_heads(ph, pl_, wh, wl, vectors[1])
    added = plan.added(*arrive(last_groups, *part))
    y, yh, yl, y_scale, hh, hl, slope, uh, ul = feed_up(
        flags[1], x, added, vectors[1], up_rows[1], pieces_of(own[1], up_groups[0], last_groups[0].pieces(0, count, 1, 0, "all"))
    )
    *feed_part, dh, dl = feed_down(
        flags[1], hh, hl, vectors[1], pieces_of(own[2], down_groups[0], last_groups[1].pieces(0, count, 1, 0, "all"))
    )
    keep(1, xh, xl, x_scale, ph, pl_, wh, wl, oh, ol, lse, yh, yl, y_scale, hh, hl, slope, uh, ul, dh, dl)
    x, added = y, plan.added(*feed_part)
    last = (x, *added)

    quarter = width // plan.planes
    plane_flags = jnp.stack([z, core]).astype(jnp.int32)

    def beside(value):
        return plan.permute(value, lambda zz, d: (zz ^ 1, d) if d % 2 == zz // 2 else None)

    def beyond(mine, theirs):
        both = jnp.concatenate([mine[:, quarter:], theirs[:, quarter:]], axis=1)
        return plan.permute(both, lambda zz, d: (zz ^ 2, d) if d % 2 == zz // 2 else None)

    def settle_rows(mine, theirs, arrived):
        first = jnp.where(local, mine[:, :quarter], arrived[:, :quarter])
        second = jnp.where(local, theirs[:, :quarter], arrived[:, quarter:])
        odd = z % 2 == 1
        return jnp.concatenate([jnp.where(odd, second, first), jnp.where(odd, first, second)])

    def ride(kernel, riding, *args):
        lists = [total.riders() for total in riding]
        values = list(kernel(*args, riders=[r for some in lists for r in some]))
        taken = sum(len(some) for some in lists)
        results, extra = values[: len(values) - taken], values[len(values) - taken :]
        for total, some in zip(riding, lists):
            total.take(extra[: len(some)])
            extra = extra[len(some) :]
        return results

    small = [None] * 2
    (vec, xh, xl, x_scale, ph, pl_, wh, wl, oh, ol, lse, yh, yl, y_scale, hh, hl, slope, uh, ul, dh, dl) = kept[1]
    g, duh, dul, *pieces, up_bias_sum, down_bias_sum = feed_back_one(1, flags[1], g, (), dh, dl, hh, hl, slope)
    down_1 = Sum(plan, 1, pieces)
    out_near, out_far = leave(plane_flags, after(last[0], up_bias_sum), last[1:])
    out_beside = beside(out_far)
    *e, ffn_vec = feed_back_two("e", 0, flags[1], after(duh, out_near), dul, yh, yl, vec, uh, ul)
    e = plan.added(*e)
    pieces = feed_back_two("w", 2, flags[1], after(duh, ffn_vec), dul, yh, yl, vec, uh, ul)
    up_1 = Sum(plan, 2, pieces)
    g, out_beside, *others = lax.optimization_barrier((g, out_beside, *e[2:], pieces[0]))[:4]
    g, doh, dol, do, out_bias_sum = attn_back_one(g, (*e[:2], *others), yh, yl, y_scale, wh, wl, oh, ol)
    grads = attn_heads_back(ph, pl_, doh, dol, oh, ol, lse)
    *e, attn_vec = ride(attn_back_two, [down_1], "e", 0, flags[1], grads, xh, xl, vec, wh, wl, do)
    e = plan.added(*e)
    out_beyond = beyond(out_near, after(out_beside, attn_vec))
    *pieces, pair_sum = ride(attn_back_two, [up_1], "w", 2, flags[1], grads, xh, xl, vec, wh, wl, after(do, attn_vec))
    attn_1 = Sum(plan, 2, pieces)
    g, *others = lax.optimization_barrier((g, *e[2:], pair_sum))[:3]
    pulled = (*e[:2], *others, xh, xl, x_scale)
    small[1] = (attn_vec, pair_sum, out_bias_sum, ffn_vec, up_bias_sum, down_bias_sum)

    (vec, xh, xl, x_scale, ph, pl_, wh, wl, oh, ol, lse, yh, yl, y_scale, hh, hl, slope, uh, ul, dh, dl) = kept[0]
    g, duh, dul, *pieces, up_bias_sum, down_bias_sum = feed_back_one(1, flags[0], g, pulled, dh, dl, hh, hl, slope)
    down_0 = Sum(plan, 1, pieces)
    feed_1 = down_1.merge(up_1)
    duh, out_beyond = lax.optimization_barrier((duh, out_beyond))
    *e, ffn_vec = ride(feed_back_two, [feed_1], "e", 0, flags[0], duh, dul, yh, yl, vec, uh, ul)
    e = plan.added(*e)
    pieces = feed_back_two("w", 3, flags[0], after(duh, ffn_vec), dul, yh, yl, vec, uh, ul)
    up_0 = Sum(plan, 3, pieces)
    g, *others = lax.optimization_barrier((g, *e[2:], pieces[0]))[:3]
    g, doh, dol, do, out_bias_sum = ride(
        attn_back_one, [feed_1, attn_1, down_0], g, (*e[:2], *others), yh, yl, y_scale, wh, wl, oh, ol
    )
    grads = attn_heads_back(ph, pl_, doh, dol, oh, ol, lse)
    mixed = attn_1.merge(down_0)
    *pieces, pair_sum = ride(attn_back_two, [mixed, up_0], "w", 3, flags[0], grads, xh, xl, vec, wh, wl, do)
    attn_0 = Sum(plan, 3, pieces)
    *e, attn_vec = attn_back_two("e", 0, flags[0], [after(grads[0], pair_sum), *grads[1:]], xh, xl, vec, wh, wl, do)
    e = plan.added(*mixed.wait(*up_0.wait(*e)))
    small[0] = (attn_vec, pair_sum, out_bias_sum, ffn_vec, up_bias_sum, down_bias_sum)
    grad_near, grad_far, row_sum = ride(finish, [up_0, mixed], plane_flags, g, e, xh, xl, x_scale, mask)
    out_rows = settle_rows(out_near, out_beside, out_beyond)

    pack_flags = jnp.stack([z % 2, core, sequence]).astype(jnp.int32)
    grad_beside = beside(grad_far)
    table = pack(pack_flags, small, row_sum, columns, timesteps.shape[0])

    def cross(low, high):
        on = jnp.where(low_planes, high, low)
        return jnp.where(low_planes, low, high), on, plan.along_z(on, 2)

    feed_1, mixed = feed_1.finish(), mixed.finish()
    down_mine, down_on, down_got = cross(mixed[count:], feed_1[:count])
    table = plan.sum_step(table, 0)
    down_got, table = attn_0.wait(down_got, table)
    attn_0.advance()
    table, grad_beside = up_0.wait(*attn_0.wait(table, grad_beside))
    attn_0.advance()
    up_mine, up_on, up_got = cross(up_0.finish(), feed_1[count:])
    table = plan.sum_step(table, 1)
    up_got, table = attn_0.wait(up_got, table)
    attn_mine, attn_on, attn_got = cross(attn_0.finish(), mixed[:count])
    grad_beside, table = lax.optimization_barrier((grad_beside, table, attn_on))[:2]
    grad_beyond = beyond(grad_near, grad_beside)
    for step in (2, 3, 4):
        table = plan.sum_step(table, step)
    grad_rows = settle_rows(grad_near, grad_beside, grad_beyond)
    down_mine, up_mine, attn_mine = down_mine + down_got, up_mine + up_got, attn_mine + attn_got

    def exchange(rows_all):
        halves = rows_all.reshape(2, -1, width)
        mine = lax.dynamic_index_in_dim(halves, core, 0, keepdims=False)
        theirs = plan.across(lax.dynamic_index_in_dim(halves, 1 - core, 0, keepdims=False))
        first = core == 0
        return jnp.where(first, mine, theirs), jnp.where(first, theirs, mine)

    zero, one = exchange(attn_mine)
    count = zero.shape[0]
    joint = jnp.stack([v[:, : 3 * inner_half].reshape(count, 3, inner_half) for v in (zero, one)], axis=2)
    joint_grad = joint.reshape(count, 3 * inner)
    out_grad = jnp.concatenate([zero[:, 3 * inner_half :], one[:, 3 * inner_half :]], axis=1).T
    zero, one = exchange(down_mine)
    down_grad = jnp.stack([v.reshape(count, columns, block) for v in (zero, one)], axis=2).reshape(count, hidden).T
    up_grad = up_mine.reshape(-1, width).T

    mine = lax.dynamic_slice_in_dim(table, VEC_ROWS * z, VEC_ROWS, 0)
    device = 2 * column + core
    share = lax.dynamic_slice_in_dim(mine, device * (width // plan.dp), width // plan.dp, 1)
    up_count = hidden // width
    up_share = lax.dynamic_slice_in_dim(
        mine[7 : 7 + up_count].reshape(-1), device * (hidden // plan.dp), hidden // plan.dp, 0
    )

    seq_rows = table[4 * VEC_ROWS : 4 * VEC_ROWS + timesteps.shape[0]]
    seq_cols = lax.dynamic_slice_in_dim(seq_rows, z * quarter, quarter, 1)
    picks = (timesteps[:, None] == jnp.arange(time_table.shape[0], dtype=jnp.int32)[None, :]).astype(f32)
    table_grad = jnp.einsum("st,sd->td", picks, seq_cols, precision=lax.Precision.HIGHEST)
    mask_grad = jnp.sum(seq_cols, axis=0)

    return (
        out_rows,
        grad_rows,
        mask_grad,
        table_grad,
        share[0:1],
        share[1:2],
        joint_grad[None],
        share[2:3],
        out_grad[None],
        share[3:4],
        share[4:5],
        share[5:6],
        up_grad[None],
        up_share[None],
        down_grad[None],
        share[6:7],
    )


def solution(mesh):
    placed = (
        P("dp", None), P("dp"), P(), P(), P(),
        P("section", None), P("section", None), P("section", None, None), P("section", None),
        P("section", None, None), P("section", None), P("section", None), P("section", None),
        P("section", None, None), P("section", None), P("section", None, None), P("section", None),
        P("dp", None),
    )
    vector = P("section", "dp")
    return jax.shard_map(
        body,
        mesh=mesh,
        in_specs=placed,
        out_specs=(
            P("dp", "section"), P("dp", "section"), P("section"), P(None, "section"),
            vector, vector, P("section", "dp", None), vector, P("section", None, "dp"), vector,
            vector, vector, P("section", None, "dp"), vector, P("section", None, "dp"), vector,
        ),
        check_vma=False,
    )
```

```python
import functools
import math

import jax
import jax.numpy as jnp
from jax import lax
from jax.experimental import pallas as pl
from jax.experimental.pallas import tpu as pltpu
from jax.sharding import PartitionSpec as P

HS = 64
LEN = 1024
EPS = 1e-05
AXES = ("section", "dp")
f32 = jnp.float32
bf16 = jnp.bfloat16

NN = ((1,), (0,))
NT = ((1,), (1,))
TN = ((0,), (0,))
BM = 256
VMEM_LIMIT = 60 * 1024 * 1024


def dot(a, b, dims):
    return lax.dot_general(a, b, (dims, ((), ())), preferred_element_type=f32)


def split(value):
    high = value.astype(bf16)
    return high, (value - high.astype(f32)).astype(bf16)


def dot3(ah, al, bh, bl, dims):
    return dot(ah, bh, dims) + (dot(ah, bl, dims) + dot(al, bh, dims))


def unit_rows(x):
    center = x - jnp.mean(x, axis=-1, keepdims=True)
    scale = lax.rsqrt(jnp.mean(center * center, axis=-1, keepdims=True) + EPS)
    return center * scale, scale


def pull_rows(n, scale, e):
    return (e - jnp.mean(e, axis=-1, keepdims=True) - n * jnp.mean(e * n, axis=-1, keepdims=True)) * scale


class Pieces:
    def __init__(self, entries):
        self.arrays, self.entries = [], []
        for array, *rest in entries:
            index = next((i for i, known in enumerate(self.arrays) if known is array), len(self.arrays))
            if index == len(self.arrays):
                self.arrays.append(array)
            self.entries.append((index, *rest))


def load_split(entries, flags, refs, stage, sems, high_out, low_out):
    quarter = stage.shape[1] // 4
    near = flags[0] == 1
    copies = {"near": [], "far": [], "all": []}
    for number, (index, first, count, slot, place, offset, when) in enumerate(entries):
        row = offset if place is None else pl.multiple_of(flags[1 + place] * quarter + offset, 8)
        copies[when].append(
            pltpu.make_async_copy(
                refs[index].at[pl.ds(first, count)], stage.at[slot, pl.ds(row, count)], sems.at[number]
            )
        )
    for act in ("start", "wait"):

        @pl.when(near)
        def _():
            for copy in copies["near"]:
                getattr(copy, act)()

        @pl.when(jnp.logical_not(near))
        def _():
            for copy in copies["far"]:
                getattr(copy, act)()

        for copy in copies["all"]:
            getattr(copy, act)()
    for slot in range(2):
        high, low = split(stage[slot])
        high_out[slot] = high
        low_out[slot] = low


def store_pieces(flags, read, order, refs):
    split_rows = order == 3
    for number, ref in enumerate(refs):
        send = number % 2 == 0
        along = 1 + number // 2 if split_rows else order
        kinds = ((1, 3) if send else (0, 2)) if along == 1 else ((2, 3) if send else (0, 1))
        count = ref.shape[2]
        for slot in range(2):
            for place, k in enumerate(kinds):
                step = 2 * count if split_rows else count
                row = pl.multiple_of(flags[1 + k] * step + (number // 2) * count, 8)
                ref[place, slot] = read(slot, row, count)


def full(shape):
    zeros = (0,) * len(shape)
    return pl.BlockSpec(shape, lambda i: zeros)


def rows(width, bm=BM):
    return pl.BlockSpec((bm, width), lambda i: (i, 0))


def lanes(height, bm=BM):
    return pl.BlockSpec((height, bm), lambda i: (0, i))


def halves(width, bm=BM):
    first = LEN // bm // 2
    return [
        pl.BlockSpec((bm, width), lambda i: (jnp.minimum(i, first - 1), 0)),
        pl.BlockSpec((bm, width), lambda i: (jnp.maximum(i - first, 0), 0)),
    ]


def read_halves(first, second):
    early = pl.program_id(0) < pl.num_programs(0) // 2
    return jnp.where(early, first[...], second[...])


def write_halves(first, second, value):
    early = pl.program_id(0) < pl.num_programs(0) // 2

    @pl.when(early)
    def _():
        first[...] = value

    @pl.when(jnp.logical_not(early))
    def _():
        second[...] = value


ANY = pl.BlockSpec(memory_space=pl.ANY)
SMEM = pl.BlockSpec(memory_space=pltpu.SMEM)


class Rider:
    def __init__(self, count, *segments):
        self.count, self.segments = count, segments

    def arrays(self):
        return [v for a, _, b, _ in self.segments for v in (a, b)]

    def specs(self, grid):
        each = grid // len(self.segments)
        block, width = self.count // each, self.segments[0][0].shape[1]
        result = []
        for number, (_, first_a, _, first_b) in enumerate(self.segments):
            for first in (first_a, first_b):
                def place(i, start=number * each, base=first // block):
                    return (base + jnp.clip(i - start, 0, each - 1), 0)

                result.append(pl.BlockSpec((block, width), place))
        return result

    def out(self, grid):
        width = self.segments[0][0].shape[1]
        total = self.count * len(self.segments)
        return pl.BlockSpec((total // grid, width), lambda i: (i, 0)), ((total, width), f32)

    def run(self, grid, refs, out):
        each = grid // len(self.segments)
        value = refs[0][...] + refs[1][...]
        for number in range(1, len(self.segments)):
            other = refs[2 * number][...] + refs[2 * number + 1][...]
            value = jnp.where(pl.program_id(0) >= number * each, other, value)
        out[...] = value


def call(kernel, grid, in_specs, out_specs, out_shapes, scratch, name, flops, nbytes, *args, riders=()):
    ins, outs = len(in_specs), len(out_specs)
    extra = [v for rider in riders for v in rider.arrays()]
    in_specs = list(in_specs) + [v for rider in riders for v in rider.specs(grid)]
    rider_outs = [rider.out(grid) for rider in riders]

    def whole(*refs):
        mine, refs = refs[:ins], refs[ins:]
        sources, refs = refs[: len(extra)], refs[len(extra) :]
        results, refs = refs[:outs], refs[outs:]
        sums, refs = refs[: len(riders)], refs[len(riders) :]
        kernel(*mine, *results, *refs)
        for rider, out in zip(riders, sums):
            own, sources = sources[: len(rider.arrays())], sources[len(rider.arrays()) :]
            rider.run(grid, own, out)

    return pl.pallas_call(
        whole,
        grid=(grid,),
        in_specs=in_specs,
        out_specs=list(out_specs) + [spec for spec, _ in rider_outs],
        out_shape=[jax.ShapeDtypeStruct(s, t) for s, t in list(out_shapes) + [shape for _, shape in rider_outs]],
        scratch_shapes=scratch,
        name=name,
        cost_estimate=pl.CostEstimate(flops=1, bytes_accessed=1, transcendentals=0),
        compiler_params=pltpu.CompilerParams(
            vmem_limit_bytes=VMEM_LIMIT, dimension_semantics=("arbitrary",)
        ),
    )(*args, *extra)


def attn_in_kernel(added, entries, count, flags, *refs):
    base = refs[0]
    refs = refs[1:]
    if added:
        added_refs, refs = refs[:4], refs[4:]
    vec, bias = refs[:2]
    sources, refs = refs[2 : 2 + count], refs[2 + count :]
    if added:
        x_out = refs[0]
        refs = refs[1:]
    nh_out, nl_out, scale_out, ph_out, pl_out, wh_out, wl_out, stage, sems = refs
    inner = 3 * (ph_out.shape[0] // 6)

    @pl.when(pl.program_id(0) == 0)
    def _():
        load_split(entries, flags, sources, stage, sems, wh_out, wl_out)

    x = base[...]
    if added:
        x = x + (read_halves(*added_refs[:2]) + read_halves(*added_refs[2:]))
        x_out[...] = x
    n, scale = unit_rows(x)
    high, low = split(n)
    nh_out[...] = high
    nl_out[...] = low
    scale_out[...] = scale
    third = inner // 3
    for slot in range(2):
        ah, al = split(n * vec[slot, 0:1, :] + vec[slot, 1:2, :])
        projected = dot3(wh_out[slot, :inner], wl_out[slot, :inner], ah, al, NT)
        projected = projected + bias[slot * inner : (slot + 1) * inner]
        queries = projected[:third] * (1.0 / math.sqrt(HS))
        for first, value in ((0, queries), (third, projected[third:])):
            high, low = split(value)
            start = slot * inner + first
            ph_out[start : start + value.shape[0]] = high
            pl_out[start : start + value.shape[0]] = low


def attn_in(flags, x, added, vec, bias, pieces):
    length, width = x.shape
    inner = bias.shape[0] // 2
    outs = [((length, width), f32)] if added else []
    out_specs = [rows(width)] if added else []
    outs += [
        ((length, width), bf16),
        ((length, width), bf16),
        ((length, 1), f32),
        ((2 * inner, length), bf16),
        ((2 * inner, length), bf16),
        ((2, width, width), bf16),
        ((2, width, width), bf16),
    ]
    out_specs += [rows(width), rows(width), rows(1), lanes(2 * inner), lanes(2 * inner)]
    out_specs += [full((2, width, width))] * 2
    in_specs = [SMEM, rows(width)] + halves(width) * (len(added) // 2) + [full(vec.shape), full(bias.shape)]
    in_specs += [ANY] * len(pieces.arrays)
    result = call(
        functools.partial(attn_in_kernel, bool(added), pieces.entries, len(pieces.arrays)),
        length // BM,
        in_specs,
        out_specs,
        outs,
        [pltpu.VMEM((2, width, width), f32), pltpu.SemaphoreType.DMA((len(pieces.entries),))],
        "attn_in",
        6 * length * width * 2 * inner,
        20e6,
        flags, x, *added, vec, bias, *pieces.arrays,
    )
    if not added:
        result = [x] + list(result)
    return result


def heads_kernel(qh, ql, kh, kl, vh, vl, wh, wl, vec, oh_out, ol_out, lse_out, part_a, part_b, oh_all, ol_all):
    head = pl.program_id(0)
    keys = jnp.concatenate([kh[...], kh[...], kl[...]], axis=0)
    values = jnp.concatenate([vh[...], vl[...]], axis=0)
    value_high = vh[...]
    for block in range(qh.shape[1] // BM):
        cut = slice(block * BM, (block + 1) * BM)
        queries = jnp.concatenate([qh[:, cut], ql[:, cut], qh[:, cut]], axis=0)
        scores = dot(keys, queries, TN)
        top = jnp.max(scores, axis=0, keepdims=True)
        weights = jnp.exp(scores - top)
        total = jnp.sum(weights, axis=0, keepdims=True)
        high, low = split(weights)
        both = dot(values, high, NN)
        attended = (both[:HS] + (both[HS:] + dot(value_high, low, NN))) / total
        high, low = split(attended)
        oh_out[:, cut] = high
        ol_out[:, cut] = low
        lse_out[0, :, cut] = top + jnp.log(total)
    place = pl.ds(pl.multiple_of(head * HS, HS), HS)
    oh_all[place, :] = oh_out[...]
    ol_all[place, :] = ol_out[...]

    @pl.when(head == pl.num_programs(0) - 1)
    def _():
        inner, width = oh_all.shape[0], wh.shape[2]
        offset = 0.5 * (vec[0, 3:4, :] + vec[1, 3:4, :])
        for part, cut in ((part_a, slice(0, LEN // 2)), (part_b, slice(LEN // 2, LEN))):
            part[...] = offset + dot3(
                oh_all[:, cut], ol_all[:, cut], wh[...].reshape(inner, width), wl[...].reshape(inner, width), TN
            )


def head_spec(length, which, half_heads):
    return pl.BlockSpec(
        (HS, length), lambda h: (3 * half_heads * (h // half_heads) + which * half_heads + h % half_heads, 0)
    )


def attn_heads(ph, pl_, wh, wl, vec):
    inner2, length = ph.shape
    width = wh.shape[2]
    heads = inner2 // (3 * HS)
    half = heads // 2
    out_rows = half * HS
    specs = []
    for which in range(3):
        specs += [head_spec(length, which, half)] * 2
    tail = pl.BlockSpec((2, out_rows, width), lambda h: (0, width // out_rows - 1, 0))
    return call(
        heads_kernel,
        heads,
        specs + [tail, tail, full(vec.shape)],
        [
            pl.BlockSpec((HS, length), lambda h: (h, 0)),
            pl.BlockSpec((HS, length), lambda h: (h, 0)),
            pl.BlockSpec((1, 1, length), lambda h: (h, 0, 0)),
            full((length // 2, width)),
            full((length // 2, width)),
        ],
        [
            ((heads * HS, length), bf16),
            ((heads * HS, length), bf16),
            ((heads, 1, length), f32),
            ((length // 2, width), f32),
            ((length // 2, width), f32),
        ],
        [pltpu.VMEM((heads * HS, length), bf16)] * 2,
        "attn_heads",
        heads * length * length * HS * 2 * 10,
        15e6,
        ph, pl_, ph, pl_, ph, pl_, wh, wl, vec,
    )


def gate(u):
    phi = 0.5 * (1.0 + lax.erf(u * math.sqrt(0.5)))
    slope = phi + u * (jnp.exp(-0.5 * u * u) * (1.0 / math.sqrt(2.0 * math.pi)))
    return u * phi, slope


def feed_up_kernel(entries, count, flags, base, mine_a, mine_b, other_a, other_b, vec, bias, *refs):
    y_out, nh_out, nl_out, scale_out, hh_out, hl_out, slope_out, uh_out, ul_out, stage, sems = refs[count:]
    hidden = stage.shape[1]

    @pl.when(pl.program_id(0) == 0)
    def _():
        load_split(entries, flags, refs[:count], stage, sems, uh_out, ul_out)

    y = base[...] + (read_halves(mine_a, mine_b) + read_halves(other_a, other_b))
    y_out[...] = y
    n, scale = unit_rows(y)
    high, low = split(n)
    nh_out[...] = high
    nl_out[...] = low
    scale_out[...] = scale
    for slot in range(2):
        ah, al = split(n * vec[slot, 4:5, :] + vec[slot, 5:6, :])
        before = dot3(ah, al, uh_out[slot], ul_out[slot], NT) + bias[slot : slot + 1, :]
        active, slope = gate(before)
        cut = slice(slot * hidden, (slot + 1) * hidden)
        slope_out[:, cut] = slope
        high, low = split(active)
        hh_out[:, cut] = high
        hl_out[:, cut] = low


def feed_up(flags, base, added, vec, bias, pieces):
    length, width = base.shape
    hidden = bias.shape[1]
    weight = ((2, hidden, width), bf16)
    return call(
        functools.partial(feed_up_kernel, pieces.entries, len(pieces.arrays)),
        length // BM,
        [SMEM, rows(width)] + halves(width) * 2 + [full(vec.shape), full(bias.shape)] + [ANY] * len(pieces.arrays),
        [rows(width)] * 3 + [rows(1)] + [rows(2 * hidden)] * 3 + [full(weight[0])] * 2,
        [
            ((length, width), f32),
            ((length, width), bf16),
            ((length, width), bf16),
            ((length, 1), f32),
            ((length, 2 * hidden), bf16),
            ((length, 2 * hidden), bf16),
            ((length, 2 * hidden), f32),
            weight, weight,
        ],
        [pltpu.VMEM((2, hidden, width), f32), pltpu.SemaphoreType.DMA((len(pieces.entries),))],
        "feed_up",
        6 * length * width * 2 * hidden,
        40e6,
        flags, base, *added, vec, bias, *pieces.arrays,
    )


def feed_down_kernel(entries, count, flags, hh, hl, vec, *refs):
    part_a, part_b, dh_out, dl_out, stage, sems = refs[count:]
    hidden = stage.shape[1]

    @pl.when(pl.program_id(0) == 0)
    def _():
        load_split(entries, flags, refs[:count], stage, sems, dh_out, dl_out)

    partial = 0.5 * (vec[0, 6:7, :] + vec[1, 6:7, :])
    for slot in range(2):
        cut = slice(slot * hidden, (slot + 1) * hidden)
        partial = partial + dot3(hh[:, cut], hl[:, cut], dh_out[slot], dl_out[slot], NN)
    write_halves(part_a, part_b, partial)


def feed_down(flags, hh, hl, vec, pieces):
    length, hidden, width = hh.shape[0], hh.shape[1] // 2, vec.shape[2]
    weight = ((2, hidden, width), bf16)
    return call(
        functools.partial(feed_down_kernel, pieces.entries, len(pieces.arrays)),
        length // BM,
        [SMEM] + [rows(2 * hidden)] * 2 + [full(vec.shape)] + [ANY] * len(pieces.arrays),
        halves(width) + [full(weight[0])] * 2,
        [((length // 2, width), f32)] * 2 + [weight, weight],
        [pltpu.VMEM((2, hidden, width), f32), pltpu.SemaphoreType.DMA((len(pieces.entries),))],
        "feed_down",
        6 * length * width * 2 * hidden,
        25e6,
        flags, hh, hl, vec, *pieces.arrays,
    )


def piece_outs(width, order):
    count = 4 if order == 3 else 2
    shape = (2, 2, width // 2 // count, width)
    return [full(shape)] * count, [(shape, f32)] * count


def feed_back_one_kernel(pulled, order, flags, g_in, *refs):
    if pulled:
        added_refs, (nh, nl, scale) = refs[:4], refs[4:7]
        refs = refs[7:]
    (dh, dl, hh, hl, slope, g_out, uh_out, ul_out, *piece_refs, bias_out, total_out, acc) = refs
    step = pl.program_id(0)
    hidden = dh.shape[1]
    g = g_in[...]
    if pulled:
        n = nh[...].astype(f32) + nl[...].astype(f32)
        g = g + pull_rows(n, scale[...], read_halves(*added_refs[:2]) + read_halves(*added_refs[2:]))
    g_out[...] = g

    @pl.when(step == 0)
    def _():
        acc[...] = jnp.zeros_like(acc)
        bias_out[...] = jnp.zeros_like(bias_out)
        total_out[...] = jnp.zeros_like(total_out)

    total_out[...] += jnp.sum(g, axis=0, keepdims=True)
    gh, gl = split(g)
    for slot in range(2):
        cut = slice(slot * hidden, (slot + 1) * hidden)
        delta = dot3(gh, gl, dh[slot], dl[slot], NT) * slope[:, cut]
        bias_out[slot : slot + 1, :] += jnp.sum(delta, axis=0, keepdims=True)
        high, low = split(delta)
        uh_out[:, cut] = high
        ul_out[:, cut] = low
        acc[slot] += dot3(gh, gl, hh[:, cut], hl[:, cut], TN)

    @pl.when(step == pl.num_programs(0) - 1)
    def _():
        store_pieces(flags, lambda slot, row, count: acc[slot, pl.ds(row, count), :], order, piece_refs)


def feed_back_one(order, flags, g, pulled, dh, dl, hh, hl, slope, riders=()):
    length, width = g.shape
    hidden = dh.shape[1]
    piece_specs, piece_shapes = piece_outs(width, order)
    pulled_specs = halves(width) * 2 + [rows(width)] * 2 + [rows(1)] if pulled else []
    return call(
        functools.partial(feed_back_one_kernel, bool(pulled), order),
        length // BM,
        [SMEM, rows(width)] + pulled_specs + [full(dh.shape)] * 2 + [rows(2 * hidden)] * 3,
        [rows(width)] + [rows(2 * hidden)] * 2 + piece_specs + [full((2, hidden)), full((1, width))],
        [((length, width), f32), ((length, 2 * hidden), bf16), ((length, 2 * hidden), bf16)]
        + piece_shapes
        + [((2, hidden), f32), ((1, width), f32)],
        [pltpu.VMEM((2, width, hidden), f32)],
        "feed_back_one",
        6 * length * width * 4 * hidden,
        40e6,
        flags, g, *pulled, dh, dl, hh, hl, slope,
        riders=riders,
    )


def feed_back_two_kernel(parts, order, flags, uh, ul, nh, nl, vec, *refs):
    if "e" in parts:
        wh, wl, e_a, e_b, vec_out = refs
    else:
        *piece_refs, acc = refs
    step = pl.program_id(0)
    hidden = uh.shape[1] // 2

    @pl.when(step == 0)
    def _():
        if "e" in parts:
            vec_out[...] = jnp.zeros_like(vec_out)
        else:
            acc[...] = jnp.zeros_like(acc)

    n = nh[...].astype(f32) + nl[...].astype(f32)
    e = None
    for slot in range(2):
        cut = slice(slot * hidden, (slot + 1) * hidden)
        gain = vec[slot, 4:5, :]
        if "e" in parts:
            delta = dot3(uh[:, cut], ul[:, cut], wh[slot], wl[slot], NN)
            vec_out[2 * slot : 2 * slot + 1, :] += jnp.sum(delta * n, axis=0, keepdims=True)
            vec_out[2 * slot + 1 : 2 * slot + 2, :] += jnp.sum(delta, axis=0, keepdims=True)
            e = delta * gain if e is None else e + delta * gain
        else:
            ah, al = split(n * gain + vec[slot, 5:6, :])
            acc[slot] += dot3(uh[:, cut], ul[:, cut], ah, al, TN)
    if "e" in parts:
        write_halves(e_a, e_b, e)
    else:

        @pl.when(step == pl.num_programs(0) - 1)
        def _():
            store_pieces(flags, lambda slot, row, count: acc[slot, pl.ds(row, count), :], order, piece_refs)


def feed_back_two(parts, order, flags, uh, ul, nh, nl, vec, wh, wl, riders=()):
    length, width = nh.shape
    hidden = wh.shape[1]
    piece_specs, piece_shapes = piece_outs(width, order)
    if parts == "e":
        weights, out_specs = (wh, wl), halves(width) + [full((4, width))]
        out_shapes = [((length // 2, width), f32)] * 2 + [((4, width), f32)]
    else:
        weights, out_specs, out_shapes = (), piece_specs, piece_shapes
    return call(
        functools.partial(feed_back_two_kernel, parts, order),
        length // BM,
        [SMEM] + [rows(2 * hidden)] * 2 + [rows(width)] * 2 + [full(vec.shape)] + [full(w.shape) for w in weights],
        out_specs,
        out_shapes,
        [pltpu.VMEM((2, hidden, width), f32)] if parts == "w" else [],
        "feed_back_two_" + parts,
        6 * length * width * 2 * hidden,
        25e6,
        flags, uh, ul, nh, nl, vec, *weights,
        riders=riders,
    )


def attn_back_one_kernel(
    g_in, mine_a, mine_b, other_a, other_b, nh, nl, scale, wh, wl, oh, ol, g_out, dh_out, dl_out, do_out, total_out
):
    step = pl.program_id(0)
    inner, width = oh.shape[0], g_in.shape[1]

    @pl.when(step == 0)
    def _():
        do_out[...] = jnp.zeros_like(do_out)
        total_out[...] = jnp.zeros_like(total_out)

    n = nh[...].astype(f32) + nl[...].astype(f32)
    g = g_in[...] + pull_rows(n, scale[...], read_halves(mine_a, mine_b) + read_halves(other_a, other_b))
    g_out[...] = g
    total_out[...] += jnp.sum(g, axis=0, keepdims=True)
    gh, gl = split(g)
    delta = dot3(wh[...].reshape(inner, width), wl[...].reshape(inner, width), gh, gl, NT)
    high, low = split(delta)
    dh_out[...] = high
    dl_out[...] = low
    do_out[...] += dot3(oh[...], ol[...], gh, gl, NN)


def attn_back_one(g, added, nh, nl, scale, wh, wl, oh, ol, riders=()):
    length, width = g.shape
    inner = oh.shape[0]
    out_rows = inner // 2
    tail = pl.BlockSpec((2, out_rows, width), lambda i: (0, width // out_rows - 1, 0))
    return call(
        attn_back_one_kernel,
        length // BM,
        [rows(width)] + halves(width) * 2 + [rows(width)] * 2 + [rows(1)] + [tail, tail] + [lanes(inner)] * 2,
        [rows(width), lanes(inner), lanes(inner), full((inner, width)), full((1, width))],
        [
            ((length, width), f32),
            ((inner, length), bf16),
            ((inner, length), bf16),
            ((inner, width), f32),
            ((1, width), f32),
        ],
        [],
        "attn_back_one",
        6 * length * width * 2 * inner,
        20e6,
        g, *added, nh, nl, scale, wh, wl, oh, ol,
        riders=riders,
    )


def heads_back_kernel(qh, ql, kh, kl, vh, vl, dh, dl, oh, ol, lse, dqh, dql, dkh, dkl, dvh, dvl, acc_k, acc_v):
    keys = jnp.concatenate([kh[...], kh[...], kl[...]], axis=0)
    keys_two = jnp.concatenate([kh[...], kl[...]], axis=0)
    values = jnp.concatenate([vh[...], vh[...], vl[...]], axis=0)
    key_high = kh[...]
    for block in range(qh.shape[1] // BM):
        cut = slice(block * BM, (block + 1) * BM)
        q_high, q_low = qh[:, cut], ql[:, cut]
        d_high, d_low = dh[:, cut], dl[:, cut]
        delta = d_high.astype(f32) + d_low.astype(f32)
        attended = oh[:, cut].astype(f32) + ol[:, cut].astype(f32)
        diagonal = jnp.sum(delta * attended, axis=0, keepdims=True)
        scores = dot(keys, jnp.concatenate([q_high, q_low, q_high], axis=0), TN)
        probs = jnp.exp(scores - lse[0, :, cut])
        p_high, p_low = split(probs)
        delta_probs = dot(values, jnp.concatenate([d_high, d_low, d_high], axis=0), TN)
        delta_scores = probs * (delta_probs - diagonal)
        s_high, s_low = split(delta_scores)
        both = dot(jnp.concatenate([d_high, d_low], axis=0), p_high, NT)
        part_v = both[:HS] + (both[HS:] + dot(d_high, p_low, NT))
        both = dot(jnp.concatenate([q_high, q_low], axis=0), s_high, NT)
        part_k = both[:HS] + (both[HS:] + dot(q_high, s_low, NT))
        if block == 0:
            acc_v[...] = part_v
            acc_k[...] = part_k
        else:
            acc_v[...] += part_v
            acc_k[...] += part_k
        both = dot(keys_two, s_high, NN)
        delta_q = (both[:HS] + (both[HS:] + dot(key_high, s_low, NN))) * (1.0 / math.sqrt(HS))
        high, low = split(delta_q)
        dqh[:, cut] = high
        dql[:, cut] = low
    high, low = split(acc_k[...])
    dkh[...] = high
    dkl[...] = low
    high, low = split(acc_v[...])
    dvh[...] = high
    dvl[...] = low


def attn_heads_back(ph, pl_, dh, dl, oh, ol, lse, riders=()):
    inner2, length = ph.shape
    heads = inner2 // (3 * HS)
    half = heads // 2
    specs = []
    for which in range(3):
        specs += [head_spec(length, which, half)] * 2
    plain = pl.BlockSpec((HS, length), lambda h: (h, 0))
    return call(
        heads_back_kernel,
        heads,
        specs + [plain] * 4 + [pl.BlockSpec((1, 1, length), lambda h: (h, 0, 0))],
        [plain] * 6,
        [((heads * HS, length), bf16)] * 6,
        [pltpu.VMEM((HS, length), f32)] * 2,
        "attn_heads_back",
        heads * length * length * HS * 2 * 26,
        15e6,
        ph, pl_, ph, pl_, ph, pl_, dh, dl, oh, ol, lse,
        riders=riders,
    )


def attn_back_two_kernel(parts, order, flags, *refs):
    dqh, dql, dkh, dkl, dvh, dvl, nh, nl, vec = refs[:9]
    refs = refs[9:]
    if "e" in parts:
        (wh, wl), refs = refs[:2], refs[2:]
    if "w" in parts:
        do, refs = refs[0], refs[1:]
    if "e" in parts:
        (e_a, e_b, vec_out), refs = refs[:3], refs[3:]
    if "w" in parts:
        *piece_refs, pair_out, acc, turned = refs
    step = pl.program_id(0)
    third = dqh.shape[0] // 2
    inner = 3 * third

    @pl.when(step == 0)
    def _():
        if "e" in parts:
            vec_out[...] = jnp.zeros_like(vec_out)
        if "w" in parts:
            acc[...] = jnp.zeros_like(acc)
            pair_out[...] = jnp.zeros_like(pair_out)

    n = nh[...].astype(f32) + nl[...].astype(f32)
    ones = jnp.ones((8, n.shape[0]), bf16)
    e = None
    for slot in range(2):
        cut = slice(slot * third, (slot + 1) * third)
        high = jnp.concatenate([dqh[cut], dkh[cut], dvh[cut]], axis=0)
        low = jnp.concatenate([dql[cut], dkl[cut], dvl[cut]], axis=0)
        gain = vec[slot, 0:1, :]
        if "w" in parts:
            ah, al = split(n * gain + vec[slot, 1:2, :])
            acc[slot] += dot3(high, low, ah, al, NN)
            pair_out[slot] += dot(ones, high, NT) + dot(ones, low, NT)
        if "e" in parts:
            delta = dot3(high, low, wh[slot, :inner], wl[slot, :inner], TN)
            vec_out[2 * slot : 2 * slot + 1, :] += jnp.sum(delta * n, axis=0, keepdims=True)
            vec_out[2 * slot + 1 : 2 * slot + 2, :] += jnp.sum(delta, axis=0, keepdims=True)
            e = delta * gain if e is None else e + delta * gain
    if "e" in parts:
        write_halves(e_a, e_b, e)

    if "w" in parts:

        @pl.when(step == pl.num_programs(0) - 1)
        def _():
            for slot in range(2):
                whole = jnp.concatenate([acc[slot], do[slot * third : (slot + 1) * third]], axis=0)
                turned[slot] = jnp.transpose(whole)
            store_pieces(flags, lambda slot, row, count: turned[slot, pl.ds(row, count), :], order, piece_refs)


def attn_back_two(parts, order, flags, grads, nh, nl, vec, wh, wl, do, riders=()):
    length, width = nh.shape
    heads_rows = grads[0].shape[0]
    inner = 3 * heads_rows // 2
    piece_specs, piece_shapes = piece_outs(width, order)
    in_specs = [SMEM] + [lanes(heads_rows)] * 6 + [rows(width)] * 2 + [full(vec.shape)]
    args = [flags, *grads, nh, nl, vec]
    out_specs, out_shapes, scratch = [], [], []
    if "e" in parts:
        in_specs += [full(wh.shape)] * 2
        args += [wh, wl]
        out_specs += halves(width) + [full((4, width))]
        out_shapes += [((length // 2, width), f32)] * 2 + [((4, width), f32)]
    if "w" in parts:
        in_specs += [full(do.shape)]
        args += [do]
        out_specs += piece_specs + [full((2, 8, inner))]
        out_shapes += piece_shapes + [((2, 8, inner), f32)]
        scratch = [pltpu.VMEM((2, inner, width), f32), pltpu.VMEM((2, width, width), f32)]
    return call(
        functools.partial(attn_back_two_kernel, parts, order),
        length // BM,
        in_specs,
        out_specs,
        out_shapes,
        scratch,
        "attn_back_two_" + parts,
        6 * length * width * 2 * inner * len(parts),
        15e6 * len(parts),
        *args,
        riders=riders,
    )


def by_planes(flags, value, near_out, far_out):
    quarter = value.shape[1] // 4
    parts = [value[:, k * quarter : (k + 1) * quarter] for k in range(4)]
    odd, high = flags[0] % 2 == 1, flags[0] // 2 == 1
    parts = [jnp.where(odd, parts[k ^ 1], parts[k]) for k in range(4)]
    parts = [jnp.where(high, parts[k ^ 2], parts[k]) for k in range(4)]
    near_out[...] = jnp.concatenate([parts[0], parts[2]], axis=1)
    far_out[...] = jnp.concatenate([parts[1], parts[3]], axis=1)


def finish_kernel(flags, g_in, mine_a, mine_b, other_a, other_b, nh, nl, scale, mask, near_out, far_out, sums_out):
    @pl.when(pl.program_id(0) == 0)
    def _():
        sums_out[...] = jnp.zeros_like(sums_out)

    n = nh[...].astype(f32) + nl[...].astype(f32)
    g = g_in[...] + pull_rows(n, scale[...], read_halves(mine_a, mine_b) + read_halves(other_a, other_b))
    absorbed = mask[...]
    by_planes(flags, g * (1.0 - absorbed), near_out, far_out)
    sums_out[...] += jnp.sum(g * absorbed, axis=0, keepdims=True)


def finish(flags, g, added, nh, nl, scale, mask, riders=()):
    length, width = g.shape
    return call(
        finish_kernel,
        length // BM,
        [SMEM, rows(width)] + halves(width) * 2 + [rows(width)] * 2 + [rows(1)] * 2,
        [rows(width // 2)] * 2 + [full((1, width))],
        [((length, width // 2), f32)] * 2 + [((1, width), f32)],
        [],
        "finish",
        10 * length * width,
        15e6,
        flags, g, *added, nh, nl, scale, mask,
        riders=riders,
    )


def leave_kernel(flags, base, mine_a, mine_b, other_a, other_b, near_out, far_out):
    value = base[...] + (read_halves(mine_a, mine_b) + read_halves(other_a, other_b))
    by_planes(flags, value, near_out, far_out)


def leave(flags, base, added):
    length, width = base.shape
    return call(
        leave_kernel,
        length // BM,
        [SMEM, rows(width)] + halves(width) * 2,
        [rows(width // 2)] * 2,
        [((length, width // 2), f32)] * 2,
        [],
        "leave",
        10 * length * width,
        10e6,
        flags, base, *added,
    )


VEC_ROWS = 10


def pack_kernel(columns, flags, *refs):
    table = refs[-1]
    row_sum = refs[-2]
    width = row_sum.shape[1]
    odd, core, sequence = flags[0], flags[1], flags[2]
    table[...] = jnp.zeros_like(table)

    def place(parts):
        zero = jnp.zeros_like(parts[0])
        first = jnp.concatenate([v for p in parts for v in (p, zero)], axis=1)
        second = jnp.concatenate([v for p in parts for v in (zero, p)], axis=1)
        return jnp.where(core == 0, first, second)

    for layer in range(2):
        attn_vec, pair_sum, out_total, ffn_vec, up_sum, down_total = refs[6 * layer : 6 * layer + 6]
        third = pair_sum.shape[2] // 3
        block = up_sum.shape[1] // columns
        for slot in range(2):
            section = 2 * layer + jnp.where(odd == 1, 1 - slot, slot)
            base = section * VEC_ROWS

            def put(row, value):
                table[pl.ds(base + row, 1), :] = value

            put(0, attn_vec[2 * slot : 2 * slot + 1, :])
            put(1, attn_vec[2 * slot + 1 : 2 * slot + 2, :])
            pair = pair_sum[slot, 0:1, :]
            put(2, place([pair[:, :third], pair[:, 2 * third :]]))
            put(3, 0.5 * out_total[...])
            put(4, ffn_vec[2 * slot : 2 * slot + 1, :])
            put(5, ffn_vec[2 * slot + 1 : 2 * slot + 2, :])
            put(6, 0.5 * down_total[...])
            ups = up_sum[slot : slot + 1, :]
            spread = place([ups[:, k * block : (k + 1) * block] for k in range(columns)])
            for k in range(spread.shape[1] // width):
                put(7 + k, spread[:, k * width : (k + 1) * width])
    table[pl.ds(4 * VEC_ROWS + sequence, 1), :] = 0.5 * row_sum[...]


def pack(flags, small, row_sum, columns, sequences):
    width = row_sum.shape[1]
    arrays = [*small[0], *small[1], row_sum]
    count = -(-(4 * VEC_ROWS + sequences) // 8) * 8
    return call(
        functools.partial(pack_kernel, columns),
        1,
        [SMEM] + [full(v.shape) for v in arrays],
        [full((count, width))],
        [((count, width), f32)],
        [],
        "pack",
        1e4,
        1e6,
        flags, *arrays,
    )[0]


def after(value, *others):
    return lax.optimization_barrier((value, *others))[0]


class Plan:
    def __init__(self, planes, dp):
        self.planes, self.dp, self.columns = planes, dp, dp // 2
        self.z = lax.axis_index("section")
        device = lax.axis_index("dp")
        self.column, self.core = device // 2, device % 2

    def permute(self, value, target):
        pairs = []
        for z in range(self.planes):
            for d in range(self.dp):
                to = target(z, d)
                if to is not None:
                    pairs.append((z * self.dp + d, to[0] * self.dp + to[1]))
        return lax.ppermute(value, AXES, pairs)

    def groups(self):
        return [
            [z * self.dp + 2 * j + c for j in range(self.columns)] for z in range(self.planes) for c in range(2)
        ]

    def across(self, value):
        return self.permute(value, lambda z, d: (z, d ^ 1))

    def added(self, first, second):
        return (first, second, self.across(first), self.across(second))

    def along_z(self, value, bit, planes=None):
        return self.permute(value, lambda z, d: (z ^ bit, d) if planes is None or z in planes else None)

    def in_plane(self, value, bit):
        return self.permute(value, lambda z, d: (z, d ^ (2 * bit)))

    def whole(self, shard):
        return lax.all_gather(shard, AXES, axis_index_groups=self.groups(), axis=0, tiled=True)

    def sum_step(self, table, step):
        if self.columns != 4:
            return lax.psum(table, AXES) if step == 0 else table
        if step == 0:
            return table + self.across(table)
        if step < 3:
            return table + self.in_plane(table, step)
        return table + self.along_z(table, step - 2)


class Group:
    def __init__(self, plan, shard, order):
        self.plan, self.shard, self.order = plan, shard, order
        if plan.columns == 4:
            self.got = plan.in_plane(shard, order)

    def step(self):
        if self.plan.columns != 4:
            return self.shard
        self.kept = self.got
        on = jnp.concatenate([self.shard, self.kept])
        self.last = self.plan.in_plane(on, 3 - self.order)
        return on

    def pieces(self, first, count, slot, offset, when):
        if self.plan.columns != 4:
            whole = self.plan.whole(self.shard[first : first + count])
            return [(whole, 0, whole.shape[0], slot, None, 0, when)]
        rows_all = self.shard.shape[0]
        near, far = (1, 2) if self.order == 1 else (2, 1)
        return [
            (self.shard, first, count, slot, 0, offset, when),
            (self.kept, first, count, slot, near, offset, when),
            (self.last, first, count, slot, far, offset, when),
            (self.last, rows_all + first, count, slot, 3, offset, when),
        ]


def arrive(groups, *others):
    names = [(g, "got" if not hasattr(g, "last") else "last") for g in groups if g.plan.columns == 4]
    values = lax.optimization_barrier((*(getattr(g, name) for g, name in names), *others))
    for (group, name), value in zip(names, values):
        setattr(group, name, value)
    return values[len(names) :]


class Sum:
    def __init__(self, plan, order, pieces):
        self.plan, self.stage = plan, 0
        self.ways = [1, 2] if order == 3 else [order]
        self.count = pieces[0].shape[2]
        width = pieces[0].shape[3]
        if plan.columns == 4:
            send, keep = ([v.reshape(-1, width) for v in pieces[k::2]] for k in (0, 1))
            self.mine = keep
            self.got = [plan.in_plane(v, way) for v, way in zip(send, self.ways)]
        else:
            parts = []
            for k in range(4):
                for send, keep, way in zip(pieces[0::2], pieces[1::2], self.ways):
                    kinds = ((0, 2), (1, 3)) if way == 1 else ((0, 1), (2, 3))
                    parts.append(keep[kinds[0].index(k)] if k in kinds[0] else send[kinds[1].index(k)])
            whole = jnp.concatenate(parts, axis=1)
            whole = lax.psum_scatter(whole, AXES, axis_index_groups=plan.groups(), scatter_dimension=1, tiled=True)
            self.whole = [whole]

    def merge(self, other):
        if self.plan.columns == 4:
            self.mine, self.got = self.mine + other.mine, self.got + other.got
        else:
            self.whole = self.whole + other.whole
        return self

    def riders(self):
        if self.plan.columns != 4 or self.stage == 3:
            return []
        count = self.count
        pairs = list(zip(self.mine, self.got))
        if self.stage == 0:
            return [Rider(2 * count, (m, first, v, first)) for first in (0, 2 * count) for m, v in pairs]
        if self.stage == 1:
            return [Rider(count, *((m, first, v, first) for m, v in pairs)) for first in (0, count)]
        return [Rider(self.mine[0].shape[0], *((m, 0, v, 0) for m, v in pairs))]

    def take(self, values):
        if not values:
            return self.advance()
        plan = self.plan
        self.stage += 1
        if self.stage == 1:
            half = len(values) // 2
            self.mine = values[:half]
            self.got = [plan.in_plane(v, 3 - way) for v, way in zip(values[half:], self.ways)]
        elif self.stage == 2:
            self.mine = values[:1]
            self.got = [plan.along_z(values[1], 1)]
        else:
            self.mine = values
        return values

    def advance(self):
        if self.stage == 3:
            return []
        if self.plan.columns == 4:
            values = []
            for rider in self.riders():
                parts = [
                    a[i : i + rider.count] + b[j : j + rider.count] for a, i, b, j in rider.segments
                ]
                values.append(parts[0] if len(parts) == 1 else jnp.concatenate(parts))
            return self.take(values)
        if self.stage == 0:
            self.stage = 1
            return []
        if self.stage == 1:
            return self.take([jnp.concatenate([w[slot] for w in self.whole]) for slot in range(2)])
        return self.take([self.mine[0] + self.got[0]])

    def wait(self, *others):
        if self.plan.columns != 4 and self.stage < 2:
            return others
        self.got, others = lax.optimization_barrier((self.got, others))
        return others

    def after(self, *others):
        if self.plan.columns == 4 and self.stage < 3:
            self.got = [after(v, *others) for v in self.got]
        return self

    def finish(self):
        while self.stage < 3:
            self.advance()
        return self.mine[0]


def body(
    tokens, absorbed, timesteps, mask_embedding, time_table,
    attn_gain, attn_shift, joint_weight, pair_bias, out_weight, out_bias,
    ffn_gain, ffn_shift, up_weight, up_bias, down_weight, down_bias, cotangent,
):
    plan = Plan(lax.axis_size("section"), lax.axis_size("dp"))
    z, column, core = plan.z, plan.column, plan.core
    columns = plan.columns
    width = tokens.shape[1]
    inner = out_weight.shape[1]
    hidden = up_weight.shape[2]
    inner_half, hidden_half = inner // 2, hidden // 2
    block = hidden_half // columns
    low_planes = z < 2

    joint_half = lax.dynamic_index_in_dim(joint_weight[0].reshape(width, 3, 2, inner_half), core, 2, keepdims=False)
    joint_half = joint_half.reshape(width, 3 * inner_half).T
    out_half = lax.dynamic_slice_in_dim(out_weight[0], core * inner_half, inner_half, 0)
    own_attn = jnp.concatenate([joint_half, out_half], axis=0)
    up_half = lax.dynamic_index_in_dim(up_weight[0].reshape(width, columns, 2, block), core, 2, keepdims=False)
    own_up = up_half.reshape(width, hidden_half).T
    down_half = lax.dynamic_index_in_dim(down_weight[0].reshape(columns, 2, block, width), core, 1, keepdims=False)
    own_down = down_half.reshape(hidden_half, width)
    own = (own_attn, own_up, own_down)

    own_vec = jnp.stack(
        [attn_gain[0], attn_shift[0], pair_bias[0], out_bias[0], ffn_gain[0], ffn_shift[0], down_bias[0]]
        + [up_bias[0, k * width : (k + 1) * width] for k in range(hidden // width)]
    )
    vec_count = own_vec.shape[0]
    count = width // columns

    def shard_of(matrix):
        return lax.dynamic_slice_in_dim(matrix, column * count, count, 0)

    local = core == z // 2
    which = z % 2
    sequence = 4 * column + z

    def fetch(array):
        piece = lax.dynamic_slice_in_dim(array, which * LEN, LEN, 0)
        return piece, plan.permute(piece, lambda zz, d: (zz, d ^ 1) if d % 2 == zz // 2 else None)

    tail = jnp.zeros((-vec_count % 8, width), f32)
    shard = jnp.concatenate([shard_of(own[0]), own_vec, tail])
    far_attn, near_attn = plan.along_z(shard, 2), plan.along_z(shard, 1)
    far_attn, near_attn, up_shard, down_shard = lax.optimization_barrier(
        (far_attn, near_attn, shard_of(own[1]), shard_of(own[2]))
    )
    opp_attn = plan.along_z(far_attn, 1)
    far_up = plan.along_z(up_shard, 2)
    mask_parts, token_parts = fetch(after(absorbed, far_attn)), fetch(after(tokens, far_attn))

    near_vec = jnp.stack([own_vec, near_attn[count : count + vec_count]])
    far_vec = jnp.stack([far_attn[count : count + vec_count], opp_attn[count : count + vec_count]])
    vectors = jnp.stack([jnp.where(low_planes, near_vec, far_vec), jnp.where(low_planes, far_vec, near_vec)])

    def opposite(near, far):
        return jnp.where(low_planes, near, far), jnp.where(low_planes, far, near)

    attn_opp = opposite(near_attn[:count], opp_attn[:count])
    attn_groups = [Group(plan, far_attn[:count], 1), Group(plan, attn_opp[0], 2)]
    near_up = plan.along_z(after(up_shard, attn_opp[0]), 1)
    far_up, near_up, mask_parts, token_parts = arrive(attn_groups, far_up, near_up, mask_parts, token_parts)
    sent = [group.step() for group in attn_groups]
    mask_parts, token_parts = lax.optimization_barrier((mask_parts, token_parts, *sent))[:2]
    mask_row = jnp.where(local, *mask_parts).astype(f32)
    step = lax.dynamic_index_in_dim(timesteps, sequence, 0, keepdims=False)
    step_row = lax.dynamic_slice_in_dim(time_table, step, 1, 0)
    mask = mask_row[:, None]
    x = jnp.where(mask > 0.5, mask_embedding[None, :] + step_row, jnp.where(local, *token_parts))
    weight = LEN / jnp.maximum(jnp.sum(mask_row), 1.0)
    far_down = plan.along_z(after(down_shard, far_up), 2)
    opp_up = plan.along_z(far_up, 1)
    opp_up, x = arrive(attn_groups, opp_up, x)
    near_down = plan.along_z(after(down_shard, opp_up), 1)
    up_opp = opposite(near_up, opp_up)
    pair_all = lax.dynamic_index_in_dim(vectors[:, :, 2].reshape(2, 2, 2, 2, inner_half), core, 3, keepdims=False)
    pair_rows = jnp.stack([pair_all[:, :, 0], jnp.zeros_like(pair_all[:, :, 0]), pair_all[:, :, 1]], axis=2)
    pair_cols = pair_rows.reshape(2, 2 * 3 * inner_half, 1)
    up_rows = lax.dynamic_index_in_dim(
        vectors[:, :, 7:].reshape(2, 2, columns, 2, block), core, 3, keepdims=False
    ).reshape(2, 2, hidden_half)

    natural = jnp.arange(4, dtype=jnp.int32)
    order = column ^ natural if columns == 4 else natural
    flags = [
        jnp.concatenate([(low_planes == (layer == 0)).astype(jnp.int32)[None], order.astype(jnp.int32)])
        for layer in range(2)
    ]

    def own_rows(matrix):
        return [(matrix, 0, matrix.shape[0], 0, None, 0, "near")]

    def pieces_of(matrix, par, opp):
        return Pieces(own_rows(matrix) + par.pieces(0, count, 0, 0, "far") + opp)

    kept = []

    def keep(layer, *values):
        kept.append((vectors[layer], *values))

    half = count // 2
    up_groups = [Group(plan, far_up, 1), Group(plan, up_opp[0], 2)]
    x, xh, xl, x_scale, ph, pl_, wh, wl = attn_in(
        flags[0], x, (), vectors[0], pair_cols[0], pieces_of(own[0], attn_groups[0], attn_groups[1].pieces(0, count, 1, 0, "all"))
    )
    ph, far_down, near_down, cotangent = arrive(up_groups, ph, far_down, near_down, cotangent)
    cot_parts = fetch(cotangent)
    opp_down = plan.along_z(far_down, 1)
    for group in up_groups:
        group.step()
    oh, ol, lse, *part = attn_heads(ph, pl_, wh, wl, vectors[0])
    opp_down, *part = arrive(up_groups, opp_down, *part)
    down_opp = opposite(near_down, opp_down)
    down_groups = [Group(plan, far_down, 1), Group(plan, down_opp[0], 2)]
    added = plan.added(*part)
    added = added[:2] + arrive(down_groups, *added[2:])
    for group in down_groups:
        group.step()
    if columns == 4:
        last_attn = [Group(plan, attn_opp[1][:half], 1), Group(plan, attn_opp[1][half:], 2)]
    else:
        last_attn = [Group(plan, attn_opp[1], 1)]
    y, yh, yl, y_scale, hh, hl, slope, uh, ul = feed_up(
        flags[0], x, added, vectors[0], up_rows[0], pieces_of(own[1], up_groups[0], up_groups[1].pieces(0, count, 1, 0, "all"))
    )
    hh, cot_other = arrive(last_attn, hh, cot_parts[1])
    for group in last_attn:
        group.step()
    *feed_part, dh, dl = feed_down(
        flags[0], hh, hl, vectors[0], pieces_of(own[2], down_groups[0], down_groups[1].pieces(0, count, 1, 0, "all"))
    )
    keep(0, xh, xl, x_scale, ph, pl_, wh, wl, oh, ol, lse, yh, yl, y_scale, hh, hl, slope, uh, ul, dh, dl)

    g = jnp.where(local, cot_parts[0], after(cot_other, dh)) * (mask * weight)
    last_groups = [Group(plan, up_opp[1], 1), Group(plan, down_opp[1], 2)]
    feed_part = arrive([*last_attn, *last_groups], *feed_part)
    for group in last_groups:
        group.step()
    added = plan.added(*feed_part)
    if columns == 4:
        attn_last = last_attn[0].pieces(0, half, 1, 0, "all") + last_attn[1].pieces(0, half, 1, half, "all")
    else:
        attn_last = last_attn[0].pieces(0, count, 1, 0, "all")
    x, xh, xl, x_scale, ph, pl_, wh, wl = attn_in(
        flags[1], y, added, vectors[1], pair_cols[1], pieces_of(own[0], attn_groups[0], attn_last)
    )
    oh, ol, lse, *part = attn_heads(ph, pl_, wh, wl, vectors[1])
    added = plan.added(*arrive(last_groups, *part))
    y, yh, yl, y_scale, hh, hl, slope, uh, ul = feed_up(
        flags[1], x, added, vectors[1], up_rows[1], pieces_of(own[1], up_groups[0], last_groups[0].pieces(0, count, 1, 0, "all"))
    )
    *feed_part, dh, dl = feed_down(
        flags[1], hh, hl, vectors[1], pieces_of(own[2], down_groups[0], last_groups[1].pieces(0, count, 1, 0, "all"))
    )
    keep(1, xh, xl, x_scale, ph, pl_, wh, wl, oh, ol, lse, yh, yl, y_scale, hh, hl, slope, uh, ul, dh, dl)
    x, added = y, plan.added(*feed_part)
    last = (x, *added)

    quarter = width // plan.planes
    plane_flags = jnp.stack([z, core]).astype(jnp.int32)

    def beside(value):
        return plan.permute(value, lambda zz, d: (zz ^ 1, d) if d % 2 == zz // 2 else None)

    def beyond(mine, theirs):
        both = jnp.concatenate([mine[:, quarter:], theirs[:, quarter:]], axis=1)
        return plan.permute(both, lambda zz, d: (zz ^ 2, d) if d % 2 == zz // 2 else None)

    def settle_rows(mine, theirs, arrived):
        first = jnp.where(local, mine[:, :quarter], arrived[:, :quarter])
        second = jnp.where(local, theirs[:, :quarter], arrived[:, quarter:])
        odd = z % 2 == 1
        return jnp.concatenate([jnp.where(odd, second, first), jnp.where(odd, first, second)])

    def ride(kernel, riding, *args):
        lists = [total.riders() for total in riding]
        values = list(kernel(*args, riders=[r for some in lists for r in some]))
        taken = sum(len(some) for some in lists)
        results, extra = values[: len(values) - taken], values[len(values) - taken :]
        for total, some in zip(riding, lists):
            total.take(extra[: len(some)])
            extra = extra[len(some) :]
        return results

    small = [None] * 2
    (vec, xh, xl, x_scale, ph, pl_, wh, wl, oh, ol, lse, yh, yl, y_scale, hh, hl, slope, uh, ul, dh, dl) = kept[1]
    g, duh, dul, *pieces, up_bias_sum, down_bias_sum = feed_back_one(1, flags[1], g, (), dh, dl, hh, hl, slope)
    down_1 = Sum(plan, 1, pieces)
    out_near, out_far = leave(plane_flags, after(last[0], up_bias_sum), last[1:])
    out_beside = beside(out_far)
    *e, ffn_vec = feed_back_two("e", 0, flags[1], after(duh, out_near), dul, yh, yl, vec, uh, ul)
    e = plan.added(*e)
    pieces = feed_back_two("w", 2, flags[1], after(duh, ffn_vec), dul, yh, yl, vec, uh, ul)
    up_1 = Sum(plan, 2, pieces)
    g, out_beside, *others = lax.optimization_barrier((g, out_beside, *e[2:], pieces[0]))[:4]
    g, doh, dol, do, out_bias_sum = attn_back_one(g, (*e[:2], *others), yh, yl, y_scale, wh, wl, oh, ol)
    grads = attn_heads_back(ph, pl_, doh, dol, oh, ol, lse)
    *e, attn_vec = ride(attn_back_two, [down_1], "e", 0, flags[1], grads, xh, xl, vec, wh, wl, do)
    e = plan.added(*e)
    out_beyond = beyond(out_near, after(out_beside, attn_vec))
    *pieces, pair_sum = ride(attn_back_two, [up_1], "w", 2, flags[1], grads, xh, xl, vec, wh, wl, after(do, attn_vec))
    attn_1 = Sum(plan, 2, pieces)
    g, *others = lax.optimization_barrier((g, *e[2:], pair_sum))[:3]
    pulled = (*e[:2], *others, xh, xl, x_scale)
    small[1] = (attn_vec, pair_sum, out_bias_sum, ffn_vec, up_bias_sum, down_bias_sum)

    (vec, xh, xl, x_scale, ph, pl_, wh, wl, oh, ol, lse, yh, yl, y_scale, hh, hl, slope, uh, ul, dh, dl) = kept[0]
    g, duh, dul, *pieces, up_bias_sum, down_bias_sum = feed_back_one(1, flags[0], g, pulled, dh, dl, hh, hl, slope)
    down_0 = Sum(plan, 1, pieces)
    feed_1 = down_1.merge(up_1)
    duh, out_beyond = lax.optimization_barrier((duh, out_beyond))
    *e, ffn_vec = ride(feed_back_two, [feed_1], "e", 0, flags[0], duh, dul, yh, yl, vec, uh, ul)
    e = plan.added(*e)
    pieces = feed_back_two("w", 3, flags[0], after(duh, ffn_vec), dul, yh, yl, vec, uh, ul)
    up_0 = Sum(plan, 3, pieces)
    g, *others = lax.optimization_barrier((g, *e[2:], pieces[0]))[:3]
    g, doh, dol, do, out_bias_sum = ride(
        attn_back_one, [attn_1], g, (*e[:2], *others), yh, yl, y_scale, wh, wl, oh, ol
    )
    doh = after(doh, *down_0.after(out_bias_sum).advance())
    grads = ride(attn_heads_back, [feed_1], ph, pl_, doh, dol, oh, ol, lse)
    mixed = attn_1.merge(down_0)
    grads[0] = after(grads[0], *mixed.after(grads[0]).advance())
    *pieces, pair_sum = ride(attn_back_two, [up_0], "w", 3, flags[0], grads, xh, xl, vec, wh, wl, do)
    attn_0 = Sum(plan, 3, pieces)
    *e, attn_vec = attn_back_two("e", 0, flags[0], [after(grads[0], pair_sum), *grads[1:]], xh, xl, vec, wh, wl, do)
    e = plan.added(*mixed.wait(*up_0.wait(*e)))
    small[0] = (attn_vec, pair_sum, out_bias_sum, ffn_vec, up_bias_sum, down_bias_sum)

    def cross(low, high):
        on = jnp.where(low_planes, high, low)
        return jnp.where(low_planes, low, high), on, plan.along_z(on, 2)

    feed_1, mixed = feed_1.finish(), mixed.finish()
    down_mine, down_on, down_got = cross(mixed[count:], feed_1[:count])
    g = after(g, down_on, *up_0.advance())
    grad_near, grad_far, row_sum = finish(plane_flags, g, e, xh, xl, x_scale, mask)
    out_rows = settle_rows(out_near, out_beside, out_beyond)
    grad_beside = beside(after(grad_far, down_got))

    up_mine, up_on, up_got = cross(up_0.after(grad_far).finish(), feed_1[count:])
    pack_flags = jnp.stack([z % 2, core, sequence]).astype(jnp.int32)
    table = pack(pack_flags, small, row_sum, columns, timesteps.shape[0])
    table = plan.sum_step(table, 0)
    (table,) = attn_0.after(up_on).wait(table)
    attn_0.advance()
    table = plan.sum_step(table, 3)
    grad_beside, table = attn_0.wait(grad_beside, table)
    on = attn_0.advance()
    (grad_beside,) = arrive([], grad_beside, *on)[:1]
    grad_beyond = beyond(grad_near, grad_beside)
    table = plan.sum_step(table, 4)
    up_got, table = attn_0.wait(up_got, table)
    attn_mine, attn_on, attn_got = cross(attn_0.finish(), mixed[:count])
    for step in (1, 2):
        table = plan.sum_step(table, step)
    down_mine, up_mine = down_mine + down_got, up_mine + up_got

    def exchange(rows_all):
        halves = rows_all.reshape(2, -1, width)
        mine = lax.dynamic_index_in_dim(halves, core, 0, keepdims=False)
        theirs = plan.across(lax.dynamic_index_in_dim(halves, 1 - core, 0, keepdims=False))
        first = core == 0
        return jnp.where(first, mine, theirs), jnp.where(first, theirs, mine)

    zero, one = exchange(down_mine)
    down_grad = jnp.stack([v.reshape(-1, columns, block) for v in (zero, one)], axis=2).reshape(-1, hidden).T
    up_grad = up_mine.reshape(-1, width).T
    attn_got, table = lax.optimization_barrier((attn_got, table, down_grad, up_grad))[:2]
    zero, one = exchange(attn_mine + attn_got)
    grad_rows = settle_rows(grad_near, grad_beside, grad_beyond)
    joint = jnp.stack([v[:, : 3 * inner_half].reshape(-1, 3, inner_half) for v in (zero, one)], axis=2)
    joint_grad = joint.reshape(-1, 3 * inner)
    out_grad = jnp.concatenate([zero[:, 3 * inner_half :], one[:, 3 * inner_half :]], axis=1).T

    mine = lax.dynamic_slice_in_dim(table, VEC_ROWS * z, VEC_ROWS, 0)
    device = 2 * column + core
    share = lax.dynamic_slice_in_dim(mine, device * (width // plan.dp), width // plan.dp, 1)
    up_count = hidden // width
    up_share = lax.dynamic_slice_in_dim(
        mine[7 : 7 + up_count].reshape(-1), device * (hidden // plan.dp), hidden // plan.dp, 0
    )

    seq_rows = table[4 * VEC_ROWS : 4 * VEC_ROWS + timesteps.shape[0]]
    seq_cols = lax.dynamic_slice_in_dim(seq_rows, z * quarter, quarter, 1)
    picks = (timesteps[:, None] == jnp.arange(time_table.shape[0], dtype=jnp.int32)[None, :]).astype(f32)
    table_grad = jnp.einsum("st,sd->td", picks, seq_cols, precision=lax.Precision.HIGHEST)
    mask_grad = jnp.sum(seq_cols, axis=0)

    return (
        out_rows,
        grad_rows,
        mask_grad,
        table_grad,
        share[0:1],
        share[1:2],
        joint_grad[None],
        share[2:3],
        out_grad[None],
        share[3:4],
        share[4:5],
        share[5:6],
        up_grad[None],
        up_share[None],
        down_grad[None],
        share[6:7],
    )


def solution(mesh):
    placed = (
        P("dp", None), P("dp"), P(), P(), P(),
        P("section", None), P("section", None), P("section", None, None), P("section", None),
        P("section", None, None), P("section", None), P("section", None), P("section", None),
        P("section", None, None), P("section", None), P("section", None, None), P("section", None),
        P("dp", None),
    )
    vector = P("section", "dp")
    return jax.shard_map(
        body,
        mesh=mesh,
        in_specs=placed,
        out_specs=(
            P("dp", "section"), P("dp", "section"), P("section"), P(None, "section"),
            vector, vector, P("section", "dp", None), vector, P("section", None, "dp"), vector,
            vector, vector, P("section", None, "dp"), vector, P("section", None, "dp"), vector,
        ),
        check_vma=False,
    )
```

```python
import functools
import math

import jax
import jax.numpy as jnp
from jax import lax
from jax.experimental import pallas as pl
from jax.experimental.pallas import tpu as pltpu
from jax.sharding import PartitionSpec as P

HS = 64
LEN = 1024
EPS = 1e-05
AXES = ("section", "dp")
f32 = jnp.float32
bf16 = jnp.bfloat16

NN = ((1,), (0,))
NT = ((1,), (1,))
TN = ((0,), (0,))
BM = 256
VMEM_LIMIT = 60 * 1024 * 1024


def dot(a, b, dims):
    return lax.dot_general(a, b, (dims, ((), ())), preferred_element_type=f32)


def split(value):
    high = value.astype(bf16)
    return high, (value - high.astype(f32)).astype(bf16)


def dot3(ah, al, bh, bl, dims):
    return dot(ah, bh, dims) + (dot(ah, bl, dims) + dot(al, bh, dims))


def unit_rows(x):
    center = x - jnp.mean(x, axis=-1, keepdims=True)
    scale = lax.rsqrt(jnp.mean(center * center, axis=-1, keepdims=True) + EPS)
    return center * scale, scale


def pull_rows(n, scale, e):
    return (e - jnp.mean(e, axis=-1, keepdims=True) - n * jnp.mean(e * n, axis=-1, keepdims=True)) * scale


class Pieces:
    def __init__(self, entries):
        self.arrays, self.entries = [], []
        for array, *rest in entries:
            index = next((i for i, known in enumerate(self.arrays) if known is array), len(self.arrays))
            if index == len(self.arrays):
                self.arrays.append(array)
            self.entries.append((index, *rest))


def load_split(entries, flags, refs, stage, sems, high_out, low_out):
    quarter = stage.shape[1] // 4
    near = flags[0] == 1
    copies = {"near": [], "far": [], "all": []}
    for number, (index, first, count, slot, place, offset, when) in enumerate(entries):
        row = offset if place is None else pl.multiple_of(flags[1 + place] * quarter + offset, 8)
        copies[when].append(
            pltpu.make_async_copy(
                refs[index].at[pl.ds(first, count)], stage.at[slot, pl.ds(row, count)], sems.at[number]
            )
        )
    for act in ("start", "wait"):

        @pl.when(near)
        def _():
            for copy in copies["near"]:
                getattr(copy, act)()

        @pl.when(jnp.logical_not(near))
        def _():
            for copy in copies["far"]:
                getattr(copy, act)()

        for copy in copies["all"]:
            getattr(copy, act)()
    for slot in range(2):
        high, low = split(stage[slot])
        high_out[slot] = high
        low_out[slot] = low


def store_pieces(flags, read, order, refs):
    split_rows = order == 3
    for number, ref in enumerate(refs):
        send = number % 2 == 0
        along = 1 + number // 2 if split_rows else order
        kinds = ((1, 3) if send else (0, 2)) if along == 1 else ((2, 3) if send else (0, 1))
        count = ref.shape[2]
        for slot in range(2):
            for place, k in enumerate(kinds):
                step = 2 * count if split_rows else count
                row = pl.multiple_of(flags[1 + k] * step + (number // 2) * count, 8)
                ref[place, slot] = read(slot, row, count)


def full(shape):
    zeros = (0,) * len(shape)
    return pl.BlockSpec(shape, lambda i: zeros)


def rows(width, bm=BM):
    return pl.BlockSpec((bm, width), lambda i: (i, 0))


def lanes(height, bm=BM):
    return pl.BlockSpec((height, bm), lambda i: (0, i))


def halves(width, bm=BM):
    first = LEN // bm // 2
    return [
        pl.BlockSpec((bm, width), lambda i: (jnp.minimum(i, first - 1), 0)),
        pl.BlockSpec((bm, width), lambda i: (jnp.maximum(i - first, 0), 0)),
    ]


def read_halves(first, second):
    early = pl.program_id(0) < pl.num_programs(0) // 2
    return jnp.where(early, first[...], second[...])


def write_halves(first, second, value):
    early = pl.program_id(0) < pl.num_programs(0) // 2

    @pl.when(early)
    def _():
        first[...] = value

    @pl.when(jnp.logical_not(early))
    def _():
        second[...] = value


ANY = pl.BlockSpec(memory_space=pl.ANY)
SMEM = pl.BlockSpec(memory_space=pltpu.SMEM)


class Rider:
    def __init__(self, count, *segments):
        self.count, self.segments = count, segments

    def arrays(self):
        return [v for a, _, b, _ in self.segments for v in (a, b)]

    def specs(self, grid):
        each = grid // len(self.segments)
        block, width = self.count // each, self.segments[0][0].shape[1]
        result = []
        for number, (_, first_a, _, first_b) in enumerate(self.segments):
            for first in (first_a, first_b):
                def place(i, start=number * each, base=first // block):
                    return (base + jnp.clip(i - start, 0, each - 1), 0)

                result.append(pl.BlockSpec((block, width), place))
        return result

    def out(self, grid):
        width = self.segments[0][0].shape[1]
        total = self.count * len(self.segments)
        return pl.BlockSpec((total // grid, width), lambda i: (i, 0)), ((total, width), f32)

    def run(self, grid, refs, out):
        each = grid // len(self.segments)
        value = refs[0][...] + refs[1][...]
        for number in range(1, len(self.segments)):
            other = refs[2 * number][...] + refs[2 * number + 1][...]
            value = jnp.where(pl.program_id(0) >= number * each, other, value)
        out[...] = value


def call(kernel, grid, in_specs, out_specs, out_shapes, scratch, name, flops, nbytes, *args, riders=()):
    ins, outs = len(in_specs), len(out_specs)
    extra = [v for rider in riders for v in rider.arrays()]
    in_specs = list(in_specs) + [v for rider in riders for v in rider.specs(grid)]
    rider_outs = [rider.out(grid) for rider in riders]

    def whole(*refs):
        mine, refs = refs[:ins], refs[ins:]
        sources, refs = refs[: len(extra)], refs[len(extra) :]
        results, refs = refs[:outs], refs[outs:]
        sums, refs = refs[: len(riders)], refs[len(riders) :]
        kernel(*mine, *results, *refs)
        for rider, out in zip(riders, sums):
            own, sources = sources[: len(rider.arrays())], sources[len(rider.arrays()) :]
            rider.run(grid, own, out)

    return pl.pallas_call(
        whole,
        grid=(grid,),
        in_specs=in_specs,
        out_specs=list(out_specs) + [spec for spec, _ in rider_outs],
        out_shape=[jax.ShapeDtypeStruct(s, t) for s, t in list(out_shapes) + [shape for _, shape in rider_outs]],
        scratch_shapes=scratch,
        name=name,
        cost_estimate=pl.CostEstimate(flops=1, bytes_accessed=1, transcendentals=0),
        compiler_params=pltpu.CompilerParams(
            vmem_limit_bytes=VMEM_LIMIT, dimension_semantics=("arbitrary",)
        ),
    )(*args, *extra)


def attn_in_kernel(added, entries, count, flags, *refs):
    base = refs[0]
    refs = refs[1:]
    if added:
        added_refs, refs = refs[:4], refs[4:]
    vec, bias = refs[:2]
    sources, refs = refs[2 : 2 + count], refs[2 + count :]
    if added:
        x_out = refs[0]
        refs = refs[1:]
    nh_out, nl_out, scale_out, ph_out, pl_out, wh_out, wl_out, stage, sems = refs
    inner = 3 * (ph_out.shape[0] // 6)

    @pl.when(pl.program_id(0) == 0)
    def _():
        load_split(entries, flags, sources, stage, sems, wh_out, wl_out)

    x = base[...]
    if added:
        x = x + (read_halves(*added_refs[:2]) + read_halves(*added_refs[2:]))
        x_out[...] = x
    n, scale = unit_rows(x)
    high, low = split(n)
    nh_out[...] = high
    nl_out[...] = low
    scale_out[...] = scale
    third = inner // 3
    for slot in range(2):
        ah, al = split(n * vec[slot, 0:1, :] + vec[slot, 1:2, :])
        projected = dot3(wh_out[slot, :inner], wl_out[slot, :inner], ah, al, NT)
        projected = projected + bias[slot * inner : (slot + 1) * inner]
        queries = projected[:third] * (1.0 / math.sqrt(HS))
        for first, value in ((0, queries), (third, projected[third:])):
            high, low = split(value)
            start = slot * inner + first
            ph_out[start : start + value.shape[0]] = high
            pl_out[start : start + value.shape[0]] = low


def attn_in(flags, x, added, vec, bias, pieces):
    length, width = x.shape
    inner = bias.shape[0] // 2
    outs = [((length, width), f32)] if added else []
    out_specs = [rows(width)] if added else []
    outs += [
        ((length, width), bf16),
        ((length, width), bf16),
        ((length, 1), f32),
        ((2 * inner, length), bf16),
        ((2 * inner, length), bf16),
        ((2, width, width), bf16),
        ((2, width, width), bf16),
    ]
    out_specs += [rows(width), rows(width), rows(1), lanes(2 * inner), lanes(2 * inner)]
    out_specs += [full((2, width, width))] * 2
    in_specs = [SMEM, rows(width)] + halves(width) * (len(added) // 2) + [full(vec.shape), full(bias.shape)]
    in_specs += [ANY] * len(pieces.arrays)
    result = call(
        functools.partial(attn_in_kernel, bool(added), pieces.entries, len(pieces.arrays)),
        length // BM,
        in_specs,
        out_specs,
        outs,
        [pltpu.VMEM((2, width, width), f32), pltpu.SemaphoreType.DMA((len(pieces.entries),))],
        "attn_in",
        6 * length * width * 2 * inner,
        20e6,
        flags, x, *added, vec, bias, *pieces.arrays,
    )
    if not added:
        result = [x] + list(result)
    return result


def heads_kernel(qh, ql, kh, kl, vh, vl, wh, wl, vec, oh_out, ol_out, lse_out, part_a, part_b, oh_all, ol_all):
    head = pl.program_id(0)
    keys = jnp.concatenate([kh[...], kh[...], kl[...]], axis=0)
    values = jnp.concatenate([vh[...], vl[...]], axis=0)
    value_high = vh[...]
    for block in range(qh.shape[1] // BM):
        cut = slice(block * BM, (block + 1) * BM)
        queries = jnp.concatenate([qh[:, cut], ql[:, cut], qh[:, cut]], axis=0)
        scores = dot(keys, queries, TN)
        top = jnp.max(scores, axis=0, keepdims=True)
        weights = jnp.exp(scores - top)
        total = jnp.sum(weights, axis=0, keepdims=True)
        high, low = split(weights)
        both = dot(values, high, NN)
        attended = (both[:HS] + (both[HS:] + dot(value_high, low, NN))) / total
        high, low = split(attended)
        oh_out[:, cut] = high
        ol_out[:, cut] = low
        lse_out[0, :, cut] = top + jnp.log(total)
    place = pl.ds(pl.multiple_of(head * HS, HS), HS)
    oh_all[place, :] = oh_out[...]
    ol_all[place, :] = ol_out[...]

    @pl.when(head == pl.num_programs(0) - 1)
    def _():
        inner, width = oh_all.shape[0], wh.shape[2]
        offset = 0.5 * (vec[0, 3:4, :] + vec[1, 3:4, :])
        for part, cut in ((part_a, slice(0, LEN // 2)), (part_b, slice(LEN // 2, LEN))):
            part[...] = offset + dot3(
                oh_all[:, cut], ol_all[:, cut], wh[...].reshape(inner, width), wl[...].reshape(inner, width), TN
            )


def head_spec(length, which, half_heads):
    return pl.BlockSpec(
        (HS, length), lambda h: (3 * half_heads * (h // half_heads) + which * half_heads + h % half_heads, 0)
    )


def attn_heads(ph, pl_, wh, wl, vec):
    inner2, length = ph.shape
    width = wh.shape[2]
    heads = inner2 // (3 * HS)
    half = heads // 2
    out_rows = half * HS
    specs = []
    for which in range(3):
        specs += [head_spec(length, which, half)] * 2
    tail = pl.BlockSpec((2, out_rows, width), lambda h: (0, width // out_rows - 1, 0))
    return call(
        heads_kernel,
        heads,
        specs + [tail, tail, full(vec.shape)],
        [
            pl.BlockSpec((HS, length), lambda h: (h, 0)),
            pl.BlockSpec((HS, length), lambda h: (h, 0)),
            pl.BlockSpec((1, 1, length), lambda h: (h, 0, 0)),
            full((length // 2, width)),
            full((length // 2, width)),
        ],
        [
            ((heads * HS, length), bf16),
            ((heads * HS, length), bf16),
            ((heads, 1, length), f32),
            ((length // 2, width), f32),
            ((length // 2, width), f32),
        ],
        [pltpu.VMEM((heads * HS, length), bf16)] * 2,
        "attn_heads",
        heads * length * length * HS * 2 * 10,
        15e6,
        ph, pl_, ph, pl_, ph, pl_, wh, wl, vec,
    )


def gate(u):
    phi = 0.5 * (1.0 + lax.erf(u * math.sqrt(0.5)))
    slope = phi + u * (jnp.exp(-0.5 * u * u) * (1.0 / math.sqrt(2.0 * math.pi)))
    return u * phi, slope


def feed_up_kernel(entries, count, flags, base, mine_a, mine_b, other_a, other_b, vec, bias, *refs):
    y_out, nh_out, nl_out, scale_out, hh_out, hl_out, slope_out, uh_out, ul_out, stage, sems = refs[count:]
    hidden = stage.shape[1]

    @pl.when(pl.program_id(0) == 0)
    def _():
        load_split(entries, flags, refs[:count], stage, sems, uh_out, ul_out)

    y = base[...] + (read_halves(mine_a, mine_b) + read_halves(other_a, other_b))
    y_out[...] = y
    n, scale = unit_rows(y)
    high, low = split(n)
    nh_out[...] = high
    nl_out[...] = low
    scale_out[...] = scale
    for slot in range(2):
        ah, al = split(n * vec[slot, 4:5, :] + vec[slot, 5:6, :])
        before = dot3(ah, al, uh_out[slot], ul_out[slot], NT) + bias[slot : slot + 1, :]
        active, slope = gate(before)
        cut = slice(slot * hidden, (slot + 1) * hidden)
        slope_out[:, cut] = slope
        high, low = split(active)
        hh_out[:, cut] = high
        hl_out[:, cut] = low


def feed_up(flags, base, added, vec, bias, pieces):
    length, width = base.shape
    hidden = bias.shape[1]
    weight = ((2, hidden, width), bf16)
    return call(
        functools.partial(feed_up_kernel, pieces.entries, len(pieces.arrays)),
        length // BM,
        [SMEM, rows(width)] + halves(width) * 2 + [full(vec.shape), full(bias.shape)] + [ANY] * len(pieces.arrays),
        [rows(width)] * 3 + [rows(1)] + [rows(2 * hidden)] * 3 + [full(weight[0])] * 2,
        [
            ((length, width), f32),
            ((length, width), bf16),
            ((length, width), bf16),
            ((length, 1), f32),
            ((length, 2 * hidden), bf16),
            ((length, 2 * hidden), bf16),
            ((length, 2 * hidden), f32),
            weight, weight,
        ],
        [pltpu.VMEM((2, hidden, width), f32), pltpu.SemaphoreType.DMA((len(pieces.entries),))],
        "feed_up",
        6 * length * width * 2 * hidden,
        40e6,
        flags, base, *added, vec, bias, *pieces.arrays,
    )


def feed_down_kernel(entries, count, flags, hh, hl, vec, *refs):
    part_a, part_b, dh_out, dl_out, stage, sems = refs[count:]
    hidden = stage.shape[1]

    @pl.when(pl.program_id(0) == 0)
    def _():
        load_split(entries, flags, refs[:count], stage, sems, dh_out, dl_out)

    partial = 0.5 * (vec[0, 6:7, :] + vec[1, 6:7, :])
    for slot in range(2):
        cut = slice(slot * hidden, (slot + 1) * hidden)
        partial = partial + dot3(hh[:, cut], hl[:, cut], dh_out[slot], dl_out[slot], NN)
    write_halves(part_a, part_b, partial)


def feed_down(flags, hh, hl, vec, pieces):
    length, hidden, width = hh.shape[0], hh.shape[1] // 2, vec.shape[2]
    weight = ((2, hidden, width), bf16)
    return call(
        functools.partial(feed_down_kernel, pieces.entries, len(pieces.arrays)),
        length // BM,
        [SMEM] + [rows(2 * hidden)] * 2 + [full(vec.shape)] + [ANY] * len(pieces.arrays),
        halves(width) + [full(weight[0])] * 2,
        [((length // 2, width), f32)] * 2 + [weight, weight],
        [pltpu.VMEM((2, hidden, width), f32), pltpu.SemaphoreType.DMA((len(pieces.entries),))],
        "feed_down",
        6 * length * width * 2 * hidden,
        25e6,
        flags, hh, hl, vec, *pieces.arrays,
    )


def piece_outs(width, order):
    count = 4 if order == 3 else 2
    shape = (2, 2, width // 2 // count, width)
    return [full(shape)] * count, [(shape, f32)] * count


def feed_back_one_kernel(pulled, order, flags, g_in, *refs):
    if pulled:
        added_refs, (nh, nl, scale) = refs[:4], refs[4:7]
        refs = refs[7:]
    (dh, dl, hh, hl, slope, g_out, uh_out, ul_out, *piece_refs, bias_out, total_out, acc) = refs
    step = pl.program_id(0)
    hidden = dh.shape[1]
    g = g_in[...]
    if pulled:
        n = nh[...].astype(f32) + nl[...].astype(f32)
        g = g + pull_rows(n, scale[...], read_halves(*added_refs[:2]) + read_halves(*added_refs[2:]))
    g_out[...] = g

    @pl.when(step == 0)
    def _():
        acc[...] = jnp.zeros_like(acc)
        bias_out[...] = jnp.zeros_like(bias_out)
        total_out[...] = jnp.zeros_like(total_out)

    total_out[...] += jnp.sum(g, axis=0, keepdims=True)
    gh, gl = split(g)
    for slot in range(2):
        cut = slice(slot * hidden, (slot + 1) * hidden)
        delta = dot3(gh, gl, dh[slot], dl[slot], NT) * slope[:, cut]
        bias_out[slot : slot + 1, :] += jnp.sum(delta, axis=0, keepdims=True)
        high, low = split(delta)
        uh_out[:, cut] = high
        ul_out[:, cut] = low
        acc[slot] += dot3(gh, gl, hh[:, cut], hl[:, cut], TN)

    @pl.when(step == pl.num_programs(0) - 1)
    def _():
        store_pieces(flags, lambda slot, row, count: acc[slot, pl.ds(row, count), :], order, piece_refs)


def feed_back_one(order, flags, g, pulled, dh, dl, hh, hl, slope, riders=()):
    length, width = g.shape
    hidden = dh.shape[1]
    piece_specs, piece_shapes = piece_outs(width, order)
    pulled_specs = halves(width) * 2 + [rows(width)] * 2 + [rows(1)] if pulled else []
    return call(
        functools.partial(feed_back_one_kernel, bool(pulled), order),
        length // BM,
        [SMEM, rows(width)] + pulled_specs + [full(dh.shape)] * 2 + [rows(2 * hidden)] * 3,
        [rows(width)] + [rows(2 * hidden)] * 2 + piece_specs + [full((2, hidden)), full((1, width))],
        [((length, width), f32), ((length, 2 * hidden), bf16), ((length, 2 * hidden), bf16)]
        + piece_shapes
        + [((2, hidden), f32), ((1, width), f32)],
        [pltpu.VMEM((2, width, hidden), f32)],
        "feed_back_one",
        6 * length * width * 4 * hidden,
        40e6,
        flags, g, *pulled, dh, dl, hh, hl, slope,
        riders=riders,
    )


def feed_back_two_kernel(parts, order, flags, uh, ul, nh, nl, vec, *refs):
    if "e" in parts:
        wh, wl, e_a, e_b, vec_out = refs
    else:
        *piece_refs, acc = refs
    step = pl.program_id(0)
    hidden = uh.shape[1] // 2

    @pl.when(step == 0)
    def _():
        if "e" in parts:
            vec_out[...] = jnp.zeros_like(vec_out)
        else:
            acc[...] = jnp.zeros_like(acc)

    n = nh[...].astype(f32) + nl[...].astype(f32)
    e = None
    for slot in range(2):
        cut = slice(slot * hidden, (slot + 1) * hidden)
        gain = vec[slot, 4:5, :]
        if "e" in parts:
            delta = dot3(uh[:, cut], ul[:, cut], wh[slot], wl[slot], NN)
            vec_out[2 * slot : 2 * slot + 1, :] += jnp.sum(delta * n, axis=0, keepdims=True)
            vec_out[2 * slot + 1 : 2 * slot + 2, :] += jnp.sum(delta, axis=0, keepdims=True)
            e = delta * gain if e is None else e + delta * gain
        else:
            ah, al = split(n * gain + vec[slot, 5:6, :])
            acc[slot] += dot3(uh[:, cut], ul[:, cut], ah, al, TN)
    if "e" in parts:
        write_halves(e_a, e_b, e)
    else:

        @pl.when(step == pl.num_programs(0) - 1)
        def _():
            store_pieces(flags, lambda slot, row, count: acc[slot, pl.ds(row, count), :], order, piece_refs)


def feed_back_two(parts, order, flags, uh, ul, nh, nl, vec, wh, wl, riders=()):
    length, width = nh.shape
    hidden = wh.shape[1]
    piece_specs, piece_shapes = piece_outs(width, order)
    if parts == "e":
        weights, out_specs = (wh, wl), halves(width) + [full((4, width))]
        out_shapes = [((length // 2, width), f32)] * 2 + [((4, width), f32)]
    else:
        weights, out_specs, out_shapes = (), piece_specs, piece_shapes
    return call(
        functools.partial(feed_back_two_kernel, parts, order),
        length // BM,
        [SMEM] + [rows(2 * hidden)] * 2 + [rows(width)] * 2 + [full(vec.shape)] + [full(w.shape) for w in weights],
        out_specs,
        out_shapes,
        [pltpu.VMEM((2, hidden, width), f32)] if parts == "w" else [],
        "feed_back_two_" + parts,
        6 * length * width * 2 * hidden,
        25e6,
        flags, uh, ul, nh, nl, vec, *weights,
        riders=riders,
    )


def attn_back_one_kernel(
    g_in, mine_a, mine_b, other_a, other_b, nh, nl, scale, wh, wl, oh, ol, g_out, dh_out, dl_out, do_out, total_out
):
    step = pl.program_id(0)
    inner, width = oh.shape[0], g_in.shape[1]

    @pl.when(step == 0)
    def _():
        do_out[...] = jnp.zeros_like(do_out)
        total_out[...] = jnp.zeros_like(total_out)

    n = nh[...].astype(f32) + nl[...].astype(f32)
    g = g_in[...] + pull_rows(n, scale[...], read_halves(mine_a, mine_b) + read_halves(other_a, other_b))
    g_out[...] = g
    total_out[...] += jnp.sum(g, axis=0, keepdims=True)
    gh, gl = split(g)
    delta = dot3(wh[...].reshape(inner, width), wl[...].reshape(inner, width), gh, gl, NT)
    high, low = split(delta)
    dh_out[...] = high
    dl_out[...] = low
    do_out[...] += dot3(oh[...], ol[...], gh, gl, NN)


def attn_back_one(g, added, nh, nl, scale, wh, wl, oh, ol, riders=()):
    length, width = g.shape
    inner = oh.shape[0]
    out_rows = inner // 2
    tail = pl.BlockSpec((2, out_rows, width), lambda i: (0, width // out_rows - 1, 0))
    return call(
        attn_back_one_kernel,
        length // BM,
        [rows(width)] + halves(width) * 2 + [rows(width)] * 2 + [rows(1)] + [tail, tail] + [lanes(inner)] * 2,
        [rows(width), lanes(inner), lanes(inner), full((inner, width)), full((1, width))],
        [
            ((length, width), f32),
            ((inner, length), bf16),
            ((inner, length), bf16),
            ((inner, width), f32),
            ((1, width), f32),
        ],
        [],
        "attn_back_one",
        6 * length * width * 2 * inner,
        20e6,
        g, *added, nh, nl, scale, wh, wl, oh, ol,
        riders=riders,
    )


def heads_back_kernel(qh, ql, kh, kl, vh, vl, dh, dl, oh, ol, lse, dqh, dql, dkh, dkl, dvh, dvl, acc_k, acc_v):
    keys = jnp.concatenate([kh[...], kh[...], kl[...]], axis=0)
    keys_two = jnp.concatenate([kh[...], kl[...]], axis=0)
    values = jnp.concatenate([vh[...], vh[...], vl[...]], axis=0)
    key_high = kh[...]
    for block in range(qh.shape[1] // BM):
        cut = slice(block * BM, (block + 1) * BM)
        q_high, q_low = qh[:, cut], ql[:, cut]
        d_high, d_low = dh[:, cut], dl[:, cut]
        delta = d_high.astype(f32) + d_low.astype(f32)
        attended = oh[:, cut].astype(f32) + ol[:, cut].astype(f32)
        diagonal = jnp.sum(delta * attended, axis=0, keepdims=True)
        scores = dot(keys, jnp.concatenate([q_high, q_low, q_high], axis=0), TN)
        probs = jnp.exp(scores - lse[0, :, cut])
        p_high, p_low = split(probs)
        delta_probs = dot(values, jnp.concatenate([d_high, d_low, d_high], axis=0), TN)
        delta_scores = probs * (delta_probs - diagonal)
        s_high, s_low = split(delta_scores)
        both = dot(jnp.concatenate([d_high, d_low], axis=0), p_high, NT)
        part_v = both[:HS] + (both[HS:] + dot(d_high, p_low, NT))
        both = dot(jnp.concatenate([q_high, q_low], axis=0), s_high, NT)
        part_k = both[:HS] + (both[HS:] + dot(q_high, s_low, NT))
        if block == 0:
            acc_v[...] = part_v
            acc_k[...] = part_k
        else:
            acc_v[...] += part_v
            acc_k[...] += part_k
        both = dot(keys_two, s_high, NN)
        delta_q = (both[:HS] + (both[HS:] + dot(key_high, s_low, NN))) * (1.0 / math.sqrt(HS))
        high, low = split(delta_q)
        dqh[:, cut] = high
        dql[:, cut] = low
    high, low = split(acc_k[...])
    dkh[...] = high
    dkl[...] = low
    high, low = split(acc_v[...])
    dvh[...] = high
    dvl[...] = low


def attn_heads_back(ph, pl_, dh, dl, oh, ol, lse, riders=()):
    inner2, length = ph.shape
    heads = inner2 // (3 * HS)
    half = heads // 2
    specs = []
    for which in range(3):
        specs += [head_spec(length, which, half)] * 2
    plain = pl.BlockSpec((HS, length), lambda h: (h, 0))
    return call(
        heads_back_kernel,
        heads,
        specs + [plain] * 4 + [pl.BlockSpec((1, 1, length), lambda h: (h, 0, 0))],
        [plain] * 6,
        [((heads * HS, length), bf16)] * 6,
        [pltpu.VMEM((HS, length), f32)] * 2,
        "attn_heads_back",
        heads * length * length * HS * 2 * 26,
        15e6,
        ph, pl_, ph, pl_, ph, pl_, dh, dl, oh, ol, lse,
        riders=riders,
    )


def attn_back_two_kernel(parts, order, flags, *refs):
    dqh, dql, dkh, dkl, dvh, dvl, nh, nl, vec = refs[:9]
    refs = refs[9:]
    if "e" in parts:
        (wh, wl), refs = refs[:2], refs[2:]
    if "w" in parts:
        do, refs = refs[0], refs[1:]
    if "e" in parts:
        (e_a, e_b, vec_out), refs = refs[:3], refs[3:]
    if "w" in parts:
        *piece_refs, pair_out, acc, turned = refs
    step = pl.program_id(0)
    third = dqh.shape[0] // 2
    inner = 3 * third

    @pl.when(step == 0)
    def _():
        if "e" in parts:
            vec_out[...] = jnp.zeros_like(vec_out)
        if "w" in parts:
            acc[...] = jnp.zeros_like(acc)
            pair_out[...] = jnp.zeros_like(pair_out)

    n = nh[...].astype(f32) + nl[...].astype(f32)
    ones = jnp.ones((8, n.shape[0]), bf16)
    e = None
    for slot in range(2):
        cut = slice(slot * third, (slot + 1) * third)
        high = jnp.concatenate([dqh[cut], dkh[cut], dvh[cut]], axis=0)
        low = jnp.concatenate([dql[cut], dkl[cut], dvl[cut]], axis=0)
        gain = vec[slot, 0:1, :]
        if "w" in parts:
            ah, al = split(n * gain + vec[slot, 1:2, :])
            acc[slot] += dot3(high, low, ah, al, NN)
            pair_out[slot] += dot(ones, high, NT) + dot(ones, low, NT)
        if "e" in parts:
            delta = dot3(high, low, wh[slot, :inner], wl[slot, :inner], TN)
            vec_out[2 * slot : 2 * slot + 1, :] += jnp.sum(delta * n, axis=0, keepdims=True)
            vec_out[2 * slot + 1 : 2 * slot + 2, :] += jnp.sum(delta, axis=0, keepdims=True)
            e = delta * gain if e is None else e + delta * gain
    if "e" in parts:
        write_halves(e_a, e_b, e)

    if "w" in parts:

        @pl.when(step == pl.num_programs(0) - 1)
        def _():
            for slot in range(2):
                whole = jnp.concatenate([acc[slot], do[slot * third : (slot + 1) * third]], axis=0)
                turned[slot] = jnp.transpose(whole)
            store_pieces(flags, lambda slot, row, count: turned[slot, pl.ds(row, count), :], order, piece_refs)


def attn_back_two(parts, order, flags, grads, nh, nl, vec, wh, wl, do, riders=()):
    length, width = nh.shape
    heads_rows = grads[0].shape[0]
    inner = 3 * heads_rows // 2
    piece_specs, piece_shapes = piece_outs(width, order)
    in_specs = [SMEM] + [lanes(heads_rows)] * 6 + [rows(width)] * 2 + [full(vec.shape)]
    args = [flags, *grads, nh, nl, vec]
    out_specs, out_shapes, scratch = [], [], []
    if "e" in parts:
        in_specs += [full(wh.shape)] * 2
        args += [wh, wl]
        out_specs += halves(width) + [full((4, width))]
        out_shapes += [((length // 2, width), f32)] * 2 + [((4, width), f32)]
    if "w" in parts:
        in_specs += [full(do.shape)]
        args += [do]
        out_specs += piece_specs + [full((2, 8, inner))]
        out_shapes += piece_shapes + [((2, 8, inner), f32)]
        scratch = [pltpu.VMEM((2, inner, width), f32), pltpu.VMEM((2, width, width), f32)]
    return call(
        functools.partial(attn_back_two_kernel, parts, order),
        length // BM,
        in_specs,
        out_specs,
        out_shapes,
        scratch,
        "attn_back_two_" + parts,
        6 * length * width * 2 * inner * len(parts),
        15e6 * len(parts),
        *args,
        riders=riders,
    )


def by_planes(flags, value, near_out, far_out):
    quarter = value.shape[1] // 4
    parts = [value[:, k * quarter : (k + 1) * quarter] for k in range(4)]
    odd, high = flags[0] % 2 == 1, flags[0] // 2 == 1
    parts = [jnp.where(odd, parts[k ^ 1], parts[k]) for k in range(4)]
    parts = [jnp.where(high, parts[k ^ 2], parts[k]) for k in range(4)]
    near_out[...] = jnp.concatenate([parts[0], parts[2]], axis=1)
    far_out[...] = jnp.concatenate([parts[1], parts[3]], axis=1)


def finish_kernel(flags, g_in, mine_a, mine_b, other_a, other_b, nh, nl, scale, mask, near_out, far_out, sums_out):
    @pl.when(pl.program_id(0) == 0)
    def _():
        sums_out[...] = jnp.zeros_like(sums_out)

    n = nh[...].astype(f32) + nl[...].astype(f32)
    g = g_in[...] + pull_rows(n, scale[...], read_halves(mine_a, mine_b) + read_halves(other_a, other_b))
    absorbed = mask[...]
    by_planes(flags, g * (1.0 - absorbed), near_out, far_out)
    sums_out[...] += jnp.sum(g * absorbed, axis=0, keepdims=True)


def finish(flags, g, added, nh, nl, scale, mask, riders=()):
    length, width = g.shape
    return call(
        finish_kernel,
        length // BM,
        [SMEM, rows(width)] + halves(width) * 2 + [rows(width)] * 2 + [rows(1)] * 2,
        [rows(width // 2)] * 2 + [full((1, width))],
        [((length, width // 2), f32)] * 2 + [((1, width), f32)],
        [],
        "finish",
        10 * length * width,
        15e6,
        flags, g, *added, nh, nl, scale, mask,
        riders=riders,
    )


def leave_kernel(flags, base, mine_a, mine_b, other_a, other_b, near_out, far_out):
    value = base[...] + (read_halves(mine_a, mine_b) + read_halves(other_a, other_b))
    by_planes(flags, value, near_out, far_out)


def leave(flags, base, added):
    length, width = base.shape
    return call(
        leave_kernel,
        length // BM,
        [SMEM, rows(width)] + halves(width) * 2,
        [rows(width // 2)] * 2,
        [((length, width // 2), f32)] * 2,
        [],
        "leave",
        10 * length * width,
        10e6,
        flags, base, *added,
    )


VEC_ROWS = 10


def pack_kernel(columns, flags, *refs):
    table = refs[-1]
    row_sum = refs[-2]
    width = row_sum.shape[1]
    odd, core, sequence = flags[0], flags[1], flags[2]
    table[...] = jnp.zeros_like(table)

    def place(parts):
        zero = jnp.zeros_like(parts[0])
        first = jnp.concatenate([v for p in parts for v in (p, zero)], axis=1)
        second = jnp.concatenate([v for p in parts for v in (zero, p)], axis=1)
        return jnp.where(core == 0, first, second)

    for layer in range(2):
        attn_vec, pair_sum, out_total, ffn_vec, up_sum, down_total = refs[6 * layer : 6 * layer + 6]
        third = pair_sum.shape[2] // 3
        block = up_sum.shape[1] // columns
        for slot in range(2):
            section = 2 * layer + jnp.where(odd == 1, 1 - slot, slot)
            base = section * VEC_ROWS

            def put(row, value):
                table[pl.ds(base + row, 1), :] = value

            put(0, attn_vec[2 * slot : 2 * slot + 1, :])
            put(1, attn_vec[2 * slot + 1 : 2 * slot + 2, :])
            pair = pair_sum[slot, 0:1, :]
            put(2, place([pair[:, :third], pair[:, 2 * third :]]))
            put(3, 0.5 * out_total[...])
            put(4, ffn_vec[2 * slot : 2 * slot + 1, :])
            put(5, ffn_vec[2 * slot + 1 : 2 * slot + 2, :])
            put(6, 0.5 * down_total[...])
            ups = up_sum[slot : slot + 1, :]
            spread = place([ups[:, k * block : (k + 1) * block] for k in range(columns)])
            for k in range(spread.shape[1] // width):
                put(7 + k, spread[:, k * width : (k + 1) * width])
    table[pl.ds(4 * VEC_ROWS + sequence, 1), :] = 0.5 * row_sum[...]


def pack(flags, small, row_sum, columns, sequences):
    width = row_sum.shape[1]
    arrays = [*small[0], *small[1], row_sum]
    count = -(-(4 * VEC_ROWS + sequences) // 8) * 8
    return call(
        functools.partial(pack_kernel, columns),
        1,
        [SMEM] + [full(v.shape) for v in arrays],
        [full((count, width))],
        [((count, width), f32)],
        [],
        "pack",
        1e4,
        1e6,
        flags, *arrays,
    )[0]


def after(value, *others):
    return lax.optimization_barrier((value, *others))[0]


class Plan:
    def __init__(self, planes, dp):
        self.planes, self.dp, self.columns = planes, dp, dp // 2
        self.z = lax.axis_index("section")
        device = lax.axis_index("dp")
        self.column, self.core = device // 2, device % 2

    def permute(self, value, target):
        pairs = []
        for z in range(self.planes):
            for d in range(self.dp):
                to = target(z, d)
                if to is not None:
                    pairs.append((z * self.dp + d, to[0] * self.dp + to[1]))
        return lax.ppermute(value, AXES, pairs)

    def groups(self):
        return [
            [z * self.dp + 2 * j + c for j in range(self.columns)] for z in range(self.planes) for c in range(2)
        ]

    def across(self, value):
        return self.permute(value, lambda z, d: (z, d ^ 1))

    def added(self, first, second):
        return (first, second, self.across(first), self.across(second))

    def along_z(self, value, bit, planes=None):
        return self.permute(value, lambda z, d: (z ^ bit, d) if planes is None or z in planes else None)

    def in_plane(self, value, bit):
        return self.permute(value, lambda z, d: (z, d ^ (2 * bit)))

    def whole(self, shard):
        return lax.all_gather(shard, AXES, axis_index_groups=self.groups(), axis=0, tiled=True)

    def sum_step(self, table, step):
        if self.columns != 4:
            return lax.psum(table, AXES) if step == 0 else table
        if step == 0:
            return table + self.across(table)
        if step < 3:
            return table + self.in_plane(table, step)
        return table + self.along_z(table, step - 2)


class Group:
    def __init__(self, plan, shard, order):
        self.plan, self.shard, self.order = plan, shard, order
        if plan.columns == 4:
            self.got = plan.in_plane(shard, order)

    def step(self):
        if self.plan.columns != 4:
            return self.shard
        self.kept = self.got
        on = jnp.concatenate([self.shard, self.kept])
        self.last = self.plan.in_plane(on, 3 - self.order)
        return on

    def pieces(self, first, count, slot, offset, when):
        if self.plan.columns != 4:
            whole = self.plan.whole(self.shard[first : first + count])
            return [(whole, 0, whole.shape[0], slot, None, 0, when)]
        rows_all = self.shard.shape[0]
        near, far = (1, 2) if self.order == 1 else (2, 1)
        return [
            (self.shard, first, count, slot, 0, offset, when),
            (self.kept, first, count, slot, near, offset, when),
            (self.last, first, count, slot, far, offset, when),
            (self.last, rows_all + first, count, slot, 3, offset, when),
        ]


def arrive(groups, *others):
    names = [(g, "got" if not hasattr(g, "last") else "last") for g in groups if g.plan.columns == 4]
    values = lax.optimization_barrier((*(getattr(g, name) for g, name in names), *others))
    for (group, name), value in zip(names, values):
        setattr(group, name, value)
    return values[len(names) :]


class Sum:
    def __init__(self, plan, order, pieces):
        self.plan, self.stage = plan, 0
        self.ways = [1, 2] if order == 3 else [order]
        self.count = pieces[0].shape[2]
        width = pieces[0].shape[3]
        if plan.columns == 4:
            send, keep = ([v.reshape(-1, width) for v in pieces[k::2]] for k in (0, 1))
            self.mine = keep
            self.got = [plan.in_plane(v, way) for v, way in zip(send, self.ways)]
        else:
            parts = []
            for k in range(4):
                for send, keep, way in zip(pieces[0::2], pieces[1::2], self.ways):
                    kinds = ((0, 2), (1, 3)) if way == 1 else ((0, 1), (2, 3))
                    parts.append(keep[kinds[0].index(k)] if k in kinds[0] else send[kinds[1].index(k)])
            whole = jnp.concatenate(parts, axis=1)
            whole = lax.psum_scatter(whole, AXES, axis_index_groups=plan.groups(), scatter_dimension=1, tiled=True)
            self.whole = [whole]

    def merge(self, other):
        if self.plan.columns == 4:
            self.mine, self.got = self.mine + other.mine, self.got + other.got
        else:
            self.whole = self.whole + other.whole
        return self

    def riders(self):
        if self.plan.columns != 4 or self.stage == 3:
            return []
        count = self.count
        pairs = list(zip(self.mine, self.got))
        if self.stage == 0:
            return [Rider(2 * count, (m, first, v, first)) for first in (0, 2 * count) for m, v in pairs]
        if self.stage == 1:
            return [Rider(count, *((m, first, v, first) for m, v in pairs)) for first in (0, count)]
        return [Rider(self.mine[0].shape[0], *((m, 0, v, 0) for m, v in pairs))]

    def take(self, values):
        if not values:
            return self.advance()
        plan = self.plan
        self.stage += 1
        if self.stage == 1:
            half = len(values) // 2
            self.mine = values[:half]
            self.got = [plan.in_plane(v, 3 - way) for v, way in zip(values[half:], self.ways)]
        elif self.stage == 2:
            self.mine = values[:1]
            self.got = [plan.along_z(values[1], 1)]
        else:
            self.mine = values
        return values

    def advance(self):
        if self.stage == 3:
            return []
        if self.plan.columns == 4:
            values = []
            for rider in self.riders():
                parts = [
                    a[i : i + rider.count] + b[j : j + rider.count] for a, i, b, j in rider.segments
                ]
                values.append(parts[0] if len(parts) == 1 else jnp.concatenate(parts))
            return self.take(values)
        if self.stage == 0:
            self.stage = 1
            return []
        if self.stage == 1:
            return self.take([jnp.concatenate([w[slot] for w in self.whole]) for slot in range(2)])
        return self.take([self.mine[0] + self.got[0]])

    def wait(self, *others):
        if self.plan.columns != 4 and self.stage < 2:
            return others
        self.got, others = lax.optimization_barrier((self.got, others))
        return others

    def after(self, *others):
        if self.plan.columns == 4 and self.stage < 3:
            self.got = [after(v, *others) for v in self.got]
        return self

    def finish(self):
        while self.stage < 3:
            self.advance()
        return self.mine[0]


def body(
    tokens, absorbed, timesteps, mask_embedding, time_table,
    attn_gain, attn_shift, joint_weight, pair_bias, out_weight, out_bias,
    ffn_gain, ffn_shift, up_weight, up_bias, down_weight, down_bias, cotangent,
):
    plan = Plan(lax.axis_size("section"), lax.axis_size("dp"))
    z, column, core = plan.z, plan.column, plan.core
    columns = plan.columns
    width = tokens.shape[1]
    inner = out_weight.shape[1]
    hidden = up_weight.shape[2]
    inner_half, hidden_half = inner // 2, hidden // 2
    block = hidden_half // columns
    low_planes = z < 2

    joint_half = lax.dynamic_index_in_dim(joint_weight[0].reshape(width, 3, 2, inner_half), core, 2, keepdims=False)
    joint_half = joint_half.reshape(width, 3 * inner_half).T
    out_half = lax.dynamic_slice_in_dim(out_weight[0], core * inner_half, inner_half, 0)
    own_attn = jnp.concatenate([joint_half, out_half], axis=0)
    up_half = lax.dynamic_index_in_dim(up_weight[0].reshape(width, columns, 2, block), core, 2, keepdims=False)
    own_up = up_half.reshape(width, hidden_half).T
    down_half = lax.dynamic_index_in_dim(down_weight[0].reshape(columns, 2, block, width), core, 1, keepdims=False)
    own_down = down_half.reshape(hidden_half, width)
    own = (own_attn, own_up, own_down)

    own_vec = jnp.stack(
        [attn_gain[0], attn_shift[0], pair_bias[0], out_bias[0], ffn_gain[0], ffn_shift[0], down_bias[0]]
        + [up_bias[0, k * width : (k + 1) * width] for k in range(hidden // width)]
    )
    vec_count = own_vec.shape[0]
    count = width // columns

    def shard_of(matrix):
        return lax.dynamic_slice_in_dim(matrix, column * count, count, 0)

    local = core == z // 2
    which = z % 2
    sequence = 4 * column + z

    def fetch(array):
        piece = lax.dynamic_slice_in_dim(array, which * LEN, LEN, 0)
        return piece, plan.permute(piece, lambda zz, d: (zz, d ^ 1) if d % 2 == zz // 2 else None)

    tail = jnp.zeros((-vec_count % 8, width), f32)
    shard = jnp.concatenate([shard_of(own[0]), own_vec, tail])
    far_attn, near_attn = plan.along_z(shard, 2), plan.along_z(shard, 1)
    far_attn, near_attn, up_shard, down_shard = lax.optimization_barrier(
        (far_attn, near_attn, shard_of(own[1]), shard_of(own[2]))
    )
    opp_attn = plan.along_z(far_attn, 1)
    far_up = plan.along_z(up_shard, 2)
    mask_parts, token_parts = fetch(after(absorbed, far_attn)), fetch(after(tokens, far_attn))

    near_vec = jnp.stack([own_vec, near_attn[count : count + vec_count]])
    far_vec = jnp.stack([far_attn[count : count + vec_count], opp_attn[count : count + vec_count]])
    vectors = jnp.stack([jnp.where(low_planes, near_vec, far_vec), jnp.where(low_planes, far_vec, near_vec)])

    def opposite(near, far):
        return jnp.where(low_planes, near, far), jnp.where(low_planes, far, near)

    attn_opp = opposite(near_attn[:count], opp_attn[:count])
    attn_groups = [Group(plan, far_attn[:count], 1), Group(plan, attn_opp[0], 2)]
    near_up = plan.along_z(after(up_shard, attn_opp[0]), 1)
    far_up, near_up, mask_parts, token_parts = arrive(attn_groups, far_up, near_up, mask_parts, token_parts)
    sent = [group.step() for group in attn_groups]
    mask_parts, token_parts = lax.optimization_barrier((mask_parts, token_parts, *sent))[:2]
    mask_row = jnp.where(local, *mask_parts).astype(f32)
    step = lax.dynamic_index_in_dim(timesteps, sequence, 0, keepdims=False)
    step_row = lax.dynamic_slice_in_dim(time_table, step, 1, 0)
    mask = mask_row[:, None]
    x = jnp.where(mask > 0.5, mask_embedding[None, :] + step_row, jnp.where(local, *token_parts))
    weight = LEN / jnp.maximum(jnp.sum(mask_row), 1.0)
    far_down = plan.along_z(after(down_shard, far_up), 2)
    opp_up = plan.along_z(far_up, 1)
    opp_up, x = arrive(attn_groups, opp_up, x)
    near_down = plan.along_z(after(down_shard, opp_up), 1)
    up_opp = opposite(near_up, opp_up)
    pair_all = lax.dynamic_index_in_dim(vectors[:, :, 2].reshape(2, 2, 2, 2, inner_half), core, 3, keepdims=False)
    pair_rows = jnp.stack([pair_all[:, :, 0], jnp.zeros_like(pair_all[:, :, 0]), pair_all[:, :, 1]], axis=2)
    pair_cols = pair_rows.reshape(2, 2 * 3 * inner_half, 1)
    up_rows = lax.dynamic_index_in_dim(
        vectors[:, :, 7:].reshape(2, 2, columns, 2, block), core, 3, keepdims=False
    ).reshape(2, 2, hidden_half)

    natural = jnp.arange(4, dtype=jnp.int32)
    order = column ^ natural if columns == 4 else natural
    flags = [
        jnp.concatenate([(low_planes == (layer == 0)).astype(jnp.int32)[None], order.astype(jnp.int32)])
        for layer in range(2)
    ]

    def own_rows(matrix):
        return [(matrix, 0, matrix.shape[0], 0, None, 0, "near")]

    def pieces_of(matrix, par, opp):
        return Pieces(own_rows(matrix) + par.pieces(0, count, 0, 0, "far") + opp)

    kept = []

    def keep(layer, *values):
        kept.append((vectors[layer], *values))

    half = count // 2
    up_groups = [Group(plan, far_up, 1), Group(plan, up_opp[0], 2)]
    x, xh, xl, x_scale, ph, pl_, wh, wl = attn_in(
        flags[0], x, (), vectors[0], pair_cols[0], pieces_of(own[0], attn_groups[0], attn_groups[1].pieces(0, count, 1, 0, "all"))
    )
    ph, far_down, near_down, cotangent = arrive(up_groups, ph, far_down, near_down, cotangent)
    cot_parts = fetch(cotangent)
    opp_down = plan.along_z(far_down, 1)
    for group in up_groups:
        group.step()
    oh, ol, lse, *part = attn_heads(ph, pl_, wh, wl, vectors[0])
    opp_down, *part = arrive(up_groups, opp_down, *part)
    down_opp = opposite(near_down, opp_down)
    down_groups = [Group(plan, far_down, 1), Group(plan, down_opp[0], 2)]
    added = plan.added(*part)
    added = added[:2] + arrive(down_groups, *added[2:])
    for group in down_groups:
        group.step()
    if columns == 4:
        last_attn = [Group(plan, attn_opp[1][:half], 1), Group(plan, attn_opp[1][half:], 2)]
    else:
        last_attn = [Group(plan, attn_opp[1], 1)]
    y, yh, yl, y_scale, hh, hl, slope, uh, ul = feed_up(
        flags[0], x, added, vectors[0], up_rows[0], pieces_of(own[1], up_groups[0], up_groups[1].pieces(0, count, 1, 0, "all"))
    )
    hh, cot_other = arrive(last_attn, hh, cot_parts[1])
    for group in last_attn:
        group.step()
    *feed_part, dh, dl = feed_down(
        flags[0], hh, hl, vectors[0], pieces_of(own[2], down_groups[0], down_groups[1].pieces(0, count, 1, 0, "all"))
    )
    keep(0, xh, xl, x_scale, ph, pl_, wh, wl, oh, ol, lse, yh, yl, y_scale, hh, hl, slope, uh, ul, dh, dl)

    g = jnp.where(local, cot_parts[0], after(cot_other, dh)) * (mask * weight)
    last_groups = [Group(plan, up_opp[1], 1), Group(plan, down_opp[1], 2)]
    feed_part = arrive([*last_attn, *last_groups], *feed_part)
    for group in last_groups:
        group.step()
    added = plan.added(*feed_part)
    if columns == 4:
        attn_last = last_attn[0].pieces(0, half, 1, 0, "all") + last_attn[1].pieces(0, half, 1, half, "all")
    else:
        attn_last = last_attn[0].pieces(0, count, 1, 0, "all")
    x, xh, xl, x_scale, ph, pl_, wh, wl = attn_in(
        flags[1], y, added, vectors[1], pair_cols[1], pieces_of(own[0], attn_groups[0], attn_last)
    )
    oh, ol, lse, *part = attn_heads(ph, pl_, wh, wl, vectors[1])
    added = plan.added(*arrive(last_groups, *part))
    y, yh, yl, y_scale, hh, hl, slope, uh, ul = feed_up(
        flags[1], x, added, vectors[1], up_rows[1], pieces_of(own[1], up_groups[0], last_groups[0].pieces(0, count, 1, 0, "all"))
    )
    *feed_part, dh, dl = feed_down(
        flags[1], hh, hl, vectors[1], pieces_of(own[2], down_groups[0], last_groups[1].pieces(0, count, 1, 0, "all"))
    )
    keep(1, xh, xl, x_scale, ph, pl_, wh, wl, oh, ol, lse, yh, yl, y_scale, hh, hl, slope, uh, ul, dh, dl)
    x, added = y, plan.added(*feed_part)
    last = (x, *added)

    quarter = width // plan.planes
    plane_flags = jnp.stack([z, core]).astype(jnp.int32)

    def beside(value):
        return plan.permute(value, lambda zz, d: (zz ^ 1, d) if d % 2 == zz // 2 else None)

    def beyond(mine, theirs):
        both = jnp.concatenate([mine[:, quarter:], theirs[:, quarter:]], axis=1)
        return plan.permute(both, lambda zz, d: (zz ^ 2, d) if d % 2 == zz // 2 else None)

    def settle_rows(mine, theirs, arrived):
        first = jnp.where(local, mine[:, :quarter], arrived[:, :quarter])
        second = jnp.where(local, theirs[:, :quarter], arrived[:, quarter:])
        odd = z % 2 == 1
        return jnp.concatenate([jnp.where(odd, second, first), jnp.where(odd, first, second)])

    def ride(kernel, riding, *args):
        lists = [total.riders() for total in riding]
        values = list(kernel(*args, riders=[r for some in lists for r in some]))
        taken = sum(len(some) for some in lists)
        results, extra = values[: len(values) - taken], values[len(values) - taken :]
        for total, some in zip(riding, lists):
            total.take(extra[: len(some)])
            extra = extra[len(some) :]
        return results

    small = [None] * 2
    (vec, xh, xl, x_scale, ph, pl_, wh, wl, oh, ol, lse, yh, yl, y_scale, hh, hl, slope, uh, ul, dh, dl) = kept[1]
    g, duh, dul, *pieces, up_bias_sum, down_bias_sum = feed_back_one(1, flags[1], g, (), dh, dl, hh, hl, slope)
    down_1 = Sum(plan, 1, pieces)
    out_near, out_far = leave(plane_flags, after(last[0], up_bias_sum), last[1:])
    out_beside = beside(out_far)
    *e, ffn_vec = feed_back_two("e", 0, flags[1], after(duh, out_near), dul, yh, yl, vec, uh, ul)
    e = plan.added(*e)
    pieces = feed_back_two("w", 2, flags[1], after(duh, ffn_vec), dul, yh, yl, vec, uh, ul)
    up_1 = Sum(plan, 2, pieces)
    g, out_beside, *others = lax.optimization_barrier((g, out_beside, *e[2:], pieces[0]))[:4]
    g, doh, dol, do, out_bias_sum = attn_back_one(g, (*e[:2], *others), yh, yl, y_scale, wh, wl, oh, ol)
    grads = attn_heads_back(ph, pl_, doh, dol, oh, ol, lse)
    *e, attn_vec = ride(attn_back_two, [down_1], "e", 0, flags[1], grads, xh, xl, vec, wh, wl, do)
    e = plan.added(*e)
    out_beyond = beyond(out_near, after(out_beside, attn_vec))
    *pieces, pair_sum = ride(attn_back_two, [up_1], "w", 2, flags[1], grads, xh, xl, vec, wh, wl, after(do, attn_vec))
    attn_1 = Sum(plan, 2, pieces)
    g, *others = lax.optimization_barrier((g, *e[2:], pair_sum))[:3]
    pulled = (*e[:2], *others, xh, xl, x_scale)
    small[1] = (attn_vec, pair_sum, out_bias_sum, ffn_vec, up_bias_sum, down_bias_sum)

    (vec, xh, xl, x_scale, ph, pl_, wh, wl, oh, ol, lse, yh, yl, y_scale, hh, hl, slope, uh, ul, dh, dl) = kept[0]
    g, duh, dul, *pieces, up_bias_sum, down_bias_sum = feed_back_one(1, flags[0], g, pulled, dh, dl, hh, hl, slope)
    down_0 = Sum(plan, 1, pieces)
    feed_1 = down_1.merge(up_1)
    duh, out_beyond = lax.optimization_barrier((duh, out_beyond))
    *e, ffn_vec = ride(feed_back_two, [feed_1], "e", 0, flags[0], duh, dul, yh, yl, vec, uh, ul)
    e = plan.added(*e)
    pieces = feed_back_two("w", 3, flags[0], after(duh, ffn_vec), dul, yh, yl, vec, uh, ul)
    up_0 = Sum(plan, 3, pieces)
    g, *others = lax.optimization_barrier((g, *e[2:], pieces[0]))[:3]
    g, doh, dol, do, out_bias_sum = ride(
        attn_back_one, [attn_1], g, (*e[:2], *others), yh, yl, y_scale, wh, wl, oh, ol
    )
    doh = after(doh, *down_0.after(out_bias_sum).advance())
    grads = ride(attn_heads_back, [feed_1], ph, pl_, doh, dol, oh, ol, lse)
    mixed = attn_1.merge(down_0)
    *e, attn_vec = attn_back_two("e", 0, flags[0], grads, xh, xl, vec, wh, wl, do)
    e = plan.added(*e)
    grads[0] = after(grads[0], attn_vec, *mixed.after(attn_vec).advance())
    *pieces, pair_sum = ride(attn_back_two, [up_0], "w", 3, flags[0], grads, xh, xl, vec, wh, wl, do)
    attn_0 = Sum(plan, 3, pieces)
    e = (*e[:2], after(e[2], pair_sum), after(e[3], pair_sum))
    small[0] = (attn_vec, pair_sum, out_bias_sum, ffn_vec, up_bias_sum, down_bias_sum)

    def cross(low, high):
        on = jnp.where(low_planes, high, low)
        return jnp.where(low_planes, low, high), on, plan.along_z(on, 2)

    grad_near, grad_far, row_sum = finish(plane_flags, g, e, xh, xl, x_scale, mask)
    feed_1, mixed = feed_1.finish(), mixed.after(grad_far).finish()
    down_mine, down_on, down_got = cross(mixed[count:], feed_1[:count])
    up_0.after(grad_far).advance()
    out_rows = settle_rows(out_near, out_beside, out_beyond)
    grad_beside = beside(grad_far)

    up_mine, up_on, up_got = cross(up_0.after(grad_far).finish(), feed_1[count:])
    pack_flags = jnp.stack([z % 2, core, sequence]).astype(jnp.int32)
    table = pack(pack_flags, small, row_sum, columns, timesteps.shape[0])
    table = plan.sum_step(table, 0)
    (table,) = attn_0.after(up_on).wait(table)
    attn_0.advance()
    table = plan.sum_step(table, 3)
    grad_beside, table = attn_0.wait(grad_beside, table)
    on = attn_0.advance()
    (grad_beside,) = arrive([], grad_beside, *on)[:1]
    grad_beyond = beyond(grad_near, grad_beside)
    table = plan.sum_step(table, 4)
    up_got, table = attn_0.wait(up_got, table)
    attn_mine, attn_on, attn_got = cross(attn_0.finish(), mixed[:count])
    for step in (1, 2):
        table = plan.sum_step(table, step)
    down_mine, up_mine = down_mine + down_got, up_mine + up_got

    def exchange(rows_all):
        halves = rows_all.reshape(2, -1, width)
        mine = lax.dynamic_index_in_dim(halves, core, 0, keepdims=False)
        theirs = plan.across(lax.dynamic_index_in_dim(halves, 1 - core, 0, keepdims=False))
        first = core == 0
        return jnp.where(first, mine, theirs), jnp.where(first, theirs, mine)

    zero, one = exchange(down_mine)
    down_grad = jnp.stack([v.reshape(-1, columns, block) for v in (zero, one)], axis=2).reshape(-1, hidden).T
    up_grad = up_mine.reshape(-1, width).T
    attn_got, table = lax.optimization_barrier((attn_got, table, down_grad, up_grad))[:2]
    zero, one = exchange(attn_mine + attn_got)
    grad_rows = settle_rows(grad_near, grad_beside, grad_beyond)
    joint = jnp.stack([v[:, : 3 * inner_half].reshape(-1, 3, inner_half) for v in (zero, one)], axis=2)
    joint_grad = joint.reshape(-1, 3 * inner)
    out_grad = jnp.concatenate([zero[:, 3 * inner_half :], one[:, 3 * inner_half :]], axis=1).T

    mine = lax.dynamic_slice_in_dim(table, VEC_ROWS * z, VEC_ROWS, 0)
    device = 2 * column + core
    share = lax.dynamic_slice_in_dim(mine, device * (width // plan.dp), width // plan.dp, 1)
    up_count = hidden // width
    up_share = lax.dynamic_slice_in_dim(
        mine[7 : 7 + up_count].reshape(-1), device * (hidden // plan.dp), hidden // plan.dp, 0
    )

    seq_rows = table[4 * VEC_ROWS : 4 * VEC_ROWS + timesteps.shape[0]]
    seq_cols = lax.dynamic_slice_in_dim(seq_rows, z * quarter, quarter, 1)
    picks = (timesteps[:, None] == jnp.arange(time_table.shape[0], dtype=jnp.int32)[None, :]).astype(f32)
    table_grad = jnp.einsum("st,sd->td", picks, seq_cols, precision=lax.Precision.HIGHEST)
    mask_grad = jnp.sum(seq_cols, axis=0)

    return (
        out_rows,
        grad_rows,
        mask_grad,
        table_grad,
        share[0:1],
        share[1:2],
        joint_grad[None],
        share[2:3],
        out_grad[None],
        share[3:4],
        share[4:5],
        share[5:6],
        up_grad[None],
        up_share[None],
        down_grad[None],
        share[6:7],
    )


def solution(mesh):
    placed = (
        P("dp", None), P("dp"), P(), P(), P(),
        P("section", None), P("section", None), P("section", None, None), P("section", None),
        P("section", None, None), P("section", None), P("section", None), P("section", None),
        P("section", None, None), P("section", None), P("section", None, None), P("section", None),
        P("dp", None),
    )
    vector = P("section", "dp")
    return jax.shard_map(
        body,
        mesh=mesh,
        in_specs=placed,
        out_specs=(
            P("dp", "section"), P("dp", "section"), P("section"), P(None, "section"),
            vector, vector, P("section", "dp", None), vector, P("section", None, "dp"), vector,
            vector, vector, P("section", None, "dp"), vector, P("section", None, "dp"), vector,
        ),
        check_vma=False,
    )
```
